256 devices in a mesh: row: 8 (over z_lo, core), col: 32 (over y, z_hi, x).
Axes of the slice: x: 4, y: 4, z: 8 (z_hi: 2, z_lo: 4; z = z_hi * 4 + z_lo), core: 2. Of those that a mesh axis runs over, the one named last changes fastest.
Arguments:
- features: bfloat16 [32, 2048, 2048], P(None, 'col', 'row'), may hold values from -6 to 6
- cotangent: bfloat16 [32, 2048, 2048], P(None, 'col', 'row'), may hold values from -6 to 6
- mask: int32 [2048], replicated, may hold values 0 or 1
- w_conv: bfloat16 [3, 3, 32, 32], replicated, may hold values from -0.375 to 0.375
- w_point: bfloat16 [32, 32], replicated, may hold values from -1 to 1
- bias: float32 [32], replicated, may hold values from -3 to 3
Outputs:
- feature_grad: bfloat16 [32, 2048, 2048], P(None, 'col', 'row')
- conv_grad: float32 [3, 3, 32, 32], replicated
- point_grad: float32 [32, 32], replicated
- bias_grad: float32 [32], replicated
The draws below stay inside these ranges and needn't reach their ends.
Inputs may be any that keep to these rules, and one draw needn't show every extreme that they name: `mask`: 1 marks a mappable bin, 0 an unmappable one.
All inputs are finite; a program needn't handle non-finite values.
Results may differ from the reference program's by a relative error of at most 0.008.
Values may be sent and summed in bfloat16 or wider, within the bound.
A program may use at most 64 MiB of HBM per device.

```python
import math
import jax
import jax.numpy as jnp
from jax import lax

C = 32
DILATION_STEP = 4
N = 2048


def set_ends(entries, key, low, largest):
    index_at = [jax.random.randint(jax.random.fold_in(key, axis), (), 0, length) for axis, length in enumerate(entries.shape)]
    main_axis = entries.shape.index(max(entries.shape))
    beside = index_at[:main_axis] + [(index_at[main_axis] + 1) % entries.shape[main_axis]] + index_at[main_axis + 1:]
    return entries.at[tuple(index_at)].set(low).at[tuple(beside)].set(largest)


def steps_of(key, dims, cuts, low, largest):
    loudness = 1.0
    for axis_at, shards_of in cuts:
        draws = jax.random.uniform(jax.random.fold_in(jax.random.fold_in(key, 6), axis_at), (shards_of,), jnp.float32, low / len(cuts), largest / len(cuts))
        loudness = loudness * jnp.repeat(jnp.exp(draws), dims[axis_at] // shards_of).reshape((-1,) + (1,) * (len(dims) - 1 - axis_at))
    return loudness


def noise(key, dims, scale, most, pieces=(), kind=jnp.bfloat16):
    values = scale * jax.random.normal(key, dims, jnp.float32)
    if pieces:
        values = values * steps_of(key, dims, pieces, -0.22, 0.18)
    return jnp.clip(values, -most, most).astype(kind)


def setup_inputs(seed: int = 0) -> dict:
    key_of = jax.random.split(jax.random.key(seed), 7)
    return {
        "features": noise(key_of[0], (C, N, N), 1.0, 6.0, ((1, 32), (2, 8))),
        "cotangent": noise(key_of[1], (C, N, N), 1.0, 6.0, ((1, 32), (2, 8))),
        "mask": set_ends((jax.random.randint(key_of[2], (N,), 0, 8) < 7).astype(jnp.int32), jax.random.fold_in(key_of[2], 1), 0, 1),
        "w_conv": noise(key_of[3], (3, 3, C, C), (9 * C) ** -0.5, 0.375),
        "w_point": noise(key_of[4], (C, C), C ** -0.5, 1.0),
        "bias": noise(key_of[5], (C,), 0.5, 3.0, (), jnp.float32),
    }


def silu_grad(value):
    sig = jax.nn.sigmoid(value)
    return sig * (1.0 + value * (1.0 - sig))

def dilated_conv(bordered_input, filter_weight):
    return lax.conv_general_dilated(bordered_input[None].astype(jnp.float32), filter_weight.astype(jnp.float32), (1, 1), 'VALID', rhs_dilation=(DILATION_STEP, DILATION_STEP), precision=lax.Precision.HIGHEST)[0]

def reference(features, cotangent, mask, w_conv, w_point, bias):
    map_length = features.shape[1]
    channels = features.shape[0]
    residual_unit = math.gcd(map_length, 512)
    count = map_length // residual_unit
    border_width = 2 * DILATION_STEP
    filter_weight = jnp.transpose(w_conv, (2, 3, 0, 1))
    back_kernel = jnp.flip(jnp.transpose(w_conv, (3, 2, 0, 1)), (2, 3))
    keep_col = mask.astype(jnp.float32)
    point_weight = w_point.astype(jnp.float32)

    def step(carry, index):
        conv_sum, point_sum, bias_sum = carry
        offset_index = index * residual_unit
        extended = offset_index - border_width + jnp.arange(residual_unit + 2 * border_width, dtype=jnp.int32)
        inside = ((extended >= 0) & (extended < map_length)).astype(jnp.float32)
        safe = jnp.clip(extended, 0, map_length - 1).astype(jnp.int32)
        x_rows = jnp.take(features, safe, axis=1).astype(jnp.float32) * inside[None, :, None]
        activation_map = jax.nn.silu(x_rows).astype(jnp.bfloat16)
        activation_bordered = jnp.pad(activation_map, ((0, 0), (0, 0), (DILATION_STEP, DILATION_STEP)))
        pre_act = dilated_conv(activation_bordered, filter_weight) + bias[:, None, None]
        after_activation = jax.nn.silu(pre_act).astype(jnp.bfloat16)
        central_part = offset_index - DILATION_STEP + jnp.arange(residual_unit + 2 * DILATION_STEP, dtype=jnp.int32)
        inside_mid = ((central_part >= 0) & (central_part < map_length)).astype(jnp.float32)
        safe_mid = jnp.clip(central_part, 0, map_length - 1).astype(jnp.int32)
        g_rows = jnp.take(cotangent, safe_mid, axis=1).astype(jnp.float32)
        g_cols = jnp.swapaxes(jnp.take(cotangent, safe_mid, axis=2), 1, 2).astype(jnp.float32)
        keep_mask = (jnp.take(mask, safe_mid).astype(jnp.float32) * inside_mid)[:, None] * keep_col[None, :]
        residual_gradient = keep_mask * 0.5 * (g_rows + g_cols)
        residual_halved = residual_gradient.astype(jnp.bfloat16)
        post_grad = jnp.einsum('oi,ohw->ihw', point_weight, residual_halved.astype(jnp.float32), precision=lax.Precision.HIGHEST)
        preceding_gradient = (silu_grad(pre_act) * post_grad).astype(jnp.bfloat16)
        gradient_bordered = jnp.pad(preceding_gradient, ((0, 0), (0, 0), (DILATION_STEP, DILATION_STEP)))
        act_grad = dilated_conv(gradient_bordered, back_kernel)
        x_mid = lax.dynamic_slice_in_dim(features, offset_index, residual_unit, 1).astype(jnp.float32)
        residual_interior = residual_gradient[:, DILATION_STEP:DILATION_STEP + residual_unit]
        feature_grad = (residual_interior + silu_grad(x_mid) * act_grad).astype(jnp.bfloat16)
        interior_gradient = preceding_gradient[:, DILATION_STEP:DILATION_STEP + residual_unit].astype(jnp.float32)
        activation_interior = activation_bordered[:, DILATION_STEP:DILATION_STEP + residual_unit + 2 * DILATION_STEP].astype(jnp.float32)
        conv_terms = []
        for filter_row in range(3):
            for filter_column in range(3):
                slice_region = activation_interior[:, filter_row * DILATION_STEP:filter_row * DILATION_STEP + residual_unit, filter_column * DILATION_STEP:filter_column * DILATION_STEP + map_length]
                conv_terms.append(jnp.einsum('yuj,puj->yp', interior_gradient, slice_region, precision=lax.Precision.HIGHEST))
        conv_part = jnp.stack(conv_terms).reshape(3, 3, channels, channels)
        pointwise_piece = jnp.einsum('yuj,puj->yp', residual_halved[:, DILATION_STEP:DILATION_STEP + residual_unit].astype(jnp.float32), after_activation[:, DILATION_STEP:DILATION_STEP + residual_unit].astype(jnp.float32), precision=lax.Precision.HIGHEST)
        bias_part = lax.optimization_barrier(jnp.sum(interior_gradient, axis=(1, 2)))
        return ((conv_sum + conv_part, point_sum + pointwise_piece, bias_sum + bias_part), feature_grad)
    init = (jnp.zeros((3, 3, channels, channels), jnp.float32), jnp.zeros((channels, channels), jnp.float32), jnp.zeros((channels,), jnp.float32))
    totals, blocks = lax.scan(step, init, jnp.arange(count, dtype=jnp.int32))
    feature_grad = jnp.transpose(blocks, (1, 0, 2, 3)).reshape(channels, map_length, map_length)
    scale = 1.0 / map_length
    return (feature_grad, totals[0] * scale, totals[1] * scale, totals[2] * scale)
```

```python
import jax
import jax.numpy as jnp
from jax import lax
from jax.experimental import pallas as pl
from jax.experimental.pallas import tpu as pltpu
from jax.sharding import PartitionSpec as P

F32, BF16 = jnp.float32, jnp.bfloat16
MESH = pl.DeviceIdType.MESH
ROWS, COLS = 8, 32
TILE = 256
TAPS = 3 * TILE
TILES = 8
GROUP = 16
NT = (((1,), (1,)), ((), ()))


def iota(shape, dim):
    return lax.broadcasted_iota(jnp.int32, shape, dim)


def dot(x, y):
    return jnp.dot(x, y, preferred_element_type=F32)


def dot_nt(x, y):
    return lax.dot_general(x, y, NT, preferred_element_type=F32)


def at(start, size):
    return pl.ds(pl.multiple_of(start, size), size)


def sigmoid(v):
    return 1.0 / (1.0 + jnp.exp(-v))


def pack(tile, bottom):
    v = tile.reshape(16, 2, 8, 256)
    low = iota((16, 8, 256), 1) < 4
    if bottom:
        v = jnp.where(low, v[:, 0], pltpu.roll(v[:, 1], 4, 1))
    else:
        v = jnp.where(low, pltpu.roll(v[:, 0], 4, 1), v[:, 1])
    return v.reshape(128, 256).astype(BF16)


def unpack(packed, bottom):
    width = packed.shape[1]
    v = packed.astype(F32).reshape(16, 8, width)
    turned = pltpu.roll(v, 4, 1)
    low = iota((16, 8, width), 1) < 4
    if bottom:
        pair = [jnp.where(low, v, 0.0), jnp.where(low, turned, 0.0)]
    else:
        pair = [jnp.where(low, 0.0, turned), jnp.where(low, 0.0, v)]
    return jnp.stack(pair, axis=1).reshape(TILE, width)


def kernel(
    feat_hbm, cot_hbm, mask_ref, wconv_ref, wpoint_ref, bias_ref,
    fg_hbm, conv_ref, point_ref, biasg_ref,
    feat, cot, mir_send, mir_recv, act, grad, res, res_half, slope, pre_slope, post, gnat,
    mat_f, mat_b, mat_p, keep, prev, csum, psum, bsum, out,
    ns_send, ew_send, ns_recv, ew_recv, corner, payload, part1, sum1, part2, sum2, part3,
    in_sem, out_sem, mir_ssem, mir_rsem, halo_ssem, halo_rsem, red_ssem, red_rsem,
):
    r, c = lax.axis_index("row"), lax.axis_index("col")
    a, b = lax.div(c, 4), lax.rem(c, 4)
    y, zh = lax.div(c, 8), lax.rem(a, 2)
    group_a, group_b = zh * 8 + r, y * 4 + b

    def mirror_at(q):
        return {"row": a, "col": 4 * r + q}

    def member_a(m):
        return {"row": lax.rem(m, 8), "col": y * 8 + lax.div(m, 8) * 4 + b}

    def member_b(m):
        return {"row": r, "col": lax.div(m, 4) * 8 + zh * 4 + lax.rem(m, 4)}

    def beside(dr, dc):
        return {"row": lax.rem(r + dr + ROWS, ROWS), "col": lax.rem(c + dc + COLS, COLS)}

    own_mirror = a == r
    sides = [(0, 1), (0, -1), (1, 0), (-1, 0), (1, 1), (-1, 1), (1, -1), (-1, -1)]

    barrier = pltpu.get_barrier_semaphore()

    def greet(device):
        pl.semaphore_signal(barrier, inc=1, device_id=device, device_id_type=MESH)

    @pl.when(jnp.logical_not(own_mirror))
    def _():
        greet(mirror_at(b))

    for d in range(1, 4):
        greet(mirror_at(lax.rem(b + d, 4)))
    for dr, dc in sides:
        greet(beside(dr, dc))

    def greet_groups(d, _):
        greet(member_a(lax.rem(group_a + d, GROUP)))
        greet(member_b(lax.rem(group_b + d, GROUP)))
        return 0

    lax.fori_loop(1, GROUP, greet_groups, 0)

    load_cot = pltpu.make_async_copy(cot_hbm, cot, in_sem.at[0])
    load_feat = pltpu.make_async_copy(feat_hbm, feat, in_sem.at[1])
    load_cot.start()
    load_feat.start()

    load_cot.wait()
    ident = (iota((256, 256), 0) == iota((256, 256), 1)).astype(BF16)

    def turn(g, _):
        block = cot[at(4 * g, 4)].reshape(256, 256)
        turned = dot_nt(ident, block).astype(BF16)
        mir_send[:, :, at(16 * g, 16), :] = turned.reshape(4, 4, 16, 256)
        return 0

    lax.fori_loop(0, 8, turn, 0)

    low = iota((32, 8, 256), 1) < 4

    def put(ref, t, tile):
        ref[at(TAPS * t + TILE, TILE), :] = tile.reshape(TILE, 256).astype(BF16)

    load_feat.wait()
    prev[...] = jnp.zeros_like(prev)

    def activate(k, _):
        x = feat[:, at(16 * k, 16), :].astype(F32)
        for h in range(2):
            t = 2 * k + h
            v = x[:, 8 * h : 8 * h + 8, :]
            s = sigmoid(v)
            slope[at(TILE * t, TILE), :] = (s * (1.0 + v * (1.0 - s))).reshape(TILE, 256)
            turned = pltpu.roll(v * s, 4, 1)
            put(act, t, jnp.where(low, prev[...], turned))
            prev[...] = turned
        return 0

    lax.fori_loop(0, 4, activate, 0)
    put(act, TILES, jnp.where(low, prev[...], 0.0))

    def halo_copies(phase, ref):
        pairs = [
            (ns_send.at[phase, 1], ns_recv.at[phase, 0]),
            (ns_send.at[phase, 0], ns_recv.at[phase, 1]),
            (ew_send.at[phase], ew_recv.at[phase, 0]),
            (ew_send.at[phase], ew_recv.at[phase, 1]),
            (ns_send.at[phase, 1, :, 128:256], corner.at[phase, 0]),
            (ns_send.at[phase, 1, :, 0:128], corner.at[phase, 1]),
            (ns_send.at[phase, 0, :, 128:256], corner.at[phase, 2]),
            (ns_send.at[phase, 0, :, 0:128], corner.at[phase, 3]),
        ]
        return [
            pltpu.make_async_remote_copy(
                src_ref=src,
                dst_ref=dst,
                send_sem=halo_ssem.at[phase, n],
                recv_sem=halo_rsem.at[phase, n],
                device_id=beside(*sides[n]),
                device_id_type=MESH,
            )
            for n, (src, dst) in enumerate(pairs)
        ]

    def halo_pack(phase, ref):
        ns_send[phase, 0] = pack(ref[TILE : 2 * TILE, :].astype(F32), False)
        ns_send[phase, 1] = pack(ref[TAPS * TILES + TILE : TAPS * TILES + 2 * TILE, :].astype(F32), True)
        j, lane = iota((256, 128), 0), iota((256, 128), 1)

        def gather(t, total):
            pick = ((lane == 4 * t + j) & (j < 4)) | ((lane == 4 * t + j - 188) & (j >= 252))
            return total + dot(ref[at(TAPS * t + TILE, TILE), :], pick.astype(F32).astype(BF16))

        edge = lax.fori_loop(0, TILES + 1, gather, jnp.zeros((256, 128), F32))
        ew_send[phase] = edge.astype(BF16)

    def halo_fill(phase, ref):
        up, down, left, right = c > 0, c < COLS - 1, r > 0, r < ROWS - 1

        def only(flag, value):
            return jnp.where(flag, value, 0.0)

        def add(t, value):
            rows = slice(TAPS * t + TILE, TAPS * t + 2 * TILE)
            ref[rows, :] = (ref[rows, :].astype(F32) + value).astype(BF16)

        add(0, only(up, unpack(ns_recv[phase, 0], True)))
        add(TILES, only(down, unpack(ns_recv[phase, 1], False)))
        lane = iota((256, 128), 1)
        west = only(left, ew_recv[phase, 0].astype(F32))
        nw = pltpu.roll(unpack(corner[phase, 0], True), 68, 1)
        sw = pltpu.roll(unpack(corner[phase, 2], False), 100, 1)
        west = west + only(left & up, jnp.where((lane >= 64) & (lane < 68), nw, 0.0))
        west = west + only(left & down, jnp.where((lane >= 96) & (lane < 100), sw, 0.0))
        east = only(right, ew_recv[phase, 1].astype(F32))
        ne = unpack(corner[phase, 1], True)
        se = pltpu.roll(unpack(corner[phase, 3], False), 32, 1)
        east = east + only(right & up, jnp.where(lane < 4, ne, 0.0))
        east = east + only(right & down, jnp.where((lane >= 32) & (lane < 36), se, 0.0))
        edge = jnp.where(lane < 64, east, west).astype(BF16)
        from_j, to_j = iota((256, 512), 0), iota((256, 512), 1)
        shift = ((to_j < 256) & (from_j == to_j - 4)) | ((to_j >= 256) & (from_j == to_j - 252) )
        shift = shift.astype(F32).astype(BF16)
        lane, col = iota((128, 512), 0), iota((128, 512), 1)

        def spread(t, _):
            place = ((col < 4) & (lane == 64 + 4 * t + col)) | ((col >= 508) & (lane == 4 * t + col - 508))
            place = place.astype(F32).astype(BF16)
            both = dot(ref[at(TAPS * t + TILE, TILE), :], shift) + dot(edge, place)
            ref[at(TAPS * t, TILE), :] = both[:, :256].astype(BF16)
            ref[at(TAPS * t + 2 * TILE, TILE), :] = both[:, 256:].astype(BF16)
            return 0

        lax.fori_loop(0, TILES + 1, spread, 0)

    halo_pack(0, act)

    def mirror_copy(d, k):
        q = lax.rem(b + d, 4)
        return pltpu.make_async_remote_copy(
            src_ref=mir_send.at[q, k],
            dst_ref=mir_recv.at[b, k],
            send_sem=mir_ssem.at[d, k],
            recv_sem=mir_rsem.at[d, k],
            device_id=mirror_at(q),
            device_id_type=MESH,
        )

    def own_copy(k):
        return pltpu.make_async_copy(mir_send.at[b, k], mir_recv.at[b, k], mir_rsem.at[0, k])

    pl.semaphore_wait(barrier, 4 + 8 + 2 * (GROUP - 1) - own_mirror.astype(jnp.int32))
    for copy in halo_copies(0, act):
        copy.start()

    def send_chunk(k, _):
        @pl.when(own_mirror)
        def _():
            own_copy(k).start()

        @pl.when(jnp.logical_not(own_mirror))
        def _():
            mirror_copy(0, k).start()

        for d in range(1, 4):
            mirror_copy(d, k).start()
        return 0

    lax.fori_loop(0, 4, send_chunk, 0)

    spread_out = (lax.div(iota((256, 32), 0), 8) == iota((256, 32), 1)).astype(F32).astype(BF16)
    spread_in = (lax.div(iota((32, 256), 1), 8) == iota((32, 256), 0)).astype(F32).astype(BF16)
    row_out, row_in = lax.rem(iota((256, 256), 0), 8), lax.rem(iota((256, 256), 1), 8)

    def expand(w, turned):
        rows = dot_nt(spread_out, w) if turned else dot(spread_out, w)
        return dot(rows.astype(BF16), spread_in)

    def banded(taps):
        near = jnp.where(row_in == row_out, taps[0], 0.0) + jnp.where(row_in == row_out + 4, taps[1], 0.0)
        far = jnp.where(row_in == row_out, taps[2], 0.0) + jnp.where(row_in == row_out - 4, taps[1], 0.0)
        return near.astype(BF16), far.astype(BF16)

    for tap in range(3):
        near, far = banded([expand(wconv_ref[n, tap], False) for n in range(3)])
        mat_f[:, tap * TILE : (tap + 1) * TILE] = near
        mat_f[:, TAPS + tap * TILE : TAPS + (tap + 1) * TILE] = far
        near, far = banded([expand(wconv_ref[2 - n, 2 - tap], True) for n in range(3)])
        mat_b[:, tap * TILE : (tap + 1) * TILE] = near
        mat_b[:, TAPS + tap * TILE : TAPS + (tap + 1) * TILE] = far
    mat_p[...] = jnp.where(row_in == row_out, expand(wpoint_ref[...], True), 0.0).astype(BF16)

    bias_col = jnp.sum(
        jnp.where(lax.div(iota((256, 32), 0), 8) == iota((256, 32), 1), bias_ref[...], 0.0), axis=1, keepdims=True
    )
    mask_row = mask_ref[pl.ds(a, 1), :].astype(F32)
    diagonal = iota((64, 256), 1) == iota((64, 256), 0) + 64 * b
    row_keep = jnp.sum(jnp.where(diagonal, mask_row, 0.0), axis=1, keepdims=True)
    keep[...] = row_keep * (0.5 * mask_ref[pl.ds(r, 1), :].astype(F32))

    csum[...] = jnp.zeros_like(csum)
    psum[...] = jnp.zeros_like(psum)
    bsum[...] = jnp.zeros_like(bsum)

    for copy in halo_copies(0, act):
        copy.wait_recv()
    halo_fill(0, act)

    def forward(t, _):
        v = dot(mat_f[...], act[pl.ds(pl.multiple_of(TAPS * t, TAPS), 2 * TAPS), :])
        v = v + bias_col
        s = sigmoid(v)
        post[at(TILE * t, TILE), :] = (v * s).astype(BF16)
        pre_slope[at(TILE * t, TILE), :] = s * (1.0 + v * (1.0 - s))
        return 0

    lax.fori_loop(0, TILES, forward, 0)

    prev[...] = jnp.zeros_like(prev)
    left_half = iota((8, 8, 128), 2) < 64

    def chunk(k, _):
        @pl.when(own_mirror)
        def _():
            own_copy(k).wait()

        @pl.when(jnp.logical_not(own_mirror))
        def _():
            mirror_copy(0, k).wait_recv()

        for d in range(1, 4):
            mirror_copy(d, k).wait_recv()

        here = cot[:, at(16 * k, 16), :].astype(F32)
        keep_rows = keep[at(16 * k, 16), :]
        got = [mir_recv[n, k].astype(F32).reshape(8, 16, 256) for n in range(4)]
        for h in range(2):
            t = 2 * k + h
            part = [v[:, 8 * h : 8 * h + 8, :] for v in got]
            quads = []
            for m in range(4):
                cols = slice(128 * (m // 2), 128 * (m // 2) + 128)
                pieces = []
                for n in (0, 2):
                    one, two = part[n][:, :, cols], part[n + 1][:, :, cols]
                    if m % 2 == 0:
                        pieces.append(jnp.where(left_half, one, pltpu.roll(two, 64, 2)))
                    else:
                        pieces.append(jnp.where(left_half, pltpu.roll(one, 64, 2), two))
                quads.append(jnp.concatenate(pieces, axis=2))
            mirrored = jnp.stack(quads, axis=1).reshape(32, 8, 256)
            residual = keep_rows[8 * h : 8 * h + 8][None] * (here[:, 8 * h : 8 * h + 8, :] + mirrored)
            residual = residual.reshape(TILE, 256)
            half = residual.astype(BF16)
            res[at(TILE * t, TILE), :] = residual
            res_half[at(TILE * t, TILE), :] = half
            g = pre_slope[at(TILE * t, TILE), :] * dot(mat_p[...], half)
            gnat[at(TILE * t, TILE), :] = g.astype(BF16)
            turned = pltpu.roll(g.reshape(32, 8, 256), 4, 1)
            put(grad, t, jnp.where(low, prev[...], turned))
            prev[...] = turned

        @pl.when(k == 3)
        def _():
            put(grad, TILES, jnp.where(low, prev[...], 0.0))
            halo_pack(1, grad)
            for copy in halo_copies(1, grad):
                copy.start()

        total, point, line = csum[...], psum[...], bsum[...]
        for h in range(2):
            t = 2 * k + h
            g = gnat[at(TILE * t, TILE), :]
            total = total + dot_nt(g, act[pl.ds(pl.multiple_of(TAPS * t, TAPS), 2 * TAPS), :])
            point = point + dot_nt(res_half[at(TILE * t, TILE), :], post[at(TILE * t, TILE), :])
            wide = g.astype(F32)
            line = line + wide[:, :128] + wide[:, 128:]
        csum[...] = total
        psum[...] = point
        bsum[...] = line
        return 0

    lax.fori_loop(0, 4, chunk, 0)

    col_in = lax.div(iota((256, 128), 0), 8)
    col_out = iota((256, 128), 1)
    for quad in range(3):
        lanes = jnp.zeros((256, 128), F32)
        for slot in range(4):
            n = 4 * quad + slot
            if n > 9:
                continue
            if n == 9:
                v = jnp.where(row_in == row_out, psum[...], 0.0)
            else:
                row_tap, col_tap = n // 3, n % 3
                near = csum[:, col_tap * TILE : (col_tap + 1) * TILE]
                far = csum[:, TAPS + col_tap * TILE : TAPS + (col_tap + 1) * TILE]
                if row_tap == 0:
                    v = jnp.where(row_in == row_out, near, 0.0)
                elif row_tap == 2:
                    v = jnp.where(row_in == row_out, far, 0.0)
                else:
                    v = jnp.where(row_in == row_out + 4, near, 0.0) + jnp.where(row_in == row_out - 4, far, 0.0)
            pick = (col_out == 32 * slot + col_in).astype(F32).astype(BF16)
            high = v.astype(BF16)
            lanes = lanes + (dot(high, pick) + dot((v - high.astype(F32)).astype(BF16), pick))
        if quad == 2:
            line = jnp.sum(bsum[...], axis=1, keepdims=True)
            lanes = lanes + jnp.where((col_out >= 64) & (col_out < 96), line, 0.0)
        lanes = jnp.sum(lanes.reshape(32, 8, 128), axis=1)
        for o in range(4):
            payload[4 * quad + o] = lanes[8 * o : 8 * o + 8]
    for o in range(4):
        payload[12 + o] = jnp.zeros((8, 128), F32)

    def exchange(stage, me, member, source, dst):
        def copy(d):
            to = lax.rem(me + d, GROUP)
            return pltpu.make_async_remote_copy(
                src_ref=source(to),
                dst_ref=dst.at[me],
                send_sem=red_ssem.at[stage, d],
                recv_sem=red_rsem.at[stage, d],
                device_id=member(to),
                device_id_type=MESH,
            )

        def start(d, _):
            copy(d).start()
            return 0

        def arrive(d, _):
            copy(d).wait_recv()
            return 0

        def leave(d, _):
            copy(d).wait_send()
            return 0

        return (
            lambda: lax.fori_loop(1, GROUP, start, 0),
            lambda: lax.fori_loop(1, GROUP, arrive, 0),
            lambda: lax.fori_loop(1, GROUP, leave, 0),
        )

    start1, arrive1, leave1 = exchange(0, group_a, member_a, lambda m: payload.at[m], part1)
    start2, arrive2, leave2 = exchange(1, group_b, member_b, lambda m: sum1, part2)
    start3, arrive3, leave3 = exchange(2, group_a, member_a, lambda m: sum2, part3)

    def total_of(ref):
        total = ref[0]
        for n in range(1, GROUP):
            total = total + ref[n]
        return total

    part1[group_a] = payload[group_a]
    start1()

    for copy in halo_copies(1, grad):
        copy.wait_recv()
    halo_fill(1, grad)

    arrive1()
    sum1[...] = total_of(part1)
    part2[group_b] = sum1[...]
    start2()

    def store_out(k):
        rows = at(16 * k, 16)
        return pltpu.make_async_copy(out.at[:, rows, :], fg_hbm.at[:, rows, :], out_sem.at[k])

    def backward(k, _):
        halves = []
        for h in range(2):
            t = 2 * k + h
            v = dot(mat_b[...], grad[pl.ds(pl.multiple_of(TAPS * t, TAPS), 2 * TAPS), :])
            v = res[at(TILE * t, TILE), :] + slope[at(TILE * t, TILE), :] * v
            halves.append(v.reshape(32, 8, 256))
        out[:, at(16 * k, 16), :] = jnp.concatenate(halves, axis=1).astype(BF16)
        store_out(k).start()
        return 0

    lax.fori_loop(0, 2, backward, 0)
    arrive2()
    sum2[...] = total_of(part2)
    part3[group_a] = sum2[...]
    start3()
    lax.fori_loop(2, 4, backward, 0)
    arrive3()

    scale = 1.0 / 2048.0
    for quad in range(3):
        lanes = jnp.concatenate([part3[4 * quad + o] for o in range(4)], axis=0) * scale
        for slot in range(4):
            n = 4 * quad + slot
            block = lanes if slot == 0 else pltpu.roll(lanes, 128 - 32 * slot, 1)
            if n < 9:
                conv_ref[n // 3, n % 3] = block[:, :32]
            elif n == 9:
                point_ref[...] = block[:, :32]
            elif n == 10:
                square = block[:, :32]
                biasg_ref[...] = jnp.sum(
                    jnp.where(iota((32, 32), 0) == iota((32, 32), 1), square, 0.0), axis=0, keepdims=True
                )

    @pl.when(jnp.logical_not(own_mirror))
    def _():
        for k in range(4):
            mirror_copy(0, k).wait_send()

    for d in range(1, 4):
        for k in range(4):
            mirror_copy(d, k).wait_send()
    for phase, ref in ((0, act), (1, grad)):
        for copy in halo_copies(phase, ref):
            copy.wait_send()
    leave1()
    leave2()
    leave3()
    for k in range(4):
        store_out(k).wait()


def shards(features, cotangent, mask, w_conv, w_point, bias):
    vmem = pl.BlockSpec(memory_space=pltpu.VMEM)
    hbm = pl.BlockSpec(memory_space=pl.ANY)
    big = (TILES * TILE, 256)
    fg, conv, point, bias_grad = pl.pallas_call(
        kernel,
        out_shape=(
            jax.ShapeDtypeStruct((32, 64, 256), BF16),
            jax.ShapeDtypeStruct((3, 3, 32, 32), F32),
            jax.ShapeDtypeStruct((32, 32), F32),
            jax.ShapeDtypeStruct((1, 32), F32),
        ),
        in_specs=[hbm, hbm, vmem, vmem, vmem, vmem],
        out_specs=(hbm, vmem, vmem, vmem),
        scratch_shapes=[
            pltpu.VMEM((32, 64, 256), BF16),
            pltpu.VMEM((32, 64, 256), BF16),
            pltpu.VMEM((4, 4, 128, 256), BF16),
            pltpu.VMEM((4, 4, 128, 256), BF16),
            pltpu.VMEM(((TILES + 1) * TAPS, 256), BF16),
            pltpu.VMEM(((TILES + 1) * TAPS, 256), BF16),
            pltpu.VMEM(big, F32),
            pltpu.VMEM(big, BF16),
            pltpu.VMEM(big, F32),
            pltpu.VMEM(big, F32),
            pltpu.VMEM(big, BF16),
            pltpu.VMEM(big, BF16),
            pltpu.VMEM((TILE, 2 * TAPS), BF16),
            pltpu.VMEM((TILE, 2 * TAPS), BF16),
            pltpu.VMEM((TILE, TILE), BF16),
            pltpu.VMEM((64, 256), F32),
            pltpu.VMEM((32, 8, 256), F32),
            pltpu.VMEM((TILE, 2 * TAPS), F32),
            pltpu.VMEM((TILE, TILE), F32),
            pltpu.VMEM((TILE, 128), F32),
            pltpu.VMEM((32, 64, 256), BF16),
            pltpu.VMEM((2, 2, 128, 256), BF16),
            pltpu.VMEM((2, 256, 128), BF16),
            pltpu.VMEM((2, 2, 128, 256), BF16),
            pltpu.VMEM((2, 2, 256, 128), BF16),
            pltpu.VMEM((2, 4, 128, 128), BF16),
            pltpu.VMEM((GROUP, 8, 128), F32),
            pltpu.VMEM((GROUP, 8, 128), F32),
            pltpu.VMEM((8, 128), F32),
            pltpu.VMEM((GROUP, 8, 128), F32),
            pltpu.VMEM((8, 128), F32),
            pltpu.VMEM((GROUP, 8, 128), F32),
            pltpu.SemaphoreType.DMA((2,)),
            pltpu.SemaphoreType.DMA((4,)),
            pltpu.SemaphoreType.DMA((4, 4)),
            pltpu.SemaphoreType.DMA((4, 4)),
            pltpu.SemaphoreType.DMA((2, 8)),
            pltpu.SemaphoreType.DMA((2, 8)),
            pltpu.SemaphoreType.DMA((3, GROUP)),
            pltpu.SemaphoreType.DMA((3, GROUP)),
        ],
        compiler_params=pltpu.CompilerParams(
            collective_id=0, has_side_effects=True, vmem_limit_bytes=56 * 1024 * 1024
        ),
        cost_estimate=pl.CostEstimate(flops=5_400_000_000, bytes_accessed=3 * 1024 * 1024, transcendentals=2_000_000),
    )(features, cotangent, mask.reshape(8, 256), w_conv, w_point, bias.reshape(1, 32))
    return fg, conv, point, bias_grad.reshape(32)


def solution(mesh):
    in_specs = (P(None, "col", "row"), P(None, "col", "row"), P(), P(), P(), P())
    out_specs = (P(None, "col", "row"), P(), P(), P())
    return jax.shard_map(shards, mesh=mesh, in_specs=in_specs, out_specs=out_specs, check_vma=False)
```

```python
import jax
import jax.numpy as jnp
from jax import lax
from jax.experimental import pallas as pl
from jax.experimental.pallas import tpu as pltpu
from jax.sharding import PartitionSpec as P

F32, BF16 = jnp.float32, jnp.bfloat16
MESH = pl.DeviceIdType.MESH
ROWS, COLS = 8, 32
TILE = 256
TAPS = 3 * TILE
TILES = 8
GROUP = 16
NT = (((1,), (1,)), ((), ()))


def iota(shape, dim):
    return lax.broadcasted_iota(jnp.int32, shape, dim)


def dot(x, y):
    return jnp.dot(x, y, preferred_element_type=F32)


def dot_nt(x, y):
    return lax.dot_general(x, y, NT, preferred_element_type=F32)


def at(start, size):
    return pl.ds(pl.multiple_of(start, size), size)


def sigmoid(v):
    return 1.0 / (1.0 + jnp.exp(-v))


def pack(tile, bottom):
    v = tile.reshape(16, 2, 8, 256)
    low = iota((16, 8, 256), 1) < 4
    if bottom:
        v = jnp.where(low, v[:, 0], pltpu.roll(v[:, 1], 4, 1))
    else:
        v = jnp.where(low, pltpu.roll(v[:, 0], 4, 1), v[:, 1])
    return v.reshape(128, 256).astype(BF16)


def unpack(packed, bottom):
    width = packed.shape[1]
    v = packed.astype(F32).reshape(16, 8, width)
    turned = pltpu.roll(v, 4, 1)
    low = iota((16, 8, width), 1) < 4
    if bottom:
        pair = [jnp.where(low, v, 0.0), jnp.where(low, turned, 0.0)]
    else:
        pair = [jnp.where(low, 0.0, turned), jnp.where(low, 0.0, v)]
    return jnp.stack(pair, axis=1).reshape(TILE, width)


def kernel(
    feat_hbm, cot_hbm, mask_ref, wconv_ref, wpoint_ref, bias_ref,
    fg_hbm, conv_ref, point_ref, biasg_ref,
    feat, cot, mir_send, relay, mir_recv, act, grad, res, res_half, slope, pre_slope, post, gnat,
    mat_f, mat_b, mat_p, keep, prev, csum, psum, bsum, out,
    ns_send, ew_send, ns_recv, ew_recv, corner, payload, part1, sum1, part2, sum2, part3,
    in_sem, out_sem, spread_ssem, spread_rsem, mir_ssem, mir_rsem, halo_ssem, halo_rsem, red_ssem, red_rsem,
):
    r, c = lax.axis_index("row"), lax.axis_index("col")
    a, b = lax.div(c, 4), lax.rem(c, 4)
    y, zh = lax.div(c, 8), lax.rem(a, 2)
    group_a, group_b = zh * 8 + r, y * 4 + b

    def relay_to(row):
        return {"row": 2 * row + zh, "col": 4 * r + b}

    def relay_from(row):
        return {"row": a, "col": 8 * row + 4 * lax.rem(r, 2) + b}

    def member_a(m):
        return {"row": lax.rem(m, 8), "col": y * 8 + lax.div(m, 8) * 4 + b}

    def member_b(m):
        return {"row": r, "col": lax.div(m, 4) * 8 + zh * 4 + lax.rem(m, 4)}

    def beside(dr, dc):
        return {"row": lax.rem(r + dr + ROWS, ROWS), "col": lax.rem(c + dc + COLS, COLS)}

    own_mirror = a == r
    sides = [(0, 1), (0, -1), (1, 0), (-1, 0), (1, 1), (-1, 1), (1, -1), (-1, -1)]

    barrier = pltpu.get_barrier_semaphore()

    def greet(device):
        pl.semaphore_signal(barrier, inc=1, device_id=device, device_id_type=MESH)

    @pl.when(jnp.logical_not(own_mirror))
    def _():
        greet(relay_to(y))
        greet(relay_from(y))

    for d in range(1, 4):
        greet(relay_to(lax.rem(y + d, 4)))
        greet(relay_from(lax.rem(y + d, 4)))
    for dr, dc in sides:
        greet(beside(dr, dc))

    def greet_groups(d, _):
        greet(member_a(lax.rem(group_a + d, GROUP)))
        greet(member_b(lax.rem(group_b + d, GROUP)))
        return 0

    lax.fori_loop(1, GROUP, greet_groups, 0)

    load_cot = pltpu.make_async_copy(cot_hbm, cot, in_sem.at[0])
    load_feat = pltpu.make_async_copy(feat_hbm, feat, in_sem.at[1])
    load_cot.start()
    load_feat.start()

    load_cot.wait()
    ident = (iota((256, 256), 0) == iota((256, 256), 1)).astype(BF16)

    def turn(g, _):
        block = cot[at(4 * g, 4)].reshape(256, 256)
        turned = dot_nt(ident, block).astype(BF16)
        mir_send[:, :, at(16 * g, 16), :] = turned.reshape(4, 4, 16, 256)
        return 0

    lax.fori_loop(0, 8, turn, 0)

    low = iota((32, 8, 256), 1) < 4

    def put(ref, t, tile):
        ref[at(TAPS * t + TILE, TILE), :] = tile.reshape(TILE, 256).astype(BF16)

    def activations():
        load_feat.wait()
        prev[...] = jnp.zeros_like(prev)

        def activate(k, _):
            x = feat[:, at(16 * k, 16), :].astype(F32)
            for h in range(2):
                t = 2 * k + h
                v = x[:, 8 * h : 8 * h + 8, :]
                s = sigmoid(v)
                slope[at(TILE * t, TILE), :] = (s * (1.0 + v * (1.0 - s))).reshape(TILE, 256)
                turned = pltpu.roll(v * s, 4, 1)
                put(act, t, jnp.where(low, prev[...], turned))
                prev[...] = turned
            return 0

        lax.fori_loop(0, 4, activate, 0)
        put(act, TILES, jnp.where(low, prev[...], 0.0))

    def halo_copies(phase, ref):
        pairs = [
            (ns_send.at[phase, 1], ns_recv.at[phase, 0]),
            (ns_send.at[phase, 0], ns_recv.at[phase, 1]),
            (ew_send.at[phase], ew_recv.at[phase, 0]),
            (ew_send.at[phase], ew_recv.at[phase, 1]),
            (ns_send.at[phase, 1, :, 128:256], corner.at[phase, 0]),
            (ns_send.at[phase, 1, :, 0:128], corner.at[phase, 1]),
            (ns_send.at[phase, 0, :, 128:256], corner.at[phase, 2]),
            (ns_send.at[phase, 0, :, 0:128], corner.at[phase, 3]),
        ]
        return [
            pltpu.make_async_remote_copy(
                src_ref=src,
                dst_ref=dst,
                send_sem=halo_ssem.at[phase, n],
                recv_sem=halo_rsem.at[phase, n],
                device_id=beside(*sides[n]),
                device_id_type=MESH,
            )
            for n, (src, dst) in enumerate(pairs)
        ]

    def halo_pack(phase, ref):
        ns_send[phase, 0] = pack(ref[TILE : 2 * TILE, :].astype(F32), False)
        ns_send[phase, 1] = pack(ref[TAPS * TILES + TILE : TAPS * TILES + 2 * TILE, :].astype(F32), True)
        j, lane = iota((256, 128), 0), iota((256, 128), 1)

        def gather(t, total):
            pick = ((lane == 4 * t + j) & (j < 4)) | ((lane == 4 * t + j - 188) & (j >= 252))
            return total + dot(ref[at(TAPS * t + TILE, TILE), :], pick.astype(F32).astype(BF16))

        edge = lax.fori_loop(0, TILES + 1, gather, jnp.zeros((256, 128), F32))
        ew_send[phase] = edge.astype(BF16)

    def halo_fill(phase, ref):
        up, down, left, right = c > 0, c < COLS - 1, r > 0, r < ROWS - 1

        def only(flag, value):
            return jnp.where(flag, value, 0.0)

        def add(t, value):
            rows = slice(TAPS * t + TILE, TAPS * t + 2 * TILE)
            ref[rows, :] = (ref[rows, :].astype(F32) + value).astype(BF16)

        add(0, only(up, unpack(ns_recv[phase, 0], True)))
        add(TILES, only(down, unpack(ns_recv[phase, 1], False)))
        lane = iota((256, 128), 1)
        west = only(left, ew_recv[phase, 0].astype(F32))
        nw = pltpu.roll(unpack(corner[phase, 0], True), 68, 1)
        sw = pltpu.roll(unpack(corner[phase, 2], False), 100, 1)
        west = west + only(left & up, jnp.where((lane >= 64) & (lane < 68), nw, 0.0))
        west = west + only(left & down, jnp.where((lane >= 96) & (lane < 100), sw, 0.0))
        east = only(right, ew_recv[phase, 1].astype(F32))
        ne = unpack(corner[phase, 1], True)
        se = pltpu.roll(unpack(corner[phase, 3], False), 32, 1)
        east = east + only(right & up, jnp.where(lane < 4, ne, 0.0))
        east = east + only(right & down, jnp.where((lane >= 32) & (lane < 36), se, 0.0))
        edge = jnp.where(lane < 64, east, west).astype(BF16)
        from_j, to_j = iota((256, 512), 0), iota((256, 512), 1)
        shift = ((to_j < 256) & (from_j == to_j - 4)) | ((to_j >= 256) & (from_j == to_j - 252) )
        shift = shift.astype(F32).astype(BF16)
        lane, col = iota((128, 512), 0), iota((128, 512), 1)

        def spread(t, _):
            place = ((col < 4) & (lane == 64 + 4 * t + col)) | ((col >= 508) & (lane == 4 * t + col - 508))
            place = place.astype(F32).astype(BF16)
            both = dot(ref[at(TAPS * t + TILE, TILE), :], shift) + dot(edge, place)
            ref[at(TAPS * t, TILE), :] = both[:, :256].astype(BF16)
            ref[at(TAPS * t + 2 * TILE, TILE), :] = both[:, 256:].astype(BF16)
            return 0

        lax.fori_loop(0, TILES + 1, spread, 0)

    def steps(n):
        dx = lax.rem(n, 4)
        return dx, lax.rem(dx + lax.div(n, 4), 4)

    def spread_copy(n):
        dx, dy = steps(n)
        to_x, to_y = lax.rem(b + dx, 4), lax.rem(y + dy, 4)
        return pltpu.make_async_remote_copy(
            src_ref=mir_send.at[to_x, to_y],
            dst_ref=relay.at[y, b],
            send_sem=spread_ssem.at[n],
            recv_sem=spread_rsem.at[n],
            device_id=member_b(4 * to_y + to_x),
            device_id_type=MESH,
        )

    def relay_copy(n):
        dx, dy = steps(n)
        from_x, from_y = lax.rem(b - dx + 4, 4), lax.rem(y - dy + 4, 4)
        return pltpu.make_async_remote_copy(
            src_ref=relay.at[from_y, from_x],
            dst_ref=mir_recv.at[from_x, y],
            send_sem=mir_ssem.at[n],
            recv_sem=mir_rsem.at[from_x, y],
            device_id=relay_to(from_y),
            device_id_type=MESH,
        )

    def own_copy(n):
        from_x = lax.rem(b - steps(n)[0] + 4, 4)
        return pltpu.make_async_copy(relay.at[y, from_x], mir_recv.at[from_x, y], mir_rsem.at[from_x, y])

    def stays(n):
        return own_mirror & (steps(n)[1] == 0)

    def start_relay(n):
        @pl.when(stays(n))
        def _():
            own_copy(n).start()

        @pl.when(jnp.logical_not(stays(n)))
        def _():
            relay_copy(n).start()

    def arrival(k, n):
        return pltpu.make_async_remote_copy(
            src_ref=relay.at[0, n],
            dst_ref=mir_recv.at[n, k],
            send_sem=mir_ssem.at[n],
            recv_sem=mir_rsem.at[n, k],
            device_id=relay_from(k),
            device_id_type=MESH,
        )

    def own_arrival(n):
        return pltpu.make_async_copy(relay.at[y, n], mir_recv.at[n, y], mir_rsem.at[n, y])

    relay[y, b] = mir_send[b, y]
    pl.semaphore_wait(barrier, 8 + 8 + 2 * (GROUP - 1) - 2 * own_mirror.astype(jnp.int32))

    def send_spread(n, _):
        spread_copy(n).start()
        return 0

    lax.fori_loop(1, GROUP, send_spread, 0)
    start_relay(0)
    activations()
    halo_pack(0, act)
    for copy in halo_copies(0, act):
        copy.start()

    spread_out = (lax.div(iota((256, 32), 0), 8) == iota((256, 32), 1)).astype(F32).astype(BF16)
    spread_in = (lax.div(iota((32, 256), 1), 8) == iota((32, 256), 0)).astype(F32).astype(BF16)
    row_out, row_in = lax.rem(iota((256, 256), 0), 8), lax.rem(iota((256, 256), 1), 8)

    def expand(w, turned):
        rows = dot_nt(spread_out, w) if turned else dot(spread_out, w)
        return dot(rows.astype(BF16), spread_in)

    def banded(taps):
        near = jnp.where(row_in == row_out, taps[0], 0.0) + jnp.where(row_in == row_out + 4, taps[1], 0.0)
        far = jnp.where(row_in == row_out, taps[2], 0.0) + jnp.where(row_in == row_out - 4, taps[1], 0.0)
        return near.astype(BF16), far.astype(BF16)

    for tap in range(3):
        near, far = banded([expand(wconv_ref[n, tap], False) for n in range(3)])
        mat_f[:, tap * TILE : (tap + 1) * TILE] = near
        mat_f[:, TAPS + tap * TILE : TAPS + (tap + 1) * TILE] = far
        near, far = banded([expand(wconv_ref[2 - n, 2 - tap], True) for n in range(3)])
        mat_b[:, tap * TILE : (tap + 1) * TILE] = near
        mat_b[:, TAPS + tap * TILE : TAPS + (tap + 1) * TILE] = far
    mat_p[...] = jnp.where(row_in == row_out, expand(wpoint_ref[...], True), 0.0).astype(BF16)

    bias_col = jnp.sum(
        jnp.where(lax.div(iota((256, 32), 0), 8) == iota((256, 32), 1), bias_ref[...], 0.0), axis=1, keepdims=True
    )
    mask_row = mask_ref[:, at(256 * a, 256)].astype(F32)
    diagonal = iota((64, 256), 1) == iota((64, 256), 0) + 64 * b
    row_keep = jnp.sum(jnp.where(diagonal, mask_row, 0.0), axis=1, keepdims=True)
    keep[...] = row_keep * (0.5 * mask_ref[:, at(256 * r, 256)].astype(F32))

    csum[...] = jnp.zeros_like(csum)
    psum[...] = jnp.zeros_like(psum)
    bsum[...] = jnp.zeros_like(bsum)

    def pass_on(n, _):
        spread_copy(n).wait_recv()
        start_relay(n)
        return 0

    lax.fori_loop(1, GROUP, pass_on, 0)
    for copy in halo_copies(0, act):
        copy.wait_recv()
    halo_fill(0, act)

    def forward(t, _):
        v = dot(mat_f[...], act[pl.ds(pl.multiple_of(TAPS * t, TAPS), 2 * TAPS), :])
        v = v + bias_col
        s = sigmoid(v)
        post[at(TILE * t, TILE), :] = (v * s).astype(BF16)
        pre_slope[at(TILE * t, TILE), :] = s * (1.0 + v * (1.0 - s))
        return 0

    lax.fori_loop(0, TILES, forward, 0)

    prev[...] = jnp.zeros_like(prev)
    left_half = iota((8, 8, 128), 2) < 64

    def chunk(k, _):
        in_place = own_mirror & (k == y)

        @pl.when(in_place)
        def _():
            for n in range(4):
                own_arrival(n).wait()

        @pl.when(jnp.logical_not(in_place))
        def _():
            for n in range(4):
                arrival(k, n).wait_recv()

        here = cot[:, at(16 * k, 16), :].astype(F32)
        keep_rows = keep[at(16 * k, 16), :]
        got = [mir_recv[n, k].astype(F32).reshape(8, 16, 256) for n in range(4)]
        for h in range(2):
            t = 2 * k + h
            part = [v[:, 8 * h : 8 * h + 8, :] for v in got]
            quads = []
            for m in range(4):
                cols = slice(128 * (m // 2), 128 * (m // 2) + 128)
                pieces = []
                for n in (0, 2):
                    one, two = part[n][:, :, cols], part[n + 1][:, :, cols]
                    if m % 2 == 0:
                        pieces.append(jnp.where(left_half, one, pltpu.roll(two, 64, 2)))
                    else:
                        pieces.append(jnp.where(left_half, pltpu.roll(one, 64, 2), two))
                quads.append(jnp.concatenate(pieces, axis=2))
            mirrored = jnp.stack(quads, axis=1).reshape(32, 8, 256)
            residual = keep_rows[8 * h : 8 * h + 8][None] * (here[:, 8 * h : 8 * h + 8, :] + mirrored)
            residual = residual.reshape(TILE, 256)
            half = residual.astype(BF16)
            res[at(TILE * t, TILE), :] = residual
            res_half[at(TILE * t, TILE), :] = half
            g = pre_slope[at(TILE * t, TILE), :] * dot(mat_p[...], half)
            gnat[at(TILE * t, TILE), :] = g.astype(BF16)
            turned = pltpu.roll(g.reshape(32, 8, 256), 4, 1)
            put(grad, t, jnp.where(low, prev[...], turned))
            prev[...] = turned

        @pl.when(k == 3)
        def _():
            put(grad, TILES, jnp.where(low, prev[...], 0.0))
            halo_pack(1, grad)
            for copy in halo_copies(1, grad):
                copy.start()

        total, point, line = csum[...], psum[...], bsum[...]
        for h in range(2):
            t = 2 * k + h
            g = gnat[at(TILE * t, TILE), :]
            total = total + dot_nt(g, act[pl.ds(pl.multiple_of(TAPS * t, TAPS), 2 * TAPS), :])
            point = point + dot_nt(res_half[at(TILE * t, TILE), :], post[at(TILE * t, TILE), :])
            wide = g.astype(F32)
            line = line + wide[:, :128] + wide[:, 128:]
        csum[...] = total
        psum[...] = point
        bsum[...] = line
        return 0

    lax.fori_loop(0, 4, chunk, 0)

    col_in = lax.div(iota((256, 128), 0), 8)
    col_out = iota((256, 128), 1)
    for quad in range(3):
        lanes = jnp.zeros((256, 128), F32)
        for slot in range(4):
            n = 4 * quad + slot
            if n > 9:
                continue
            if n == 9:
                v = jnp.where(row_in == row_out, psum[...], 0.0)
            else:
                row_tap, col_tap = n // 3, n % 3
                near = csum[:, col_tap * TILE : (col_tap + 1) * TILE]
                far = csum[:, TAPS + col_tap * TILE : TAPS + (col_tap + 1) * TILE]
                if row_tap == 0:
                    v = jnp.where(row_in == row_out, near, 0.0)
                elif row_tap == 2:
                    v = jnp.where(row_in == row_out, far, 0.0)
                else:
                    v = jnp.where(row_in == row_out + 4, near, 0.0) + jnp.where(row_in == row_out - 4, far, 0.0)
            pick = (col_out == 32 * slot + col_in).astype(F32).astype(BF16)
            high = v.astype(BF16)
            lanes = lanes + (dot(high, pick) + dot((v - high.astype(F32)).astype(BF16), pick))
        if quad == 2:
            line = jnp.sum(bsum[...], axis=1, keepdims=True)
            lanes = lanes + jnp.where((col_out >= 64) & (col_out < 96), line, 0.0)
        lanes = jnp.sum(lanes.reshape(32, 8, 128), axis=1)
        for o in range(4):
            payload[4 * quad + o] = lanes[8 * o : 8 * o + 8]
    for o in range(4):
        payload[12 + o] = jnp.zeros((8, 128), F32)

    def exchange(stage, me, member, source, dst):
        def copy(d):
            to = lax.rem(me + d, GROUP)
            return pltpu.make_async_remote_copy(
                src_ref=source(to),
                dst_ref=dst.at[me],
                send_sem=red_ssem.at[stage, d],
                recv_sem=red_rsem.at[stage, d],
                device_id=member(to),
                device_id_type=MESH,
            )

        def start(d, _):
            copy(d).start()
            return 0

        def arrive(d, _):
            copy(d).wait_recv()
            return 0

        def leave(d, _):
            copy(d).wait_send()
            return 0

        return (
            lambda: lax.fori_loop(1, GROUP, start, 0),
            lambda: lax.fori_loop(1, GROUP, arrive, 0),
            lambda: lax.fori_loop(1, GROUP, leave, 0),
        )

    start1, arrive1, leave1 = exchange(0, group_a, member_a, lambda m: payload.at[m], part1)
    start2, arrive2, leave2 = exchange(1, group_b, member_b, lambda m: sum1, part2)
    start3, arrive3, leave3 = exchange(2, group_a, member_a, lambda m: sum2, part3)

    def total_of(ref):
        total = ref[0]
        for n in range(1, GROUP):
            total = total + ref[n]
        return total

    part1[group_a] = payload[group_a]
    start1()

    for copy in halo_copies(1, grad):
        copy.wait_recv()
    halo_fill(1, grad)

    arrive1()
    sum1[...] = total_of(part1)
    part2[group_b] = sum1[...]
    start2()

    def store_out(k):
        rows = at(16 * k, 16)
        return pltpu.make_async_copy(out.at[:, rows, :], fg_hbm.at[:, rows, :], out_sem.at[k])

    def backward(k, _):
        halves = []
        for h in range(2):
            t = 2 * k + h
            v = dot(mat_b[...], grad[pl.ds(pl.multiple_of(TAPS * t, TAPS), 2 * TAPS), :])
            v = res[at(TILE * t, TILE), :] + slope[at(TILE * t, TILE), :] * v
            halves.append(v.reshape(32, 8, 256))
        out[:, at(16 * k, 16), :] = jnp.concatenate(halves, axis=1).astype(BF16)
        store_out(k).start()
        return 0

    lax.fori_loop(0, 2, backward, 0)
    arrive2()
    sum2[...] = total_of(part2)
    part3[group_a] = sum2[...]
    start3()
    lax.fori_loop(2, 4, backward, 0)
    arrive3()

    scale = 1.0 / 2048.0
    for quad in range(3):
        lanes = jnp.concatenate([part3[4 * quad + o] for o in range(4)], axis=0) * scale
        for slot in range(4):
            n = 4 * quad + slot
            block = lanes if slot == 0 else pltpu.roll(lanes, 128 - 32 * slot, 1)
            if n < 9:
                conv_ref[n // 3, n % 3] = block[:, :32]
            elif n == 9:
                point_ref[...] = block[:, :32]
            elif n == 10:
                square = block[:, :32]
                biasg_ref[...] = jnp.sum(
                    jnp.where(iota((32, 32), 0) == iota((32, 32), 1), square, 0.0), axis=0, keepdims=True
                )

    def left(n, _):
        @pl.when(n > 0)
        def _():
            spread_copy(n).wait_send()

        @pl.when(jnp.logical_not(stays(n)))
        def _():
            relay_copy(n).wait_send()

        return 0

    lax.fori_loop(0, GROUP, left, 0)
    for phase, ref in ((0, act), (1, grad)):
        for copy in halo_copies(phase, ref):
            copy.wait_send()
    leave1()
    leave2()
    leave3()
    for k in range(4):
        store_out(k).wait()


def shards(features, cotangent, mask, w_conv, w_point, bias):
    vmem = pl.BlockSpec(memory_space=pltpu.VMEM)
    hbm = pl.BlockSpec(memory_space=pl.ANY)
    big = (TILES * TILE, 256)
    fg, conv, point, bias_grad = pl.pallas_call(
        kernel,
        out_shape=(
            jax.ShapeDtypeStruct((32, 64, 256), BF16),
            jax.ShapeDtypeStruct((3, 3, 32, 32), F32),
            jax.ShapeDtypeStruct((32, 32), F32),
            jax.ShapeDtypeStruct((1, 32), F32),
        ),
        in_specs=[hbm, hbm, vmem, vmem, vmem, vmem],
        out_specs=(hbm, vmem, vmem, vmem),
        scratch_shapes=[
            pltpu.VMEM((32, 64, 256), BF16),
            pltpu.VMEM((32, 64, 256), BF16),
            pltpu.VMEM((4, 4, 128, 256), BF16),
            pltpu.VMEM((4, 4, 128, 256), BF16),
            pltpu.VMEM((4, 4, 128, 256), BF16),
            pltpu.VMEM(((TILES + 1) * TAPS, 256), BF16),
            pltpu.VMEM(((TILES + 1) * TAPS, 256), BF16),
            pltpu.VMEM(big, F32),
            pltpu.VMEM(big, BF16),
            pltpu.VMEM(big, F32),
            pltpu.VMEM(big, F32),
            pltpu.VMEM(big, BF16),
            pltpu.VMEM(big, BF16),
            pltpu.VMEM((TILE, 2 * TAPS), BF16),
            pltpu.VMEM((TILE, 2 * TAPS), BF16),
            pltpu.VMEM((TILE, TILE), BF16),
            pltpu.VMEM((64, 256), F32),
            pltpu.VMEM((32, 8, 256), F32),
            pltpu.VMEM((TILE, 2 * TAPS), F32),
            pltpu.VMEM((TILE, TILE), F32),
            pltpu.VMEM((TILE, 128), F32),
            pltpu.VMEM((32, 64, 256), BF16),
            pltpu.VMEM((2, 2, 128, 256), BF16),
            pltpu.VMEM((2, 256, 128), BF16),
            pltpu.VMEM((2, 2, 128, 256), BF16),
            pltpu.VMEM((2, 2, 256, 128), BF16),
            pltpu.VMEM((2, 4, 128, 128), BF16),
            pltpu.VMEM((GROUP, 8, 128), F32),
            pltpu.VMEM((GROUP, 8, 128), F32),
            pltpu.VMEM((8, 128), F32),
            pltpu.VMEM((GROUP, 8, 128), F32),
            pltpu.VMEM((8, 128), F32),
            pltpu.VMEM((GROUP, 8, 128), F32),
            pltpu.SemaphoreType.DMA((2,)),
            pltpu.SemaphoreType.DMA((4,)),
            pltpu.SemaphoreType.DMA((GROUP,)),
            pltpu.SemaphoreType.DMA((GROUP,)),
            pltpu.SemaphoreType.DMA((GROUP,)),
            pltpu.SemaphoreType.DMA((4, 4)),
            pltpu.SemaphoreType.DMA((2, 8)),
            pltpu.SemaphoreType.DMA((2, 8)),
            pltpu.SemaphoreType.DMA((3, GROUP)),
            pltpu.SemaphoreType.DMA((3, GROUP)),
        ],
        compiler_params=pltpu.CompilerParams(
            collective_id=0, has_side_effects=True, vmem_limit_bytes=56 * 1024 * 1024
        ),
        cost_estimate=pl.CostEstimate(flops=5_400_000_000, bytes_accessed=3 * 1024 * 1024, transcendentals=2_000_000),
    )(features, cotangent, mask.reshape(1, 2048), w_conv, w_point, bias.reshape(1, 32))
    return fg, conv, point, bias_grad.reshape(32)


def solution(mesh):
    in_specs = (P(None, "col", "row"), P(None, "col", "row"), P(), P(), P(), P())
    out_specs = (P(None, "col", "row"), P(), P(), P())
    return jax.shard_map(shards, mesh=mesh, in_specs=in_specs, out_specs=out_specs, check_vma=False)
```

```python
import jax
import jax.numpy as jnp
from jax import lax
from jax.experimental import pallas as pl
from jax.experimental.pallas import tpu as pltpu
from jax.sharding import PartitionSpec as P

F32, BF16 = jnp.float32, jnp.bfloat16
MESH = pl.DeviceIdType.MESH
ROWS, COLS = 8, 32
TILE = 256
TAPS = 3 * TILE
TILES = 8
GROUP = 16
NT = (((1,), (1,)), ((), ()))
TN = (((0,), (0,)), ((), ()))


def iota(shape, dim):
    return lax.broadcasted_iota(jnp.int32, shape, dim)


def dot(x, y):
    return jnp.dot(x, y, preferred_element_type=F32)


def dot_nt(x, y):
    return lax.dot_general(x, y, NT, preferred_element_type=F32)


def dot_tn(x, y):
    return lax.dot_general(x, y, TN, preferred_element_type=F32)


def one_hot(where):
    return where.astype(F32).astype(BF16)


def at(start, size):
    return pl.ds(pl.multiple_of(start, size), size)


def sigmoid(v):
    return 1.0 / (1.0 + jnp.exp(-v))


def pack(tile, bottom):
    v = tile.reshape(16, 2, 8, 256)
    low = iota((16, 8, 256), 1) < 4
    if bottom:
        v = jnp.where(low, v[:, 0], pltpu.roll(v[:, 1], 4, 1))
    else:
        v = jnp.where(low, pltpu.roll(v[:, 0], 4, 1), v[:, 1])
    return v.reshape(128, 256).astype(BF16)


def unpack(packed, bottom):
    width = packed.shape[1]
    v = packed.astype(F32).reshape(16, 8, width)
    turned = pltpu.roll(v, 4, 1)
    low = iota((16, 8, width), 1) < 4
    if bottom:
        pair = [jnp.where(low, v, 0.0), jnp.where(low, turned, 0.0)]
    else:
        pair = [jnp.where(low, 0.0, turned), jnp.where(low, 0.0, v)]
    return jnp.stack(pair, axis=1).reshape(TILE, width)


def kernel(
    feat_hbm, cot_hbm, mask_ref, wconv_ref, wpoint_ref, bias_ref,
    fg_hbm, conv_ref, point_ref, biasg_ref,
    feat, cot, mir_send, relay, mir_recv, act, grad, res, res_half, slope, pre_slope, post, gnat,
    mat_f, mat_b, mat_p, keep, prev, csum, psum, bsum, out,
    ns_send, ew_send, corner_send, ns_recv, ew_recv, corner_recv, payload, part1, sum1, part2, sum2, part3,
    in_sem, out_sem, spread_ssem, spread_rsem, mir_ssem, mir_rsem, halo_ssem, halo_rsem, red_ssem, red_rsem,
):
    r, c = lax.axis_index("row"), lax.axis_index("col")
    a, b = lax.div(c, 4), lax.rem(c, 4)
    y, zh = lax.div(c, 8), lax.rem(a, 2)
    group_a, group_b = zh * 8 + r, y * 4 + b

    def relay_to(row):
        return {"row": 2 * row + zh, "col": 4 * r + b}

    def relay_from(row):
        return {"row": a, "col": 8 * row + 4 * lax.rem(r, 2) + b}

    def member_a(m):
        return {"row": lax.rem(m, 8), "col": y * 8 + lax.div(m, 8) * 4 + b}

    def member_b(m):
        return {"row": r, "col": lax.div(m, 4) * 8 + zh * 4 + lax.rem(m, 4)}

    def beside(dr, dc):
        return {"row": lax.rem(r + dr + ROWS, ROWS), "col": lax.rem(c + dc + COLS, COLS)}

    own_mirror = a == r
    sides = [(0, 1), (0, -1), (1, 0), (-1, 0), (1, 1), (-1, 1), (1, -1), (-1, -1)]

    barrier = pltpu.get_barrier_semaphore()

    def greet(device):
        pl.semaphore_signal(barrier, inc=1, device_id=device, device_id_type=MESH)

    @pl.when(jnp.logical_not(own_mirror))
    def _():
        greet(relay_to(y))
        greet(relay_from(y))

    for d in range(1, 4):
        greet(relay_to(lax.rem(y + d, 4)))
        greet(relay_from(lax.rem(y + d, 4)))
    for dr, dc in sides:
        greet(beside(dr, dc))

    def greet_groups(d, _):
        greet(member_a(lax.rem(group_a + d, GROUP)))
        greet(member_b(lax.rem(group_b + d, GROUP)))
        return 0

    lax.fori_loop(1, GROUP, greet_groups, 0)

    load_cot = pltpu.make_async_copy(cot_hbm, cot, in_sem.at[0])
    load_feat = pltpu.make_async_copy(feat_hbm, feat, in_sem.at[1])
    load_cot.start()
    load_feat.start()

    load_cot.wait()
    ident = (iota((256, 256), 0) == iota((256, 256), 1)).astype(BF16)

    def turn(g, _):
        block = cot[at(4 * g, 4)].reshape(256, 256)
        turned = dot_nt(ident, block).astype(BF16)
        mir_send[:, :, at(16 * g, 16), :] = turned.reshape(4, 4, 16, 256)
        return 0

    lax.fori_loop(0, 8, turn, 0)

    low = iota((32, 8, 256), 1) < 4

    centre = {0: lambda t: TAPS * t + TILE, 1: lambda t: TILE * t}

    def put(phase, t, tile):
        ref = (act, grad)[phase]
        ref[at(centre[phase](t), TILE), :] = tile.reshape(TILE, 256).astype(BF16)

    def activations():
        load_feat.wait()
        prev[...] = jnp.zeros_like(prev)

        def activate(k, _):
            x = feat[:, at(16 * k, 16), :].astype(F32)
            for h in range(2):
                t = 2 * k + h
                v = x[:, 8 * h : 8 * h + 8, :]
                s = sigmoid(v)
                slope[at(TILE * t, TILE), :] = (s * (1.0 + v * (1.0 - s))).reshape(TILE, 256)
                turned = pltpu.roll(v * s, 4, 1)
                put(0, t, jnp.where(low, prev[...], turned))
                prev[...] = turned
            return 0

        lax.fori_loop(0, 4, activate, 0)
        put(0, TILES, jnp.where(low, prev[...], 0.0))

    def halo_copies(phase):
        diagonal = corner_send.at[phase]
        pairs = [
            (ns_send.at[phase, 1], ns_recv.at[phase, 0]),
            (ns_send.at[phase, 0], ns_recv.at[phase, 1]),
            (ew_send.at[phase, 48:96], ew_recv.at[phase, 48:96]),
            (ew_send.at[phase, 0:48], ew_recv.at[phase, 0:48]),
            (diagonal, corner_recv.at[phase, 0]),
            (diagonal, corner_recv.at[phase, 1]),
            (diagonal, corner_recv.at[phase, 2]),
            (diagonal, corner_recv.at[phase, 3]),
        ]
        return [
            pltpu.make_async_remote_copy(
                src_ref=src,
                dst_ref=dst,
                send_sem=halo_ssem.at[phase, n],
                recv_sem=halo_rsem.at[phase, n],
                device_id=beside(*sides[n]),
                device_id_type=MESH,
            )
            for n, (src, dst) in enumerate(pairs)
        ]

    def halo_pack(phase):
        ref = (act, grad)[phase]
        first, last = centre[phase](0), centre[phase](TILES)
        ns_send[phase, 0] = pack(ref[first : first + TILE, :].astype(F32), False)
        ns_send[phase, 1] = pack(ref[last : last + TILE, :].astype(F32), True)
        row, col = iota((96, 256), 0), iota((96, 256), 1)

        def gather(t, total):
            pick = ((row == 4 * t + col) & (col < 4)) | ((row == 4 * t + col - 204) & (col >= 252))
            return total + dot_nt(one_hot(pick), ref[at(centre[phase](t), TILE), :])

        edge = lax.fori_loop(0, TILES + 1, gather, jnp.zeros((96, 256), F32))
        ew_send[phase] = edge.astype(BF16)
        row, col = iota((8, 256), 0), iota((8, 256), 1)
        pick = one_hot(((row == col) & (row < 4)) | ((row == col - 248) & (row >= 4)))
        corners = [dot_nt(pick, ns_send[phase, n]) for n in range(2)]
        corner_send[phase] = jnp.concatenate(corners, axis=0).astype(BF16)

    up, down, left, right = c > 0, c < COLS - 1, r > 0, r < ROWS - 1

    def only(flag, value):
        return jnp.where(flag, value, 0.0)

    def halo_edge(phase):
        row, lane = iota((96, 128), 0), iota((96, 128), 1)
        straight = ((row == lane) & (row < 48) & right) | ((row == lane - 16) & (lane >= 64) & left)
        edge = dot_tn(ew_recv[phase], one_hot(straight))
        row, lane = iota((16, 128), 0), iota((16, 128), 1)

        def place(n, first, start, flag):
            hit = (row >= first) & (row < first + 4) & (lane == row - first + start) & flag
            return dot_tn(corner_recv[phase, n], one_hot(hit))

        above = place(0, 12, 64, left & up) + place(1, 8, 0, right & up)
        below = place(2, 4, 96, left & down) + place(3, 0, 32, right & down)
        return (edge + unpack(above, True) + unpack(below, False)).astype(BF16)

    def halo_rows(phase):
        above = only(up, unpack(ns_recv[phase, 0], True))
        below = only(down, unpack(ns_recv[phase, 1], False))
        return above, below

    def act_fill():
        above, below = halo_rows(0)
        for t, value in ((0, above), (TILES, below)):
            rows = slice(TAPS * t + TILE, TAPS * t + 2 * TILE)
            act[rows, :] = (act[rows, :].astype(F32) + value).astype(BF16)
        edge = halo_edge(0)
        from_j, to_j = iota((256, 512), 0), iota((256, 512), 1)
        shift = one_hot(((to_j < 256) & (from_j == to_j - 4)) | ((to_j >= 256) & (from_j == to_j - 252)))
        lane, col = iota((128, 512), 0), iota((128, 512), 1)

        def spread(t, _):
            place = ((col < 4) & (lane == 64 + 4 * t + col)) | ((col >= 508) & (lane == 4 * t + col - 508))
            both = dot(act[at(TAPS * t + TILE, TILE), :], shift) + dot(edge, one_hot(place))
            act[at(TAPS * t, TILE), :] = both[:, :256].astype(BF16)
            act[at(TAPS * t + 2 * TILE, TILE), :] = both[:, 256:].astype(BF16)
            return 0

        lax.fori_loop(0, TILES + 1, spread, 0)

    def steps(n):
        dx = lax.rem(n, 4)
        return dx, lax.rem(dx + lax.div(n, 4), 4)

    def spread_copy(n):
        dx, dy = steps(n)
        to_x, to_y = lax.rem(b + dx, 4), lax.rem(y + dy, 4)
        return pltpu.make_async_remote_copy(
            src_ref=mir_send.at[to_x, to_y],
            dst_ref=relay.at[y, b],
            send_sem=spread_ssem.at[n],
            recv_sem=spread_rsem.at[n],
            device_id=member_b(4 * to_y + to_x),
            device_id_type=MESH,
        )

    def relay_copy(n):
        dx, dy = steps(n)
        from_x, from_y = lax.rem(b - dx + 4, 4), lax.rem(y - dy + 4, 4)
        return pltpu.make_async_remote_copy(
            src_ref=relay.at[from_y, from_x],
            dst_ref=mir_recv.at[from_x, y],
            send_sem=mir_ssem.at[n],
            recv_sem=mir_rsem.at[from_x, y],
            device_id=relay_to(from_y),
            device_id_type=MESH,
        )

    def own_copy(n):
        from_x = lax.rem(b - steps(n)[0] + 4, 4)
        return pltpu.make_async_copy(relay.at[y, from_x], mir_recv.at[from_x, y], mir_rsem.at[from_x, y])

    def stays(n):
        return own_mirror & (steps(n)[1] == 0)

    def start_relay(n):
        @pl.when(stays(n))
        def _():
            own_copy(n).start()

        @pl.when(jnp.logical_not(stays(n)))
        def _():
            relay_copy(n).start()

    def arrival(k, n):
        return pltpu.make_async_remote_copy(
            src_ref=relay.at[0, n],
            dst_ref=mir_recv.at[n, k],
            send_sem=mir_ssem.at[n],
            recv_sem=mir_rsem.at[n, k],
            device_id=relay_from(k),
            device_id_type=MESH,
        )

    def own_arrival(n):
        return pltpu.make_async_copy(relay.at[y, n], mir_recv.at[n, y], mir_rsem.at[n, y])

    relay[y, b] = mir_send[b, y]
    pl.semaphore_wait(barrier, 8 + 8 + 2 * (GROUP - 1) - 2 * own_mirror.astype(jnp.int32))

    def send_spread(n, _):
        spread_copy(n).start()
        return 0

    lax.fori_loop(1, GROUP, send_spread, 0)
    start_relay(0)
    activations()
    halo_pack(0)
    for copy in halo_copies(0):
        copy.start()

    spread_out = (lax.div(iota((256, 32), 0), 8) == iota((256, 32), 1)).astype(F32).astype(BF16)
    spread_in = (lax.div(iota((32, 256), 1), 8) == iota((32, 256), 0)).astype(F32).astype(BF16)
    row_out, row_in = lax.rem(iota((256, 256), 0), 8), lax.rem(iota((256, 256), 1), 8)

    def expand(w, turned):
        rows = dot_nt(spread_out, w) if turned else dot(spread_out, w)
        return dot(rows.astype(BF16), spread_in)

    def banded(taps):
        near = jnp.where(row_in == row_out, taps[0], 0.0) + jnp.where(row_in == row_out + 4, taps[1], 0.0)
        far = jnp.where(row_in == row_out, taps[2], 0.0) + jnp.where(row_in == row_out - 4, taps[1], 0.0)
        return near.astype(BF16), far.astype(BF16)

    for tap in range(3):
        near, far = banded([expand(wconv_ref[n, tap], False) for n in range(3)])
        mat_f[:, tap * TILE : (tap + 1) * TILE] = near
        mat_f[:, TAPS + tap * TILE : TAPS + (tap + 1) * TILE] = far
        near, far = banded([expand(wconv_ref[2 - n, 2 - tap], True) for n in range(3)])
        mat_b[tap * TILE : (tap + 1) * TILE, :TILE] = near
        mat_b[tap * TILE : (tap + 1) * TILE, TILE:] = far
    mat_p[...] = jnp.where(row_in == row_out, expand(wpoint_ref[...], True), 0.0).astype(BF16)

    bias_col = jnp.sum(
        jnp.where(lax.div(iota((256, 32), 0), 8) == iota((256, 32), 1), bias_ref[...], 0.0), axis=1, keepdims=True
    )
    mask_row = mask_ref[:, at(256 * a, 256)].astype(F32)
    diagonal = iota((64, 256), 1) == iota((64, 256), 0) + 64 * b
    row_keep = jnp.sum(jnp.where(diagonal, mask_row, 0.0), axis=1, keepdims=True)
    keep[...] = row_keep * (0.5 * mask_ref[:, at(256 * r, 256)].astype(F32))

    csum[...] = jnp.zeros_like(csum)
    psum[...] = jnp.zeros_like(psum)
    bsum[...] = jnp.zeros_like(bsum)

    def pass_on(n, _):
        spread_copy(n).wait_recv()
        start_relay(n)
        return 0

    lax.fori_loop(1, GROUP, pass_on, 0)
    for copy in halo_copies(0):
        copy.wait_recv()
    act_fill()

    def forward(t, _):
        v = dot(mat_f[...], act[pl.ds(pl.multiple_of(TAPS * t, TAPS), 2 * TAPS), :])
        v = v + bias_col
        s = sigmoid(v)
        post[at(TILE * t, TILE), :] = (v * s).astype(BF16)
        pre_slope[at(TILE * t, TILE), :] = s * (1.0 + v * (1.0 - s))
        return 0

    lax.fori_loop(0, TILES, forward, 0)

    prev[...] = jnp.zeros_like(prev)
    left_half = iota((8, 8, 128), 2) < 64

    def chunk(k, _):
        in_place = own_mirror & (k == y)

        @pl.when(in_place)
        def _():
            for n in range(4):
                own_arrival(n).wait()

        @pl.when(jnp.logical_not(in_place))
        def _():
            for n in range(4):
                arrival(k, n).wait_recv()

        here = cot[:, at(16 * k, 16), :].astype(F32)
        keep_rows = keep[at(16 * k, 16), :]
        got = [mir_recv[n, k].astype(F32).reshape(8, 16, 256) for n in range(4)]
        for h in range(2):
            t = 2 * k + h
            part = [v[:, 8 * h : 8 * h + 8, :] for v in got]
            quads = []
            for m in range(4):
                cols = slice(128 * (m // 2), 128 * (m // 2) + 128)
                pieces = []
                for n in (0, 2):
                    one, two = part[n][:, :, cols], part[n + 1][:, :, cols]
                    if m % 2 == 0:
                        pieces.append(jnp.where(left_half, one, pltpu.roll(two, 64, 2)))
                    else:
                        pieces.append(jnp.where(left_half, pltpu.roll(one, 64, 2), two))
                quads.append(jnp.concatenate(pieces, axis=2))
            mirrored = jnp.stack(quads, axis=1).reshape(32, 8, 256)
            residual = keep_rows[8 * h : 8 * h + 8][None] * (here[:, 8 * h : 8 * h + 8, :] + mirrored)
            residual = residual.reshape(TILE, 256)
            half = residual.astype(BF16)
            res[at(TILE * t, TILE), :] = residual
            res_half[at(TILE * t, TILE), :] = half
            g = pre_slope[at(TILE * t, TILE), :] * dot(mat_p[...], half)
            gnat[at(TILE * t, TILE), :] = g.astype(BF16)
            turned = pltpu.roll(g.reshape(32, 8, 256), 4, 1)
            put(1, t, jnp.where(low, prev[...], turned))
            prev[...] = turned

        @pl.when(k == 3)
        def _():
            put(1, TILES, jnp.where(low, prev[...], 0.0))

        total, point, line = csum[...], psum[...], bsum[...]
        for h in range(2):
            t = 2 * k + h
            g = gnat[at(TILE * t, TILE), :]
            total = total + dot_nt(g, act[pl.ds(pl.multiple_of(TAPS * t, TAPS), 2 * TAPS), :])
            point = point + dot_nt(res_half[at(TILE * t, TILE), :], post[at(TILE * t, TILE), :])
            wide = g.astype(F32)
            line = line + wide[:, :128] + wide[:, 128:]
        csum[...] = total
        psum[...] = point
        bsum[...] = line
        return 0

    lax.fori_loop(0, 4, chunk, 0)

    col_in = lax.div(iota((256, 128), 0), 8)
    col_out = iota((256, 128), 1)
    for quad in range(3):
        lanes = jnp.zeros((256, 128), F32)
        for slot in range(4):
            n = 4 * quad + slot
            if n > 9:
                continue
            if n == 9:
                v = jnp.where(row_in == row_out, psum[...], 0.0)
            else:
                row_tap, col_tap = n // 3, n % 3
                near = csum[:, col_tap * TILE : (col_tap + 1) * TILE]
                far = csum[:, TAPS + col_tap * TILE : TAPS + (col_tap + 1) * TILE]
                if row_tap == 0:
                    v = jnp.where(row_in == row_out, near, 0.0)
                elif row_tap == 2:
                    v = jnp.where(row_in == row_out, far, 0.0)
                else:
                    v = jnp.where(row_in == row_out + 4, near, 0.0) + jnp.where(row_in == row_out - 4, far, 0.0)
            pick = (col_out == 32 * slot + col_in).astype(F32).astype(BF16)
            high = v.astype(BF16)
            lanes = lanes + (dot(high, pick) + dot((v - high.astype(F32)).astype(BF16), pick))
        if quad == 2:
            line = jnp.sum(bsum[...], axis=1, keepdims=True)
            lanes = lanes + jnp.where((col_out >= 64) & (col_out < 96), line, 0.0)
        lanes = jnp.sum(lanes.reshape(32, 8, 128), axis=1)
        for o in range(4):
            payload[4 * quad + o] = lanes[8 * o : 8 * o + 8]
    for o in range(4):
        payload[12 + o] = jnp.zeros((8, 128), F32)

    def exchange(stage, me, member, source, dst):
        def copy(d):
            to = lax.rem(me + d, GROUP)
            return pltpu.make_async_remote_copy(
                src_ref=source(to),
                dst_ref=dst.at[me],
                send_sem=red_ssem.at[stage, d],
                recv_sem=red_rsem.at[stage, d],
                device_id=member(to),
                device_id_type=MESH,
            )

        def start(d, _):
            copy(d).start()
            return 0

        def arrive(d, _):
            copy(d).wait_recv()
            return 0

        def leave(d, _):
            copy(d).wait_send()
            return 0

        return (
            lambda: lax.fori_loop(1, GROUP, start, 0),
            lambda: lax.fori_loop(1, GROUP, arrive, 0),
            lambda: lax.fori_loop(1, GROUP, leave, 0),
        )

    start1, arrive1, leave1 = exchange(0, group_a, member_a, lambda m: payload.at[m], part1)
    start2, arrive2, leave2 = exchange(1, group_b, member_b, lambda m: sum1, part2)
    start3, arrive3, leave3 = exchange(2, group_a, member_a, lambda m: sum2, part3)

    def total_of(ref):
        total = ref[0]
        for n in range(1, GROUP):
            total = total + ref[n]
        return total

    part1[group_a] = payload[group_a]
    start1()

    halo_pack(1)
    for copy in halo_copies(1):
        copy.start()

    lane256 = iota((TILE, 256), 1)

    def over_taps(v):
        west = jnp.where(lane256 >= 4, pltpu.roll(v[:TILE], 4, 1), 0.0)
        east = jnp.where(lane256 < 252, pltpu.roll(v[2 * TILE :], 252, 1), 0.0)
        return v[TILE : 2 * TILE] + west + east

    def inner(t, _):
        v = dot(mat_b[...], grad[pl.ds(pl.multiple_of(TILE * t, TILE), 2 * TILE), :])
        pre_slope[at(TILE * t, TILE), :] = over_taps(v)
        return 0

    lax.fori_loop(0, 3, inner, 0)
    arrive1()
    sum1[...] = total_of(part1)
    part2[group_b] = sum1[...]
    start2()
    lax.fori_loop(3, TILES, inner, 0)
    arrive2()
    sum2[...] = total_of(part2)
    part3[group_a] = sum2[...]
    start3()

    for copy in halo_copies(1):
        copy.wait_recv()
    above, below = halo_rows(1)
    pre_slope[:TILE, :] += over_taps(dot(mat_b[:, :TILE], above.astype(BF16)))
    pre_slope[TILE * (TILES - 1) :, :] += over_taps(dot(mat_b[:, TILE:], below.astype(BF16)))
    edge = halo_edge(1)
    from_west = dot(mat_b[:TILE, :TILE], edge) + pltpu.roll(dot(mat_b[:TILE, TILE:], edge), 124, 1)
    from_east = dot(mat_b[2 * TILE :, :TILE], edge) + pltpu.roll(dot(mat_b[2 * TILE :, TILE:], edge), 124, 1)
    lane128 = iota((TILE, 128), 1)
    outer = jnp.where(lane128 < 64, from_east, from_west)

    def store_out(k):
        rows = at(16 * k, 16)
        return pltpu.make_async_copy(out.at[:, rows, :], fg_hbm.at[:, rows, :], out_sem.at[k])

    def backward(k, _):
        halves = []
        for h in range(2):
            t = 2 * k + h
            west = jnp.where(lane128 < 4, pltpu.roll(outer, lax.rem(192 - 4 * t, 128), 1), 0.0)
            east = jnp.where(lane128 >= 124, pltpu.roll(outer, 124 - 4 * t, 1), 0.0)
            v = pre_slope[at(TILE * t, TILE), :] + jnp.concatenate([west, east], axis=1)
            v = res[at(TILE * t, TILE), :] + slope[at(TILE * t, TILE), :] * v
            halves.append(v.reshape(32, 8, 256))
        out[:, at(16 * k, 16), :] = jnp.concatenate(halves, axis=1).astype(BF16)
        store_out(k).start()
        return 0

    lax.fori_loop(0, 4, backward, 0)
    arrive3()

    scale = 1.0 / 2048.0
    for quad in range(3):
        lanes = jnp.concatenate([part3[4 * quad + o] for o in range(4)], axis=0) * scale
        for slot in range(4):
            n = 4 * quad + slot
            block = lanes if slot == 0 else pltpu.roll(lanes, 128 - 32 * slot, 1)
            if n < 9:
                conv_ref[n // 3, n % 3] = block[:, :32]
            elif n == 9:
                point_ref[...] = block[:, :32]
            elif n == 10:
                square = block[:, :32]
                biasg_ref[...] = jnp.sum(
                    jnp.where(iota((32, 32), 0) == iota((32, 32), 1), square, 0.0), axis=0, keepdims=True
                )

    def left(n, _):
        @pl.when(n > 0)
        def _():
            spread_copy(n).wait_send()

        @pl.when(jnp.logical_not(stays(n)))
        def _():
            relay_copy(n).wait_send()

        return 0

    lax.fori_loop(0, GROUP, left, 0)
    for phase in range(2):
        for copy in halo_copies(phase):
            copy.wait_send()
    leave1()
    leave2()
    leave3()
    for k in range(4):
        store_out(k).wait()


def shards(features, cotangent, mask, w_conv, w_point, bias):
    vmem = pl.BlockSpec(memory_space=pltpu.VMEM)
    hbm = pl.BlockSpec(memory_space=pl.ANY)
    big = (TILES * TILE, 256)
    fg, conv, point, bias_grad = pl.pallas_call(
        kernel,
        out_shape=(
            jax.ShapeDtypeStruct((32, 64, 256), BF16),
            jax.ShapeDtypeStruct((3, 3, 32, 32), F32),
            jax.ShapeDtypeStruct((32, 32), F32),
            jax.ShapeDtypeStruct((1, 32), F32),
        ),
        in_specs=[hbm, hbm, vmem, vmem, vmem, vmem],
        out_specs=(hbm, vmem, vmem, vmem),
        scratch_shapes=[
            pltpu.VMEM((32, 64, 256), BF16),
            pltpu.VMEM((32, 64, 256), BF16),
            pltpu.VMEM((4, 4, 128, 256), BF16),
            pltpu.VMEM((4, 4, 128, 256), BF16),
            pltpu.VMEM((4, 4, 128, 256), BF16),
            pltpu.VMEM(((TILES + 1) * TAPS, 256), BF16),
            pltpu.VMEM(((TILES + 1) * TILE, 256), BF16),
            pltpu.VMEM(big, F32),
            pltpu.VMEM(big, BF16),
            pltpu.VMEM(big, F32),
            pltpu.VMEM(big, F32),
            pltpu.VMEM(big, BF16),
            pltpu.VMEM(big, BF16),
            pltpu.VMEM((TILE, 2 * TAPS), BF16),
            pltpu.VMEM((TAPS, 2 * TILE), BF16),
            pltpu.VMEM((TILE, TILE), BF16),
            pltpu.VMEM((64, 256), F32),
            pltpu.VMEM((32, 8, 256), F32),
            pltpu.VMEM((TILE, 2 * TAPS), F32),
            pltpu.VMEM((TILE, TILE), F32),
            pltpu.VMEM((TILE, 128), F32),
            pltpu.VMEM((32, 64, 256), BF16),
            pltpu.VMEM((2, 2, 128, 256), BF16),
            pltpu.VMEM((2, 96, 256), BF16),
            pltpu.VMEM((2, 16, 128), BF16),
            pltpu.VMEM((2, 2, 128, 256), BF16),
            pltpu.VMEM((2, 96, 256), BF16),
            pltpu.VMEM((2, 4, 16, 128), BF16),
            pltpu.VMEM((GROUP, 8, 128), F32),
            pltpu.VMEM((GROUP, 8, 128), F32),
            pltpu.VMEM((8, 128), F32),
            pltpu.VMEM((GROUP, 8, 128), F32),
            pltpu.VMEM((8, 128), F32),
            pltpu.VMEM((GROUP, 8, 128), F32),
            pltpu.SemaphoreType.DMA((2,)),
            pltpu.SemaphoreType.DMA((4,)),
            pltpu.SemaphoreType.DMA((GROUP,)),
            pltpu.SemaphoreType.DMA((GROUP,)),
            pltpu.SemaphoreType.DMA((GROUP,)),
            pltpu.SemaphoreType.DMA((4, 4)),
            pltpu.SemaphoreType.DMA((2, 8)),
            pltpu.SemaphoreType.DMA((2, 8)),
            pltpu.SemaphoreType.DMA((3, GROUP)),
            pltpu.SemaphoreType.DMA((3, GROUP)),
        ],
        compiler_params=pltpu.CompilerParams(
            collective_id=0, has_side_effects=True, vmem_limit_bytes=56 * 1024 * 1024
        ),
        cost_estimate=pl.CostEstimate(flops=5_400_000_000, bytes_accessed=3 * 1024 * 1024, transcendentals=2_000_000),
    )(features, cotangent, mask.reshape(1, 2048), w_conv, w_point, bias.reshape(1, 32))
    return fg, conv, point, bias_grad.reshape(32)


def solution(mesh):
    in_specs = (P(None, "col", "row"), P(None, "col", "row"), P(), P(), P(), P())
    out_specs = (P(None, "col", "row"), P(), P(), P())
    return jax.shard_map(shards, mesh=mesh, in_specs=in_specs, out_specs=out_specs, check_vma=False)
```

```python
import jax
import jax.numpy as jnp
from jax import lax
from jax.experimental import pallas as pl
from jax.experimental.pallas import tpu as pltpu
from jax.sharding import PartitionSpec as P

F32, BF16 = jnp.float32, jnp.bfloat16
MESH = pl.DeviceIdType.MESH
ROWS, COLS = 8, 32
TILE = 256
TAPS = 3 * TILE
TILES = 8
GROUP = 16
SLICES = ((0, 3), (3, 1))
NT = (((1,), (1,)), ((), ()))
TN = (((0,), (0,)), ((), ()))


def iota(shape, dim):
    return lax.broadcasted_iota(jnp.int32, shape, dim)


def dot(x, y):
    return jnp.dot(x, y, preferred_element_type=F32)


def dot_nt(x, y):
    return lax.dot_general(x, y, NT, preferred_element_type=F32)


def dot_tn(x, y):
    return lax.dot_general(x, y, TN, preferred_element_type=F32)


def one_hot(where):
    return where.astype(F32).astype(BF16)


def at(start, size):
    return pl.ds(pl.multiple_of(start, size), size)


def sigmoid(v):
    return 1.0 / (1.0 + jnp.exp(-v))


def pack(tile, bottom):
    v = tile.reshape(16, 2, 8, 256)
    low = iota((16, 8, 256), 1) < 4
    if bottom:
        v = jnp.where(low, v[:, 0], pltpu.roll(v[:, 1], 4, 1))
    else:
        v = jnp.where(low, pltpu.roll(v[:, 0], 4, 1), v[:, 1])
    return v.reshape(128, 256).astype(BF16)


def unpack(packed, bottom):
    width = packed.shape[1]
    v = packed.astype(F32).reshape(16, 8, width)
    turned = pltpu.roll(v, 4, 1)
    low = iota((16, 8, width), 1) < 4
    if bottom:
        pair = [jnp.where(low, v, 0.0), jnp.where(low, turned, 0.0)]
    else:
        pair = [jnp.where(low, 0.0, turned), jnp.where(low, 0.0, v)]
    return jnp.stack(pair, axis=1).reshape(TILE, width)


def kernel(
    feat_hbm, cot_hbm, mask_hbm, wconv_hbm, wpoint_hbm, bias_hbm,
    fg_hbm, sums_hbm,
    mask_ref, wconv_ref, wpoint_ref, bias_ref,
    feat, cot, mir_send, relay, mir_recv, act, grad, res, res_half, slope, pre_slope, post, gnat,
    mat_f, mat_b, mat_p, keep, prev, csum, psum, bsum, out,
    ns_send, ew_send, corner_send, ns_recv, ew_recv, corner_recv, payload, part1, sum1, part2, sum2, part3,
    in_sem, out_sem, spread_ssem, spread_rsem, mir_ssem, mir_rsem, halo_ssem, halo_rsem, red_ssem, red_rsem,
):
    r, c = lax.axis_index("row"), lax.axis_index("col")
    a, b = lax.div(c, 4), lax.rem(c, 4)
    y, zh = lax.div(c, 8), lax.rem(a, 2)
    group_a, group_b = zh * 8 + r, y * 4 + b

    def mirror_to(x, row):
        return {"row": 2 * row + zh, "col": 4 * r + x}

    def mirror_from(x, row):
        return {"row": a, "col": 8 * row + 4 * lax.rem(r, 2) + x}

    def member_a(m):
        return {"row": lax.rem(m, 8), "col": y * 8 + lax.div(m, 8) * 4 + b}

    def member_b(m):
        return {"row": r, "col": lax.div(m, 4) * 8 + zh * 4 + lax.rem(m, 4)}

    def beside(dr, dc):
        return {"row": lax.rem(r + dr + ROWS, ROWS), "col": lax.rem(c + dc + COLS, COLS)}

    own_mirror = a == r
    sides = [(0, 1), (0, -1), (1, 0), (-1, 0), (1, 1), (-1, 1), (1, -1), (-1, -1)]

    barrier = pltpu.get_barrier_semaphore()

    def greet(device):
        pl.semaphore_signal(barrier, inc=1, device_id=device, device_id_type=MESH)

    @pl.when(jnp.logical_not(own_mirror))
    def _():
        greet(mirror_to(b, y))
        greet(mirror_from(b, y))

    def greet_mirrors(n, _):
        x, row = lax.rem(b + lax.div(n, 4), 4), lax.rem(y + n, 4)
        greet(mirror_to(x, row))
        greet(mirror_from(x, row))
        return 0

    lax.fori_loop(1, GROUP, greet_mirrors, 0)
    for dr, dc in sides:
        greet(beside(dr, dc))

    def greet_groups(d, _):
        greet(member_a(lax.rem(group_a + d, GROUP)))
        greet(member_b(lax.rem(group_b + d, GROUP)))
        return 0

    lax.fori_loop(1, GROUP, greet_groups, 0)

    load_cot = pltpu.make_async_copy(cot_hbm, cot, in_sem.at[0])
    load_feat = pltpu.make_async_copy(feat_hbm, feat, in_sem.at[1])
    loads = [
        pltpu.make_async_copy(source, target, in_sem.at[2 + n])
        for n, (source, target) in enumerate(
            [(mask_hbm, mask_ref), (wconv_hbm, wconv_ref), (wpoint_hbm, wpoint_ref), (bias_hbm, bias_ref)]
        )
    ]
    load_cot.start()
    load_feat.start()
    for copy in loads:
        copy.start()

    load_cot.wait()
    ident = (iota((256, 256), 0) == iota((256, 256), 1)).astype(BF16)

    def turn(g, _):
        block = cot[at(4 * g, 4)].reshape(256, 256)
        turned = dot_nt(ident, block).astype(BF16)
        mir_send[:, :, at(16 * g, 16), :] = turned.reshape(4, 4, 16, 256)
        return 0

    lax.fori_loop(0, 8, turn, 0)

    low = iota((32, 8, 256), 1) < 4

    centre = {0: lambda t: TAPS * t + TILE, 1: lambda t: TILE * t}

    def put(phase, t, tile):
        ref = (act, grad)[phase]
        ref[at(centre[phase](t), TILE), :] = tile.reshape(TILE, 256).astype(BF16)

    def activations():
        load_feat.wait()
        prev[...] = jnp.zeros_like(prev)

        def activate(k, _):
            x = feat[:, at(16 * k, 16), :].astype(F32)
            for h in range(2):
                t = 2 * k + h
                v = x[:, 8 * h : 8 * h + 8, :]
                s = sigmoid(v)
                slope[at(TILE * t, TILE), :] = (s * (1.0 + v * (1.0 - s))).reshape(TILE, 256)
                turned = pltpu.roll(v * s, 4, 1)
                put(0, t, jnp.where(low, prev[...], turned))
                prev[...] = turned
            return 0

        lax.fori_loop(0, 4, activate, 0)
        put(0, TILES, jnp.where(low, prev[...], 0.0))

    def halo_copies(phase):
        diagonal = corner_send.at[phase]
        pairs = [
            (ns_send.at[phase, 1], ns_recv.at[phase, 0]),
            (ns_send.at[phase, 0], ns_recv.at[phase, 1]),
            (ew_send.at[phase, 48:96], ew_recv.at[phase, 48:96]),
            (ew_send.at[phase, 0:48], ew_recv.at[phase, 0:48]),
            (diagonal, corner_recv.at[phase, 0]),
            (diagonal, corner_recv.at[phase, 1]),
            (diagonal, corner_recv.at[phase, 2]),
            (diagonal, corner_recv.at[phase, 3]),
        ]
        return [
            pltpu.make_async_remote_copy(
                src_ref=src,
                dst_ref=dst,
                send_sem=halo_ssem.at[phase, n],
                recv_sem=halo_rsem.at[phase, n],
                device_id=beside(*sides[n]),
                device_id_type=MESH,
            )
            for n, (src, dst) in enumerate(pairs)
        ]

    def halo_pack(phase):
        ref = (act, grad)[phase]
        first, last = centre[phase](0), centre[phase](TILES)
        ns_send[phase, 0] = pack(ref[first : first + TILE, :].astype(F32), False)
        ns_send[phase, 1] = pack(ref[last : last + TILE, :].astype(F32), True)
        row, col = iota((96, 256), 0), iota((96, 256), 1)

        def gather(t, total):
            pick = ((row == 4 * t + col) & (col < 4)) | ((row == 4 * t + col - 204) & (col >= 252))
            return total + dot_nt(one_hot(pick), ref[at(centre[phase](t), TILE), :])

        edge = lax.fori_loop(0, TILES + 1, gather, jnp.zeros((96, 256), F32))
        ew_send[phase] = edge.astype(BF16)
        row, col = iota((8, 256), 0), iota((8, 256), 1)
        pick = one_hot(((row == col) & (row < 4)) | ((row == col - 248) & (row >= 4)))
        corners = [dot_nt(pick, ns_send[phase, n]) for n in range(2)]
        corner_send[phase] = jnp.concatenate(corners, axis=0).astype(BF16)

    up, down, left, right = c > 0, c < COLS - 1, r > 0, r < ROWS - 1

    def only(flag, value):
        return jnp.where(flag, value, 0.0)

    def halo_edge(phase):
        row, lane = iota((96, 128), 0), iota((96, 128), 1)
        straight = ((row == lane) & (row < 48) & right) | ((row == lane - 16) & (lane >= 64) & left)
        edge = dot_tn(ew_recv[phase], one_hot(straight))
        row, lane = iota((16, 128), 0), iota((16, 128), 1)

        def place(n, first, start, flag):
            hit = (row >= first) & (row < first + 4) & (lane == row - first + start) & flag
            return dot_tn(corner_recv[phase, n], one_hot(hit))

        above = place(0, 12, 64, left & up) + place(1, 8, 0, right & up)
        below = place(2, 4, 96, left & down) + place(3, 0, 32, right & down)
        return (edge + unpack(above, True) + unpack(below, False)).astype(BF16)

    def halo_rows(phase):
        above = only(up, unpack(ns_recv[phase, 0], True))
        below = only(down, unpack(ns_recv[phase, 1], False))
        return above, below

    def act_fill():
        above, below = halo_rows(0)
        for t, value in ((0, above), (TILES, below)):
            rows = slice(TAPS * t + TILE, TAPS * t + 2 * TILE)
            act[rows, :] = (act[rows, :].astype(F32) + value).astype(BF16)
        edge = halo_edge(0)
        from_j, to_j = iota((256, 512), 0), iota((256, 512), 1)
        shift = one_hot(((to_j < 256) & (from_j == to_j - 4)) | ((to_j >= 256) & (from_j == to_j - 252)))
        lane, col = iota((128, 512), 0), iota((128, 512), 1)

        def spread(t, _):
            place = ((col < 4) & (lane == 64 + 4 * t + col)) | ((col >= 508) & (lane == 4 * t + col - 508))
            both = dot(act[at(TAPS * t + TILE, TILE), :], shift) + dot(edge, one_hot(place))
            act[at(TAPS * t, TILE), :] = both[:, :256].astype(BF16)
            act[at(TAPS * t + 2 * TILE, TILE), :] = both[:, 256:].astype(BF16)
            return 0

        lax.fori_loop(0, TILES + 1, spread, 0)

    def rows_of(part):
        return pl.ds(*SLICES[part])

    def spread_copy(part, n):
        dx, dy = lax.div(n, 4), lax.rem(n, 4)
        to_x, to_y = lax.rem(b + dx, 4), lax.rem(y + dy, 4)
        return pltpu.make_async_remote_copy(
            src_ref=mir_send.at[to_x, rows_of(part), at(32 * to_y, 32), :],
            dst_ref=relay.at[y, to_x, rows_of(part)],
            send_sem=spread_ssem.at[part, n],
            recv_sem=spread_rsem.at[part, n],
            device_id=member_b(4 * to_y + b),
            device_id_type=MESH,
        )

    def relay_copy(part, n):
        dx, dy = lax.div(n, 4), lax.rem(n, 4)
        to_x, from_y = lax.rem(b + dx, 4), lax.rem(y - dy + 4, 4)
        return pltpu.make_async_remote_copy(
            src_ref=relay.at[from_y, to_x, rows_of(part)],
            dst_ref=mir_recv.at[b, rows_of(part), at(32 * y, 32), :],
            send_sem=mir_ssem.at[part, n],
            recv_sem=mir_rsem.at[part, 4 * y + b],
            device_id=mirror_to(to_x, from_y),
            device_id_type=MESH,
        )

    def own_copy(part):
        return pltpu.make_async_copy(
            relay.at[y, b, rows_of(part)],
            mir_recv.at[b, rows_of(part), at(32 * y, 32), :],
            mir_rsem.at[part, 4 * y + b],
        )

    def arrival(part, n):
        from_y, from_x = lax.div(n, 4), lax.rem(n, 4)
        return pltpu.make_async_remote_copy(
            src_ref=relay.at[from_y, from_x, rows_of(part)],
            dst_ref=mir_recv.at[from_x, rows_of(part), at(32 * from_y, 32), :],
            send_sem=mir_ssem.at[part, n],
            recv_sem=mir_rsem.at[part, n],
            device_id=mirror_from(from_x, from_y),
            device_id_type=MESH,
        )

    for x in range(4):
        relay[y, x] = mir_send[x, :, at(32 * y, 32), :]
    pl.semaphore_wait(barrier, 2 * GROUP + 8 + 2 * (GROUP - 1) - 2 * own_mirror.astype(jnp.int32))

    def relayed(n):
        return lax.rem(n, 4) > 0

    def each(part, step, count=GROUP):
        lax.fori_loop(0, count, lambda n, _: step(part, n), 0)

    def send_spread(part, n):
        @pl.when(relayed(n))
        def _():
            spread_copy(part, n).start()

        return 0

    def start_own(part, m):
        stays = own_mirror & (m == 0)

        @pl.when(stays)
        def _():
            own_copy(part).start()

        @pl.when(jnp.logical_not(stays))
        def _():
            relay_copy(part, 4 * m).start()

        return 0

    def pass_on(part, n):
        @pl.when(relayed(n))
        def _():
            spread_copy(part, n).wait_recv()
            relay_copy(part, n).start()

        return 0

    def sent(part, n):
        @pl.when(relayed(n))
        def _():
            spread_copy(part, n).wait_send()

        @pl.when(jnp.logical_not(own_mirror & (n == 0)))
        def _():
            relay_copy(part, n).wait_send()

        return 0

    for part in range(len(SLICES)):
        each(part, send_spread)
    for part in range(len(SLICES)):
        each(part, start_own, 4)
    activations()
    halo_pack(0)
    for copy in halo_copies(0):
        copy.start()

    each(0, pass_on)

    for copy in loads:
        copy.wait()

    spread_out = (lax.div(iota((256, 32), 0), 8) == iota((256, 32), 1)).astype(F32).astype(BF16)
    spread_in = (lax.div(iota((32, 256), 1), 8) == iota((32, 256), 0)).astype(F32).astype(BF16)
    row_out, row_in = lax.rem(iota((256, 256), 0), 8), lax.rem(iota((256, 256), 1), 8)

    def expand(w, turned):
        rows = dot_nt(spread_out, w) if turned else dot(spread_out, w)
        return dot(rows.astype(BF16), spread_in)

    def banded(taps):
        near = jnp.where(row_in == row_out, taps[0], 0.0) + jnp.where(row_in == row_out + 4, taps[1], 0.0)
        far = jnp.where(row_in == row_out, taps[2], 0.0) + jnp.where(row_in == row_out - 4, taps[1], 0.0)
        return near.astype(BF16), far.astype(BF16)

    for tap in range(3):
        near, far = banded([expand(wconv_ref[n, tap], False) for n in range(3)])
        mat_f[:, tap * TILE : (tap + 1) * TILE] = near
        mat_f[:, TAPS + tap * TILE : TAPS + (tap + 1) * TILE] = far
        near, far = banded([expand(wconv_ref[2 - n, 2 - tap], True) for n in range(3)])
        mat_b[tap * TILE : (tap + 1) * TILE, :TILE] = near
        mat_b[tap * TILE : (tap + 1) * TILE, TILE:] = far
    mat_p[...] = jnp.where(row_in == row_out, expand(wpoint_ref[...], True), 0.0).astype(BF16)

    bias_col = jnp.sum(
        jnp.where(lax.div(iota((256, 32), 0), 8) == iota((256, 32), 1), bias_ref[...], 0.0), axis=1, keepdims=True
    )
    mask_row = mask_ref[:, at(256 * a, 256)].astype(F32)
    diagonal = iota((64, 256), 1) == iota((64, 256), 0) + 64 * b
    row_keep = jnp.sum(jnp.where(diagonal, mask_row, 0.0), axis=1, keepdims=True)
    keep[...] = row_keep * (0.5 * mask_ref[:, at(256 * r, 256)].astype(F32))

    csum[...] = jnp.zeros_like(csum)
    psum[...] = jnp.zeros_like(psum)
    bsum[...] = jnp.zeros_like(bsum)

    each(1, pass_on)
    for copy in halo_copies(0):
        copy.wait_recv()
    act_fill()

    def forward(t, _):
        v = dot(mat_f[...], act[pl.ds(pl.multiple_of(TAPS * t, TAPS), 2 * TAPS), :])
        v = v + bias_col
        s = sigmoid(v)
        post[at(TILE * t, TILE), :] = (v * s).astype(BF16)
        pre_slope[at(TILE * t, TILE), :] = s * (1.0 + v * (1.0 - s))
        return 0

    lax.fori_loop(0, TILES, forward, 0)

    prev[...] = jnp.zeros_like(prev)
    left_half = iota((8, 8, 128), 2) < 64

    def arrive(part, n):
        stays = own_mirror & (n == 4 * y + b)

        @pl.when(stays)
        def _():
            own_copy(part).wait()

        @pl.when(jnp.logical_not(stays))
        def _():
            arrival(part, n).wait_recv()

        return 0

    def chunk(k, _):
        for part, (first, _) in enumerate(SLICES):

            @pl.when(k == first)
            def _():
                each(part, arrive)

        here = cot[:, at(16 * k, 16), :].astype(F32)
        keep_rows = keep[at(16 * k, 16), :]
        got = [mir_recv[n, k].astype(F32).reshape(8, 16, 256) for n in range(4)]
        for h in range(2):
            t = 2 * k + h
            part = [v[:, 8 * h : 8 * h + 8, :] for v in got]
            quads = []
            for m in range(4):
                cols = slice(128 * (m // 2), 128 * (m // 2) + 128)
                pieces = []
                for n in (0, 2):
                    one, two = part[n][:, :, cols], part[n + 1][:, :, cols]
                    if m % 2 == 0:
                        pieces.append(jnp.where(left_half, one, pltpu.roll(two, 64, 2)))
                    else:
                        pieces.append(jnp.where(left_half, pltpu.roll(one, 64, 2), two))
                quads.append(jnp.concatenate(pieces, axis=2))
            mirrored = jnp.stack(quads, axis=1).reshape(32, 8, 256)
            residual = keep_rows[8 * h : 8 * h + 8][None] * (here[:, 8 * h : 8 * h + 8, :] + mirrored)
            residual = residual.reshape(TILE, 256)
            half = residual.astype(BF16)
            res[at(TILE * t, TILE), :] = residual
            res_half[at(TILE * t, TILE), :] = half
            g = pre_slope[at(TILE * t, TILE), :] * dot(mat_p[...], half)
            gnat[at(TILE * t, TILE), :] = g.astype(BF16)
            turned = pltpu.roll(g.reshape(32, 8, 256), 4, 1)
            put(1, t, jnp.where(low, prev[...], turned))
            prev[...] = turned

        @pl.when(k == 3)
        def _():
            put(1, TILES, jnp.where(low, prev[...], 0.0))

        total, point, line = csum[...], psum[...], bsum[...]
        for h in range(2):
            t = 2 * k + h
            g = gnat[at(TILE * t, TILE), :]
            total = total + dot_nt(g, act[pl.ds(pl.multiple_of(TAPS * t, TAPS), 2 * TAPS), :])
            point = point + dot_nt(res_half[at(TILE * t, TILE), :], post[at(TILE * t, TILE), :])
            wide = g.astype(F32)
            line = line + wide[:, :128] + wide[:, 128:]
        csum[...] = total
        psum[...] = point
        bsum[...] = line
        return 0

    lax.fori_loop(0, 4, chunk, 0)

    def exchange(stage, me, member, source, dst):
        def copy(d):
            to = lax.rem(me + d, GROUP)
            return pltpu.make_async_remote_copy(
                src_ref=source(to),
                dst_ref=dst.at[me],
                send_sem=red_ssem.at[stage, d],
                recv_sem=red_rsem.at[stage, d],
                device_id=member(to),
                device_id_type=MESH,
            )

        def start(d, _):
            copy(d).start()
            return 0

        def arrive(d, _):
            copy(d).wait_recv()
            return 0

        def leave(d, _):
            copy(d).wait_send()
            return 0

        if stage == 0:
            return (
                lambda m: copy(lax.rem(m - me + GROUP, GROUP)),
                lambda: lax.fori_loop(1, GROUP, arrive, 0),
                lambda: lax.fori_loop(1, GROUP, leave, 0),
            )
        return (
            lambda: lax.fori_loop(1, GROUP, start, 0),
            lambda: lax.fori_loop(1, GROUP, arrive, 0),
            lambda: lax.fori_loop(1, GROUP, leave, 0),
        )

    first_copy, arrive1, leave1 = exchange(0, group_a, member_a, lambda m: payload.at[m], part1)
    start2, arrive2, leave2 = exchange(1, group_b, member_b, lambda m: sum1, part2)
    start3, arrive3, leave3 = exchange(2, group_a, member_a, lambda m: sum2, part3)

    def send_payload(m):
        @pl.when(group_a == m)
        def _():
            part1[m] = payload[m]

        @pl.when(group_a != m)
        def _():
            first_copy(m).start()

    col_in = lax.div(iota((256, 128), 0), 8)
    col_out = iota((256, 128), 1)
    for quad in range(3):
        lanes = jnp.zeros((256, 128), F32)
        for slot in range(4):
            n = 4 * quad + slot
            if n > 9:
                continue
            if n == 9:
                v = jnp.where(row_in == row_out, psum[...], 0.0)
            else:
                row_tap, col_tap = n // 3, n % 3
                near = csum[:, col_tap * TILE : (col_tap + 1) * TILE]
                far = csum[:, TAPS + col_tap * TILE : TAPS + (col_tap + 1) * TILE]
                if row_tap == 0:
                    v = jnp.where(row_in == row_out, near, 0.0)
                elif row_tap == 2:
                    v = jnp.where(row_in == row_out, far, 0.0)
                else:
                    v = jnp.where(row_in == row_out + 4, near, 0.0) + jnp.where(row_in == row_out - 4, far, 0.0)
            pick = (col_out == 32 * slot + col_in).astype(F32).astype(BF16)
            high = v.astype(BF16)
            lanes = lanes + (dot(high, pick) + dot((v - high.astype(F32)).astype(BF16), pick))
        if quad == 2:
            line = jnp.sum(bsum[...], axis=1, keepdims=True)
            lanes = lanes + jnp.where((col_out >= 64) & (col_out < 96), line, 0.0)
        lanes = jnp.sum(lanes.reshape(32, 8, 128), axis=1)
        for o in range(4):
            payload[4 * quad + o] = lanes[8 * o : 8 * o + 8]
            send_payload(4 * quad + o)
    for o in range(12, GROUP):
        payload[o] = jnp.zeros((8, 128), F32)
        send_payload(o)

    def total_of(ref):
        total = ref[0]
        for n in range(1, GROUP):
            total = total + ref[n]
        return total

    halo_pack(1)
    for copy in halo_copies(1):
        copy.start()

    lane256 = iota((TILE, 256), 1)

    def over_taps(v):
        west = jnp.where(lane256 >= 4, pltpu.roll(v[:TILE], 4, 1), 0.0)
        east = jnp.where(lane256 < 252, pltpu.roll(v[2 * TILE :], 252, 1), 0.0)
        return v[TILE : 2 * TILE] + west + east

    def inner(t, _):
        v = dot(mat_b[...], grad[pl.ds(pl.multiple_of(TILE * t, TILE), 2 * TILE), :])
        pre_slope[at(TILE * t, TILE), :] = over_taps(v)
        return 0

    lax.fori_loop(0, 3, inner, 0)
    for part in range(len(SLICES)):
        each(part, sent)
    for copy in halo_copies(0):
        copy.wait_send()
    arrive1()
    sum1[...] = total_of(part1)
    part2[group_b] = sum1[...]
    start2()
    lax.fori_loop(3, TILES, inner, 0)
    leave1()
    arrive2()
    sum2[...] = total_of(part2)
    part3[group_a] = sum2[...]
    start3()

    leave2()
    for copy in halo_copies(1):
        copy.wait()
    above, below = halo_rows(1)
    pre_slope[:TILE, :] += over_taps(dot(mat_b[:, :TILE], above.astype(BF16)))
    pre_slope[TILE * (TILES - 1) :, :] += over_taps(dot(mat_b[:, TILE:], below.astype(BF16)))
    edge = halo_edge(1)
    from_west = dot(mat_b[:TILE, :TILE], edge) + pltpu.roll(dot(mat_b[:TILE, TILE:], edge), 124, 1)
    from_east = dot(mat_b[2 * TILE :, :TILE], edge) + pltpu.roll(dot(mat_b[2 * TILE :, TILE:], edge), 124, 1)
    lane128 = iota((TILE, 128), 1)
    outer = jnp.where(lane128 < 64, from_east, from_west)

    def store_out(k):
        rows = at(16 * k, 16)
        return pltpu.make_async_copy(out.at[:, rows, :], fg_hbm.at[:, rows, :], out_sem.at[k])

    def backward(k, _):
        halves = []
        for h in range(2):
            t = 2 * k + h
            west = jnp.where(lane128 < 4, pltpu.roll(outer, lax.rem(192 - 4 * t, 128), 1), 0.0)
            east = jnp.where(lane128 >= 124, pltpu.roll(outer, 124 - 4 * t, 1), 0.0)
            v = pre_slope[at(TILE * t, TILE), :] + jnp.concatenate([west, east], axis=1)
            v = res[at(TILE * t, TILE), :] + slope[at(TILE * t, TILE), :] * v
            halves.append(v.reshape(32, 8, 256))
        out[:, at(16 * k, 16), :] = jnp.concatenate(halves, axis=1).astype(BF16)
        store_out(k).start()
        return 0

    lax.fori_loop(0, 4, backward, 0)
    arrive3()

    store_sums = pltpu.make_async_copy(part3.at[0:12], sums_hbm, out_sem.at[4])
    store_sums.start()

    leave3()
    for k in range(4):
        store_out(k).wait()
    store_sums.wait()


def finish(
    fg_hbm, sums_hbm, out_hbm, conv_hbm, point_hbm, biasg_hbm, held, sums_ref, conv_ref, point_ref, biasg_ref, sem
):
    parts = [slice(8 * n, 8 * n + 8) for n in range(4)]
    loads = [pltpu.make_async_copy(fg_hbm.at[p], held.at[p], sem.at[0, n]) for n, p in enumerate(parts)]
    stores = [pltpu.make_async_copy(held.at[p], out_hbm.at[p], sem.at[1, n]) for n, p in enumerate(parts)]
    load_sums = pltpu.make_async_copy(sums_hbm, sums_ref, sem.at[2, 0])
    load_sums.start()
    for copy in loads:
        copy.start()
    for load, store in zip(loads, stores):
        load.wait()
        store.start()
    load_sums.wait()
    scale = 1.0 / 2048.0
    for quad in range(3):
        lanes = jnp.concatenate([sums_ref[4 * quad + o] for o in range(4)], axis=0) * scale
        for slot in range(4):
            n = 4 * quad + slot
            block = lanes if slot == 0 else pltpu.roll(lanes, 128 - 32 * slot, 1)
            if n < 9:
                conv_ref[n // 3, n % 3] = block[:, :32]
            elif n == 9:
                point_ref[...] = block[:, :32]
            elif n == 10:
                square = block[:, :32]
                biasg_ref[...] = jnp.sum(
                    jnp.where(iota((32, 32), 0) == iota((32, 32), 1), square, 0.0), axis=0, keepdims=True
                )
    small = [
        pltpu.make_async_copy(source, target, sem.at[2, 1 + n])
        for n, (source, target) in enumerate([(conv_ref, conv_hbm), (point_ref, point_hbm), (biasg_ref, biasg_hbm)])
    ]
    for copy in small:
        copy.start()
    for copy in stores + small:
        copy.wait()


def shards(features, cotangent, mask, w_conv, w_point, bias):
    hbm = pl.BlockSpec(memory_space=pl.ANY)
    big = (TILES * TILE, 256)
    fg, sums = pl.pallas_call(
        kernel,
        out_shape=(
            jax.ShapeDtypeStruct((32, 64, 256), BF16),
            jax.ShapeDtypeStruct((12, 8, 128), F32),
        ),
        in_specs=[hbm] * 6,
        out_specs=(hbm, hbm),
        scratch_shapes=[
            pltpu.VMEM((1, 2048), jnp.int32),
            pltpu.VMEM((3, 3, 32, 32), BF16),
            pltpu.VMEM((32, 32), BF16),
            pltpu.VMEM((1, 32), F32),
            pltpu.VMEM((32, 64, 256), BF16),
            pltpu.VMEM((32, 64, 256), BF16),
            pltpu.VMEM((4, 4, 128, 256), BF16),
            pltpu.VMEM((4, 4, 4, 32, 256), BF16),
            pltpu.VMEM((4, 4, 128, 256), BF16),
            pltpu.VMEM(((TILES + 1) * TAPS, 256), BF16),
            pltpu.VMEM(((TILES + 1) * TILE, 256), BF16),
            pltpu.VMEM(big, F32),
            pltpu.VMEM(big, BF16),
            pltpu.VMEM(big, F32),
            pltpu.VMEM(big, F32),
            pltpu.VMEM(big, BF16),
            pltpu.VMEM(big, BF16),
            pltpu.VMEM((TILE, 2 * TAPS), BF16),
            pltpu.VMEM((TAPS, 2 * TILE), BF16),
            pltpu.VMEM((TILE, TILE), BF16),
            pltpu.VMEM((64, 256), F32),
            pltpu.VMEM((32, 8, 256), F32),
            pltpu.VMEM((TILE, 2 * TAPS), F32),
            pltpu.VMEM((TILE, TILE), F32),
            pltpu.VMEM((TILE, 128), F32),
            pltpu.VMEM((32, 64, 256), BF16),
            pltpu.VMEM((2, 2, 128, 256), BF16),
            pltpu.VMEM((2, 96, 256), BF16),
            pltpu.VMEM((2, 16, 128), BF16),
            pltpu.VMEM((2, 2, 128, 256), BF16),
            pltpu.VMEM((2, 96, 256), BF16),
            pltpu.VMEM((2, 4, 16, 128), BF16),
            pltpu.VMEM((GROUP, 8, 128), F32),
            pltpu.VMEM((GROUP, 8, 128), F32),
            pltpu.VMEM((8, 128), F32),
            pltpu.VMEM((GROUP, 8, 128), F32),
            pltpu.VMEM((8, 128), F32),
            pltpu.VMEM((GROUP, 8, 128), F32),
            pltpu.SemaphoreType.DMA((6,)),
            pltpu.SemaphoreType.DMA((5,)),
            pltpu.SemaphoreType.DMA((len(SLICES), GROUP)),
            pltpu.SemaphoreType.DMA((len(SLICES), GROUP)),
            pltpu.SemaphoreType.DMA((len(SLICES), GROUP)),
            pltpu.SemaphoreType.DMA((len(SLICES), GROUP)),
            pltpu.SemaphoreType.DMA((2, 8)),
            pltpu.SemaphoreType.DMA((2, 8)),
            pltpu.SemaphoreType.DMA((3, GROUP)),
            pltpu.SemaphoreType.DMA((3, GROUP)),
        ],
        compiler_params=pltpu.CompilerParams(
            collective_id=0, has_side_effects=True, vmem_limit_bytes=56 * 1024 * 1024
        ),
        cost_estimate=pl.CostEstimate(flops=5_400_000_000, bytes_accessed=3 * 1024 * 1024, transcendentals=2_000_000),
    )(features, cotangent, mask.reshape(1, 2048), w_conv, w_point, bias.reshape(1, 32))
    fg, conv, point, bias_grad = pl.pallas_call(
        finish,
        out_shape=(
            jax.ShapeDtypeStruct((32, 64, 256), BF16),
            jax.ShapeDtypeStruct((3, 3, 32, 32), F32),
            jax.ShapeDtypeStruct((32, 32), F32),
            jax.ShapeDtypeStruct((1, 32), F32),
        ),
        in_specs=[hbm, hbm],
        out_specs=(hbm, hbm, hbm, hbm),
        scratch_shapes=[
            pltpu.VMEM((32, 64, 256), BF16),
            pltpu.VMEM((12, 8, 128), F32),
            pltpu.VMEM((3, 3, 32, 32), F32),
            pltpu.VMEM((32, 32), F32),
            pltpu.VMEM((1, 32), F32),
            pltpu.SemaphoreType.DMA((3, 4)),
        ],
    )(fg, sums)
    return fg, conv, point, bias_grad.reshape(32)


def solution(mesh):
    in_specs = (P(None, "col", "row"), P(None, "col", "row"), P(), P(), P(), P())
    out_specs = (P(None, "col", "row"), P(), P(), P())
    return jax.shard_map(shards, mesh=mesh, in_specs=in_specs, out_specs=out_specs, check_vma=False)
```

```python
import jax
import jax.numpy as jnp
from jax import lax
from jax.experimental import pallas as pl
from jax.experimental.pallas import tpu as pltpu
from jax.sharding import PartitionSpec as P

F32, BF16 = jnp.float32, jnp.bfloat16
MESH = pl.DeviceIdType.MESH
ROWS, COLS = 8, 32
TILE = 256
TAPS = 3 * TILE
TILES = 8
GROUP = 16
FIRST, SECOND = 2, 5
SLICES = ((0, 3), (3, 1))
NT = (((1,), (1,)), ((), ()))
TN = (((0,), (0,)), ((), ()))


def iota(shape, dim):
    return lax.broadcasted_iota(jnp.int32, shape, dim)


def dot(x, y):
    return jnp.dot(x, y, preferred_element_type=F32)


def dot_nt(x, y):
    return lax.dot_general(x, y, NT, preferred_element_type=F32)


def dot_tn(x, y):
    return lax.dot_general(x, y, TN, preferred_element_type=F32)


def one_hot(where):
    return where.astype(F32).astype(BF16)


def at(start, size):
    return pl.ds(pl.multiple_of(start, size), size)


def sigmoid(v):
    return 1.0 / (1.0 + jnp.exp(-v))


def pack(tile, bottom):
    v = tile.reshape(16, 2, 8, 256)
    low = iota((16, 8, 256), 1) < 4
    if bottom:
        v = jnp.where(low, v[:, 0], pltpu.roll(v[:, 1], 4, 1))
    else:
        v = jnp.where(low, pltpu.roll(v[:, 0], 4, 1), v[:, 1])
    return v.reshape(128, 256).astype(BF16)


def unpack(packed, bottom):
    width = packed.shape[1]
    v = packed.astype(F32).reshape(16, 8, width)
    turned = pltpu.roll(v, 4, 1)
    low = iota((16, 8, width), 1) < 4
    if bottom:
        pair = [jnp.where(low, v, 0.0), jnp.where(low, turned, 0.0)]
    else:
        pair = [jnp.where(low, 0.0, turned), jnp.where(low, 0.0, v)]
    return jnp.stack(pair, axis=1).reshape(TILE, width)


def kernel(
    feat_hbm, cot_hbm, mask_hbm, wconv_hbm, wpoint_hbm, bias_hbm,
    fg_hbm, sums_hbm,
    mask_ref, wconv_ref, wpoint_ref, bias_ref,
    feat, cot, mir_send, relay, mir_recv, act, grad, res, res_half, slope, pre_slope, post, gnat,
    mat_f, mat_b, mat_p, keep, prev, csum, psum, bsum, out,
    ns_send, ew_send, corner_send, ns_recv, ew_recv, corner_recv, payload, part1, sum1, part2, sum2, part3,
    in_sem, out_sem, spread_ssem, spread_rsem, mir_ssem, mir_rsem, halo_ssem, halo_rsem, red_ssem, red_rsem,
):
    r, c = lax.axis_index("row"), lax.axis_index("col")
    a, b = lax.div(c, 4), lax.rem(c, 4)
    y, zh = lax.div(c, 8), lax.rem(a, 2)
    group_a, group_b = zh * 8 + r, y * 4 + b

    def mirror_to(x, row):
        return {"row": 2 * row + zh, "col": 4 * r + x}

    def mirror_from(x, row):
        return {"row": a, "col": 8 * row + 4 * lax.rem(r, 2) + x}

    def member_a(m):
        return {"row": lax.rem(m, 8), "col": y * 8 + lax.div(m, 8) * 4 + b}

    def member_b(m):
        return {"row": r, "col": lax.div(m, 4) * 8 + zh * 4 + lax.rem(m, 4)}

    def beside(dr, dc):
        return {"row": lax.rem(r + dr + ROWS, ROWS), "col": lax.rem(c + dc + COLS, COLS)}

    own_mirror = a == r
    sides = [(0, 1), (0, -1), (1, 0), (-1, 0), (1, 1), (-1, 1), (1, -1), (-1, -1)]

    barrier = pltpu.get_barrier_semaphore()

    def greet(device):
        pl.semaphore_signal(barrier, inc=1, device_id=device, device_id_type=MESH)

    @pl.when(jnp.logical_not(own_mirror))
    def _():
        greet(mirror_to(b, y))
        greet(mirror_from(b, y))

    def greet_mirrors(n, _):
        x, row = lax.rem(b + lax.div(n, 4), 4), lax.rem(y + n, 4)
        greet(mirror_to(x, row))
        greet(mirror_from(x, row))
        return 0

    lax.fori_loop(1, GROUP, greet_mirrors, 0)
    for dr, dc in sides:
        greet(beside(dr, dc))

    def greet_groups(d, _):
        greet(member_a(lax.rem(group_a + d, GROUP)))
        greet(member_b(lax.rem(group_b + d, GROUP)))
        return 0

    lax.fori_loop(1, GROUP, greet_groups, 0)

    load_cot = pltpu.make_async_copy(cot_hbm, cot, in_sem.at[0])
    load_feat = pltpu.make_async_copy(feat_hbm, feat, in_sem.at[1])
    loads = [
        pltpu.make_async_copy(source, target, in_sem.at[2 + n])
        for n, (source, target) in enumerate(
            [(mask_hbm, mask_ref), (wconv_hbm, wconv_ref), (wpoint_hbm, wpoint_ref), (bias_hbm, bias_ref)]
        )
    ]
    load_cot.start()
    load_feat.start()
    for copy in loads:
        copy.start()

    load_cot.wait()
    ident = (iota((256, 256), 0) == iota((256, 256), 1)).astype(BF16)

    def turn(g, _):
        block = cot[at(4 * g, 4)].reshape(256, 256)
        turned = dot_nt(ident, block).astype(BF16)
        mir_send[:, :, at(16 * g, 16), :] = turned.reshape(4, 4, 16, 256)
        return 0

    lax.fori_loop(0, 8, turn, 0)

    low = iota((32, 8, 256), 1) < 4

    centre = {0: lambda t: TAPS * t + TILE, 1: lambda t: TILE * t}

    def put(phase, t, tile):
        ref = (act, grad)[phase]
        ref[at(centre[phase](t), TILE), :] = tile.reshape(TILE, 256).astype(BF16)

    def activations():
        load_feat.wait()
        prev[...] = jnp.zeros_like(prev)

        def activate(k, _):
            x = feat[:, at(16 * k, 16), :].astype(F32)
            for h in range(2):
                t = 2 * k + h
                v = x[:, 8 * h : 8 * h + 8, :]
                s = sigmoid(v)
                slope[at(TILE * t, TILE), :] = (s * (1.0 + v * (1.0 - s))).reshape(TILE, 256)
                turned = pltpu.roll(v * s, 4, 1)
                put(0, t, jnp.where(low, prev[...], turned))
                prev[...] = turned
            return 0

        lax.fori_loop(0, 4, activate, 0)
        put(0, TILES, jnp.where(low, prev[...], 0.0))

    def halo_copies(phase):
        diagonal = corner_send.at[phase]
        pairs = [
            (ns_send.at[phase, 1], ns_recv.at[phase, 0]),
            (ns_send.at[phase, 0], ns_recv.at[phase, 1]),
            (ew_send.at[phase, 48:96], ew_recv.at[phase, 48:96]),
            (ew_send.at[phase, 0:48], ew_recv.at[phase, 0:48]),
            (diagonal, corner_recv.at[phase, 0]),
            (diagonal, corner_recv.at[phase, 1]),
            (diagonal, corner_recv.at[phase, 2]),
            (diagonal, corner_recv.at[phase, 3]),
        ]
        return [
            pltpu.make_async_remote_copy(
                src_ref=src,
                dst_ref=dst,
                send_sem=halo_ssem.at[phase, n],
                recv_sem=halo_rsem.at[phase, n],
                device_id=beside(*sides[n]),
                device_id_type=MESH,
            )
            for n, (src, dst) in enumerate(pairs)
        ]

    def halo_pack(phase):
        ref = (act, grad)[phase]
        first, last = centre[phase](0), centre[phase](TILES)
        ns_send[phase, 0] = pack(ref[first : first + TILE, :].astype(F32), False)
        ns_send[phase, 1] = pack(ref[last : last + TILE, :].astype(F32), True)
        row, col = iota((96, 256), 0), iota((96, 256), 1)

        def gather(t, total):
            pick = ((row == 4 * t + col) & (col < 4)) | ((row == 4 * t + col - 204) & (col >= 252))
            return total + dot_nt(one_hot(pick), ref[at(centre[phase](t), TILE), :])

        edge = lax.fori_loop(0, TILES + 1, gather, jnp.zeros((96, 256), F32))
        ew_send[phase] = edge.astype(BF16)
        row, col = iota((8, 256), 0), iota((8, 256), 1)
        pick = one_hot(((row == col) & (row < 4)) | ((row == col - 248) & (row >= 4)))
        corners = [dot_nt(pick, ns_send[phase, n]) for n in range(2)]
        corner_send[phase] = jnp.concatenate(corners, axis=0).astype(BF16)

    up, down, left, right = c > 0, c < COLS - 1, r > 0, r < ROWS - 1

    def only(flag, value):
        return jnp.where(flag, value, 0.0)

    def halo_edge(phase):
        row, lane = iota((96, 128), 0), iota((96, 128), 1)
        straight = ((row == lane) & (row < 48) & right) | ((row == lane - 16) & (lane >= 64) & left)
        edge = dot_tn(ew_recv[phase], one_hot(straight))
        row, lane = iota((16, 128), 0), iota((16, 128), 1)

        def place(n, first, start, flag):
            hit = (row >= first) & (row < first + 4) & (lane == row - first + start) & flag
            return dot_tn(corner_recv[phase, n], one_hot(hit))

        above = place(0, 12, 64, left & up) + place(1, 8, 0, right & up)
        below = place(2, 4, 96, left & down) + place(3, 0, 32, right & down)
        return (edge + unpack(above, True) + unpack(below, False)).astype(BF16)

    def halo_rows(phase):
        above = only(up, unpack(ns_recv[phase, 0], True))
        below = only(down, unpack(ns_recv[phase, 1], False))
        return above, below

    def act_fill():
        above, below = halo_rows(0)
        for t, value in ((0, above), (TILES, below)):
            rows = slice(TAPS * t + TILE, TAPS * t + 2 * TILE)
            act[rows, :] = (act[rows, :].astype(F32) + value).astype(BF16)
        edge = halo_edge(0)
        from_j, to_j = iota((256, 512), 0), iota((256, 512), 1)
        shift = one_hot(((to_j < 256) & (from_j == to_j - 4)) | ((to_j >= 256) & (from_j == to_j - 252)))
        lane, col = iota((128, 512), 0), iota((128, 512), 1)

        def spread(t, _):
            place = ((col < 4) & (lane == 64 + 4 * t + col)) | ((col >= 508) & (lane == 4 * t + col - 508))
            both = dot(act[at(TAPS * t + TILE, TILE), :], shift) + dot(edge, one_hot(place))
            act[at(TAPS * t, TILE), :] = both[:, :256].astype(BF16)
            act[at(TAPS * t + 2 * TILE, TILE), :] = both[:, 256:].astype(BF16)
            return 0

        lax.fori_loop(0, TILES + 1, spread, 0)

    def rows_of(part):
        return pl.ds(*SLICES[part])

    def spread_copy(part, n):
        dx, dy = lax.div(n, 4), lax.rem(n, 4)
        to_x, to_y = lax.rem(b + dx, 4), lax.rem(y + dy, 4)
        return pltpu.make_async_remote_copy(
            src_ref=mir_send.at[to_x, rows_of(part), at(32 * to_y, 32), :],
            dst_ref=relay.at[y, to_x, rows_of(part)],
            send_sem=spread_ssem.at[part, n],
            recv_sem=spread_rsem.at[part, n],
            device_id=member_b(4 * to_y + b),
            device_id_type=MESH,
        )

    def relay_copy(part, n):
        dx, dy = lax.div(n, 4), lax.rem(n, 4)
        to_x, from_y = lax.rem(b + dx, 4), lax.rem(y - dy + 4, 4)
        return pltpu.make_async_remote_copy(
            src_ref=relay.at[from_y, to_x, rows_of(part)],
            dst_ref=mir_recv.at[b, rows_of(part), at(32 * y, 32), :],
            send_sem=mir_ssem.at[part, n],
            recv_sem=mir_rsem.at[part, 4 * y + b],
            device_id=mirror_to(to_x, from_y),
            device_id_type=MESH,
        )

    def own_copy(part):
        return pltpu.make_async_copy(
            relay.at[y, b, rows_of(part)],
            mir_recv.at[b, rows_of(part), at(32 * y, 32), :],
            mir_rsem.at[part, 4 * y + b],
        )

    def arrival(part, n):
        from_y, from_x = lax.div(n, 4), lax.rem(n, 4)
        return pltpu.make_async_remote_copy(
            src_ref=relay.at[from_y, from_x, rows_of(part)],
            dst_ref=mir_recv.at[from_x, rows_of(part), at(32 * from_y, 32), :],
            send_sem=mir_ssem.at[part, n],
            recv_sem=mir_rsem.at[part, n],
            device_id=mirror_from(from_x, from_y),
            device_id_type=MESH,
        )

    for x in range(4):
        relay[y, x] = mir_send[x, :, at(32 * y, 32), :]
    pl.semaphore_wait(barrier, 2 * GROUP + 8 + 2 * (GROUP - 1) - 2 * own_mirror.astype(jnp.int32))

    def relayed(n):
        return lax.rem(n, 4) > 0

    def each(part, step, count=GROUP):
        lax.fori_loop(0, count, lambda n, _: step(part, n), 0)

    def send_spread(part, n):
        @pl.when(relayed(n))
        def _():
            spread_copy(part, n).start()

        return 0

    def start_own(part, m):
        stays = own_mirror & (m == 0)

        @pl.when(stays)
        def _():
            own_copy(part).start()

        @pl.when(jnp.logical_not(stays))
        def _():
            relay_copy(part, 4 * m).start()

        return 0

    def pass_on(part, n):
        @pl.when(relayed(n))
        def _():
            spread_copy(part, n).wait_recv()
            relay_copy(part, n).start()

        return 0

    def sent(part, n):
        @pl.when(relayed(n))
        def _():
            spread_copy(part, n).wait_send()

        @pl.when(jnp.logical_not(own_mirror & (n == 0)))
        def _():
            relay_copy(part, n).wait_send()

        return 0

    for part in range(len(SLICES)):
        each(part, send_spread)
    for part in range(len(SLICES)):
        each(part, start_own, 4)
    activations()
    halo_pack(0)
    for copy in halo_copies(0):
        copy.start()

    each(0, pass_on)

    for copy in loads:
        copy.wait()

    spread_out = (lax.div(iota((256, 32), 0), 8) == iota((256, 32), 1)).astype(F32).astype(BF16)
    spread_in = (lax.div(iota((32, 256), 1), 8) == iota((32, 256), 0)).astype(F32).astype(BF16)
    row_out, row_in = lax.rem(iota((256, 256), 0), 8), lax.rem(iota((256, 256), 1), 8)

    def expand(w, turned):
        rows = dot_nt(spread_out, w) if turned else dot(spread_out, w)
        return dot(rows.astype(BF16), spread_in)

    def banded(taps):
        near = jnp.where(row_in == row_out, taps[0], 0.0) + jnp.where(row_in == row_out + 4, taps[1], 0.0)
        far = jnp.where(row_in == row_out, taps[2], 0.0) + jnp.where(row_in == row_out - 4, taps[1], 0.0)
        return near.astype(BF16), far.astype(BF16)

    for tap in range(3):
        near, far = banded([expand(wconv_ref[n, tap], False) for n in range(3)])
        mat_f[:, tap * TILE : (tap + 1) * TILE] = near
        mat_f[:, TAPS + tap * TILE : TAPS + (tap + 1) * TILE] = far
        near, far = banded([expand(wconv_ref[2 - n, 2 - tap], True) for n in range(3)])
        mat_b[tap * TILE : (tap + 1) * TILE, :TILE] = near
        mat_b[tap * TILE : (tap + 1) * TILE, TILE:] = far
    mat_p[...] = jnp.where(row_in == row_out, expand(wpoint_ref[...], True), 0.0).astype(BF16)

    bias_col = jnp.sum(
        jnp.where(lax.div(iota((256, 32), 0), 8) == iota((256, 32), 1), bias_ref[...], 0.0), axis=1, keepdims=True
    )
    mask_row = mask_ref[:, at(256 * a, 256)].astype(F32)
    diagonal = iota((64, 256), 1) == iota((64, 256), 0) + 64 * b
    row_keep = jnp.sum(jnp.where(diagonal, mask_row, 0.0), axis=1, keepdims=True)
    keep[...] = row_keep * (0.5 * mask_ref[:, at(256 * r, 256)].astype(F32))

    csum[...] = jnp.zeros_like(csum)
    psum[...] = jnp.zeros_like(psum)
    bsum[...] = jnp.zeros_like(bsum)

    each(1, pass_on)
    for copy in halo_copies(0):
        copy.wait_recv()
    act_fill()

    def forward(t, _):
        v = dot(mat_f[...], act[pl.ds(pl.multiple_of(TAPS * t, TAPS), 2 * TAPS), :])
        v = v + bias_col
        s = sigmoid(v)
        post[at(TILE * t, TILE), :] = (v * s).astype(BF16)
        pre_slope[at(TILE * t, TILE), :] = s * (1.0 + v * (1.0 - s))
        return 0

    lax.fori_loop(0, TILES, forward, 0)

    prev[...] = jnp.zeros_like(prev)
    left_half = iota((8, 8, 128), 2) < 64

    def arrive(part, n):
        stays = own_mirror & (n == 4 * y + b)

        @pl.when(stays)
        def _():
            own_copy(part).wait()

        @pl.when(jnp.logical_not(stays))
        def _():
            arrival(part, n).wait_recv()

        return 0

    def chunk(k, _):
        for part, (first, _) in enumerate(SLICES):

            @pl.when(k == first)
            def _():
                each(part, arrive)

        here = cot[:, at(16 * k, 16), :].astype(F32)
        keep_rows = keep[at(16 * k, 16), :]
        got = [mir_recv[n, k].astype(F32).reshape(8, 16, 256) for n in range(4)]
        for h in range(2):
            t = 2 * k + h
            part = [v[:, 8 * h : 8 * h + 8, :] for v in got]
            quads = []
            for m in range(4):
                cols = slice(128 * (m // 2), 128 * (m // 2) + 128)
                pieces = []
                for n in (0, 2):
                    one, two = part[n][:, :, cols], part[n + 1][:, :, cols]
                    if m % 2 == 0:
                        pieces.append(jnp.where(left_half, one, pltpu.roll(two, 64, 2)))
                    else:
                        pieces.append(jnp.where(left_half, pltpu.roll(one, 64, 2), two))
                quads.append(jnp.concatenate(pieces, axis=2))
            mirrored = jnp.stack(quads, axis=1).reshape(32, 8, 256)
            residual = keep_rows[8 * h : 8 * h + 8][None] * (here[:, 8 * h : 8 * h + 8, :] + mirrored)
            residual = residual.reshape(TILE, 256)
            half = residual.astype(BF16)
            res[at(TILE * t, TILE), :] = residual
            res_half[at(TILE * t, TILE), :] = half
            g = pre_slope[at(TILE * t, TILE), :] * dot(mat_p[...], half)
            gnat[at(TILE * t, TILE), :] = g.astype(BF16)
            turned = pltpu.roll(g.reshape(32, 8, 256), 4, 1)
            put(1, t, jnp.where(low, prev[...], turned))
            prev[...] = turned

        @pl.when(k == 3)
        def _():
            put(1, TILES, jnp.where(low, prev[...], 0.0))

        total, point, line = csum[...], psum[...], bsum[...]
        for h in range(2):
            t = 2 * k + h
            g = gnat[at(TILE * t, TILE), :]
            total = total + dot_nt(g, act[pl.ds(pl.multiple_of(TAPS * t, TAPS), 2 * TAPS), :])
            point = point + dot_nt(res_half[at(TILE * t, TILE), :], post[at(TILE * t, TILE), :])
            wide = g.astype(F32)
            line = line + wide[:, :128] + wide[:, 128:]
        csum[...] = total
        psum[...] = point
        bsum[...] = line
        return 0

    lax.fori_loop(0, 4, chunk, 0)

    def exchange(stage, me, member, source, dst):
        def copy(to):
            return pltpu.make_async_remote_copy(
                src_ref=source(to),
                dst_ref=dst.at[me],
                send_sem=red_ssem.at[stage],
                recv_sem=red_rsem.at[stage],
                device_id=member(to),
                device_id_type=MESH,
            )

        def start(d, _):
            copy(lax.rem(me + d, GROUP)).start()
            return 0

        def wait(sem):
            others = dst.at[0 : GROUP - 1]
            pltpu.make_async_copy(others, others, sem.at[stage]).wait()

        return (
            copy,
            lambda: lax.fori_loop(1, GROUP, start, 0),
            lambda: wait(red_rsem),
            lambda: wait(red_ssem),
        )

    first_copy, _, arrive1, leave1 = exchange(0, group_b, member_b, lambda m: payload.at[m], part1)
    _, start2, arrive2, leave2 = exchange(1, group_a, member_a, lambda m: sum1, part2)
    _, start3, arrive3, leave3 = exchange(2, group_b, member_b, lambda m: sum2, part3)

    def send_payload(m):
        @pl.when(group_b == m)
        def _():
            part1[m] = payload[m]

        @pl.when(group_b != m)
        def _():
            first_copy(m).start()

    col_in = lax.div(iota((256, 128), 0), 8)
    col_out = iota((256, 128), 1)
    for quad in range(3):
        lanes = jnp.zeros((256, 128), F32)
        for slot in range(4):
            n = 4 * quad + slot
            if n > 9:
                continue
            if n == 9:
                v = jnp.where(row_in == row_out, psum[...], 0.0)
            else:
                row_tap, col_tap = n // 3, n % 3
                near = csum[:, col_tap * TILE : (col_tap + 1) * TILE]
                far = csum[:, TAPS + col_tap * TILE : TAPS + (col_tap + 1) * TILE]
                if row_tap == 0:
                    v = jnp.where(row_in == row_out, near, 0.0)
                elif row_tap == 2:
                    v = jnp.where(row_in == row_out, far, 0.0)
                else:
                    v = jnp.where(row_in == row_out + 4, near, 0.0) + jnp.where(row_in == row_out - 4, far, 0.0)
            pick = (col_out == 32 * slot + col_in).astype(F32).astype(BF16)
            high = v.astype(BF16)
            lanes = lanes + (dot(high, pick) + dot((v - high.astype(F32)).astype(BF16), pick))
        if quad == 2:
            line = jnp.sum(bsum[...], axis=1, keepdims=True)
            lanes = lanes + jnp.where((col_out >= 64) & (col_out < 96), line, 0.0)
        lanes = jnp.sum(lanes.reshape(32, 8, 128), axis=1)
        for o in range(4):
            payload[4 * quad + o] = lanes[8 * o : 8 * o + 8]
            send_payload(4 * quad + o)
    for o in range(12, GROUP):
        payload[o] = jnp.zeros((8, 128), F32)
        send_payload(o)

    def total_of(ref):
        total = ref[0]
        for n in range(1, GROUP):
            total = total + ref[n]
        return total

    halo_pack(1)
    for copy in halo_copies(1):
        copy.start()

    lane256 = iota((TILE, 256), 1)

    def over_taps(v):
        west = jnp.where(lane256 >= 4, pltpu.roll(v[:TILE], 4, 1), 0.0)
        east = jnp.where(lane256 < 252, pltpu.roll(v[2 * TILE :], 252, 1), 0.0)
        return v[TILE : 2 * TILE] + west + east

    def inner(t, _):
        v = dot(mat_b[...], grad[pl.ds(pl.multiple_of(TILE * t, TILE), 2 * TILE), :])
        pre_slope[at(TILE * t, TILE), :] = over_taps(v)
        return 0

    lax.fori_loop(0, FIRST, inner, 0)
    arrive1()
    sum1[...] = total_of(part1)
    part2[group_a] = sum1[...]
    start2()
    lax.fori_loop(FIRST, SECOND, inner, 0)
    leave1()
    arrive2()
    sum2[...] = total_of(part2)
    part3[group_b] = sum2[...]
    start3()

    leave2()
    lax.fori_loop(SECOND, TILES, inner, 0)
    for copy in halo_copies(1):
        copy.wait()
    above, below = halo_rows(1)
    pre_slope[:TILE, :] += over_taps(dot(mat_b[:, :TILE], above.astype(BF16)))
    pre_slope[TILE * (TILES - 1) :, :] += over_taps(dot(mat_b[:, TILE:], below.astype(BF16)))
    edge = halo_edge(1)
    from_west = dot(mat_b[:TILE, :TILE], edge) + pltpu.roll(dot(mat_b[:TILE, TILE:], edge), 124, 1)
    from_east = dot(mat_b[2 * TILE :, :TILE], edge) + pltpu.roll(dot(mat_b[2 * TILE :, TILE:], edge), 124, 1)
    lane128 = iota((TILE, 128), 1)
    outer = jnp.where(lane128 < 64, from_east, from_west)

    def store_out(k):
        rows = at(16 * k, 16)
        return pltpu.make_async_copy(out.at[:, rows, :], fg_hbm.at[:, rows, :], out_sem.at[k])

    def backward(k, _):
        halves = []
        for h in range(2):
            t = 2 * k + h
            west = jnp.where(lane128 < 4, pltpu.roll(outer, lax.rem(192 - 4 * t, 128), 1), 0.0)
            east = jnp.where(lane128 >= 124, pltpu.roll(outer, 124 - 4 * t, 1), 0.0)
            v = pre_slope[at(TILE * t, TILE), :] + jnp.concatenate([west, east], axis=1)
            v = res[at(TILE * t, TILE), :] + slope[at(TILE * t, TILE), :] * v
            halves.append(v.reshape(32, 8, 256))
        out[:, at(16 * k, 16), :] = jnp.concatenate(halves, axis=1).astype(BF16)
        store_out(k).start()
        return 0

    lax.fori_loop(0, 4, backward, 0)
    for part in range(len(SLICES)):
        each(part, sent)
    for copy in halo_copies(0):
        copy.wait_send()
    arrive3()

    store_sums = pltpu.make_async_copy(part3.at[0:12], sums_hbm, out_sem.at[4])
    store_sums.start()

    leave3()
    for k in range(4):
        store_out(k).wait()
    store_sums.wait()


def finish(
    fg_hbm, sums_hbm, out_hbm, conv_hbm, point_hbm, biasg_hbm, held, sums_ref, conv_ref, point_ref, biasg_ref, sem
):
    parts = [slice(8 * n, 8 * n + 8) for n in range(4)]
    loads = [pltpu.make_async_copy(fg_hbm.at[p], held.at[p], sem.at[0, n]) for n, p in enumerate(parts)]
    stores = [pltpu.make_async_copy(held.at[p], out_hbm.at[p], sem.at[1, n]) for n, p in enumerate(parts)]
    load_sums = pltpu.make_async_copy(sums_hbm, sums_ref, sem.at[2, 0])
    load_sums.start()
    for copy in loads:
        copy.start()
    for load, store in zip(loads, stores):
        load.wait()
        store.start()
    load_sums.wait()
    scale = 1.0 / 2048.0
    for quad in range(3):
        lanes = jnp.concatenate([sums_ref[4 * quad + o] for o in range(4)], axis=0) * scale
        for slot in range(4):
            n = 4 * quad + slot
            block = lanes if slot == 0 else pltpu.roll(lanes, 128 - 32 * slot, 1)
            if n < 9:
                conv_ref[n // 3, n % 3] = block[:, :32]
            elif n == 9:
                point_ref[...] = block[:, :32]
            elif n == 10:
                square = block[:, :32]
                biasg_ref[...] = jnp.sum(
                    jnp.where(iota((32, 32), 0) == iota((32, 32), 1), square, 0.0), axis=0, keepdims=True
                )
    small = [
        pltpu.make_async_copy(source, target, sem.at[2, 1 + n])
        for n, (source, target) in enumerate([(conv_ref, conv_hbm), (point_ref, point_hbm), (biasg_ref, biasg_hbm)])
    ]
    for copy in small:
        copy.start()
    for copy in stores + small:
        copy.wait()


def shards(features, cotangent, mask, w_conv, w_point, bias):
    hbm = pl.BlockSpec(memory_space=pl.ANY)
    big = (TILES * TILE, 256)
    fg, sums = pl.pallas_call(
        kernel,
        out_shape=(
            jax.ShapeDtypeStruct((32, 64, 256), BF16),
            jax.ShapeDtypeStruct((12, 8, 128), F32),
        ),
        in_specs=[hbm] * 6,
        out_specs=(hbm, hbm),
        scratch_shapes=[
            pltpu.VMEM((1, 2048), jnp.int32),
            pltpu.VMEM((3, 3, 32, 32), BF16),
            pltpu.VMEM((32, 32), BF16),
            pltpu.VMEM((1, 32), F32),
            pltpu.VMEM((32, 64, 256), BF16),
            pltpu.VMEM((32, 64, 256), BF16),
            pltpu.VMEM((4, 4, 128, 256), BF16),
            pltpu.VMEM((4, 4, 4, 32, 256), BF16),
            pltpu.VMEM((4, 4, 128, 256), BF16),
            pltpu.VMEM(((TILES + 1) * TAPS, 256), BF16),
            pltpu.VMEM(((TILES + 1) * TILE, 256), BF16),
            pltpu.VMEM(big, F32),
            pltpu.VMEM(big, BF16),
            pltpu.VMEM(big, F32),
            pltpu.VMEM(big, F32),
            pltpu.VMEM(big, BF16),
            pltpu.VMEM(big, BF16),
            pltpu.VMEM((TILE, 2 * TAPS), BF16),
            pltpu.VMEM((TAPS, 2 * TILE), BF16),
            pltpu.VMEM((TILE, TILE), BF16),
            pltpu.VMEM((64, 256), F32),
            pltpu.VMEM((32, 8, 256), F32),
            pltpu.VMEM((TILE, 2 * TAPS), F32),
            pltpu.VMEM((TILE, TILE), F32),
            pltpu.VMEM((TILE, 128), F32),
            pltpu.VMEM((32, 64, 256), BF16),
            pltpu.VMEM((2, 2, 128, 256), BF16),
            pltpu.VMEM((2, 96, 256), BF16),
            pltpu.VMEM((2, 16, 128), BF16),
            pltpu.VMEM((2, 2, 128, 256), BF16),
            pltpu.VMEM((2, 96, 256), BF16),
            pltpu.VMEM((2, 4, 16, 128), BF16),
            pltpu.VMEM((GROUP, 8, 128), F32),
            pltpu.VMEM((GROUP, 8, 128), F32),
            pltpu.VMEM((8, 128), F32),
            pltpu.VMEM((GROUP, 8, 128), F32),
            pltpu.VMEM((8, 128), F32),
            pltpu.VMEM((GROUP, 8, 128), F32),
            pltpu.SemaphoreType.DMA((6,)),
            pltpu.SemaphoreType.DMA((5,)),
            pltpu.SemaphoreType.DMA((len(SLICES), GROUP)),
            pltpu.SemaphoreType.DMA((len(SLICES), GROUP)),
            pltpu.SemaphoreType.DMA((len(SLICES), GROUP)),
            pltpu.SemaphoreType.DMA((len(SLICES), GROUP)),
            pltpu.SemaphoreType.DMA((2, 8)),
            pltpu.SemaphoreType.DMA((2, 8)),
            pltpu.SemaphoreType.DMA((3,)),
            pltpu.SemaphoreType.DMA((3,)),
        ],
        compiler_params=pltpu.CompilerParams(
            collective_id=0, has_side_effects=True, vmem_limit_bytes=56 * 1024 * 1024
        ),
        cost_estimate=pl.CostEstimate(flops=5_400_000_000, bytes_accessed=3 * 1024 * 1024, transcendentals=2_000_000),
    )(features, cotangent, mask.reshape(1, 2048), w_conv, w_point, bias.reshape(1, 32))
    fg, conv, point, bias_grad = pl.pallas_call(
        finish,
        out_shape=(
            jax.ShapeDtypeStruct((32, 64, 256), BF16),
            jax.ShapeDtypeStruct((3, 3, 32, 32), F32),
            jax.ShapeDtypeStruct((32, 32), F32),
            jax.ShapeDtypeStruct((1, 32), F32),
        ),
        in_specs=[hbm, hbm],
        out_specs=(hbm, hbm, hbm, hbm),
        scratch_shapes=[
            pltpu.VMEM((32, 64, 256), BF16),
            pltpu.VMEM((12, 8, 128), F32),
            pltpu.VMEM((3, 3, 32, 32), F32),
            pltpu.VMEM((32, 32), F32),
            pltpu.VMEM((1, 32), F32),
            pltpu.SemaphoreType.DMA((3, 4)),
        ],
    )(fg, sums)
    return fg, conv, point, bias_grad.reshape(32)


def solution(mesh):
    in_specs = (P(None, "col", "row"), P(None, "col", "row"), P(), P(), P(), P())
    out_specs = (P(None, "col", "row"), P(), P(), P())
    return jax.shard_map(shards, mesh=mesh, in_specs=in_specs, out_specs=out_specs, check_vma=False)
```

```python
import jax
import jax.numpy as jnp
from jax import lax
from jax.experimental import pallas as pl
from jax.experimental.pallas import tpu as pltpu
from jax.sharding import PartitionSpec as P

F32, BF16 = jnp.float32, jnp.bfloat16
MESH = pl.DeviceIdType.MESH
ROWS, COLS = 8, 32
TILE = 256
TAPS = 3 * TILE
TILES = 8
GROUP = 16
FIRST, SECOND = 2, 5
SLICES = ((0, 3), (3, 1))
NT = (((1,), (1,)), ((), ()))
TN = (((0,), (0,)), ((), ()))


def iota(shape, dim):
    return lax.broadcasted_iota(jnp.int32, shape, dim)


def dot(x, y):
    return jnp.dot(x, y, preferred_element_type=F32)


def dot_nt(x, y):
    return lax.dot_general(x, y, NT, preferred_element_type=F32)


def dot_tn(x, y):
    return lax.dot_general(x, y, TN, preferred_element_type=F32)


def one_hot(where):
    return where.astype(F32).astype(BF16)


def at(start, size):
    return pl.ds(pl.multiple_of(start, size), size)


def sigmoid(v):
    return 1.0 / (1.0 + jnp.exp(-v))


def pack(tile, bottom):
    v = tile.reshape(16, 2, 8, 256)
    low = iota((16, 8, 256), 1) < 4
    if bottom:
        v = jnp.where(low, v[:, 0], pltpu.roll(v[:, 1], 4, 1))
    else:
        v = jnp.where(low, pltpu.roll(v[:, 0], 4, 1), v[:, 1])
    return v.reshape(128, 256).astype(BF16)


def unpack(packed, bottom):
    width = packed.shape[1]
    v = packed.astype(F32).reshape(16, 8, width)
    turned = pltpu.roll(v, 4, 1)
    low = iota((16, 8, width), 1) < 4
    if bottom:
        pair = [jnp.where(low, v, 0.0), jnp.where(low, turned, 0.0)]
    else:
        pair = [jnp.where(low, 0.0, turned), jnp.where(low, 0.0, v)]
    return jnp.stack(pair, axis=1).reshape(TILE, width)


def kernel(
    feat_hbm, cot_hbm, mask_hbm, wconv_hbm, wpoint_hbm, bias_hbm,
    fg_hbm, sums_hbm,
    mask_ref, wconv_ref, wpoint_ref, bias_ref,
    feat, cot, mir_send, relay, mir_recv, act, grad, res, res_half, slope, pre_slope, post, gnat,
    mat_f, mat_b, mat_p, keep, prev, csum, psum, bsum, out,
    ns_send, ew_send, corner_send, ns_recv, ew_recv, corner_recv, payload, part1, sum1, part2, sum2, part3,
    in_sem, out_sem, spread_ssem, spread_rsem, mir_ssem, mir_rsem, halo_ssem, halo_rsem, red_ssem, red_rsem,
):
    r, c = lax.axis_index("row"), lax.axis_index("col")
    a, b = lax.div(c, 4), lax.rem(c, 4)
    y, zh = lax.div(c, 8), lax.rem(a, 2)
    group_a, group_b = zh * 8 + r, y * 4 + b

    def mirror_to(x, row):
        return {"row": 2 * row + zh, "col": 4 * r + x}

    def mirror_from(x, row):
        return {"row": a, "col": 8 * row + 4 * lax.rem(r, 2) + x}

    def member_a(m):
        return {"row": lax.rem(m, 8), "col": y * 8 + lax.div(m, 8) * 4 + b}

    def member_b(m):
        return {"row": r, "col": lax.div(m, 4) * 8 + zh * 4 + lax.rem(m, 4)}

    def beside(dr, dc):
        return {"row": lax.rem(r + dr + ROWS, ROWS), "col": lax.rem(c + dc + COLS, COLS)}

    own_mirror = a == r
    sides = [(0, 1), (0, -1), (1, 0), (-1, 0), (1, 1), (-1, 1), (1, -1), (-1, -1)]

    barrier = pltpu.get_barrier_semaphore()

    def greet(device):
        pl.semaphore_signal(barrier, inc=1, device_id=device, device_id_type=MESH)

    @pl.when(jnp.logical_not(own_mirror))
    def _():
        greet(mirror_to(b, y))
        greet(mirror_from(b, y))

    def greet_mirrors(n, _):
        x, row = lax.rem(b + lax.div(n, 4), 4), lax.rem(y + n, 4)
        greet(mirror_to(x, row))
        greet(mirror_from(x, row))
        return 0

    lax.fori_loop(1, GROUP, greet_mirrors, 0)
    for dr, dc in sides:
        greet(beside(dr, dc))

    def greet_groups(d, _):
        greet(member_a(lax.rem(group_a + d, GROUP)))
        greet(member_b(lax.rem(group_b + d, GROUP)))
        return 0

    lax.fori_loop(1, GROUP, greet_groups, 0)

    load_cot = pltpu.make_async_copy(cot_hbm, cot, in_sem.at[0])
    load_feat = pltpu.make_async_copy(feat_hbm, feat, in_sem.at[1])
    loads = [
        pltpu.make_async_copy(source, target, in_sem.at[2 + n])
        for n, (source, target) in enumerate(
            [(mask_hbm, mask_ref), (wconv_hbm, wconv_ref), (wpoint_hbm, wpoint_ref), (bias_hbm, bias_ref)]
        )
    ]
    load_cot.start()
    load_feat.start()
    for copy in loads:
        copy.start()

    load_cot.wait()
    ident = (iota((256, 256), 0) == iota((256, 256), 1)).astype(BF16)

    def turn(g, _):
        block = cot[at(4 * g, 4)].reshape(256, 256)
        turned = dot_nt(ident, block).astype(BF16)
        mir_send[:, :, at(16 * g, 16), :] = turned.reshape(4, 4, 16, 256)
        return 0

    lax.fori_loop(0, 8, turn, 0)

    low = iota((32, 8, 256), 1) < 4

    centre = {0: lambda t: TAPS * t + TILE, 1: lambda t: TILE * t}

    def put(phase, t, tile):
        ref = (act, grad)[phase]
        ref[at(centre[phase](t), TILE), :] = tile.reshape(TILE, 256).astype(BF16)

    def activations():
        load_feat.wait()
        prev[...] = jnp.zeros_like(prev)

        def activate(k, _):
            x = feat[:, at(16 * k, 16), :].astype(F32)
            for h in range(2):
                t = 2 * k + h
                v = x[:, 8 * h : 8 * h + 8, :]
                s = sigmoid(v)
                slope[at(TILE * t, TILE), :] = (s * (1.0 + v * (1.0 - s))).reshape(TILE, 256)
                turned = pltpu.roll(v * s, 4, 1)
                put(0, t, jnp.where(low, prev[...], turned))
                prev[...] = turned
            return 0

        lax.fori_loop(0, 4, activate, 0)
        put(0, TILES, jnp.where(low, prev[...], 0.0))

    def halo_copies(phase):
        diagonal = corner_send.at[phase]
        pairs = [
            (ns_send.at[phase, 1], ns_recv.at[phase, 0]),
            (ns_send.at[phase, 0], ns_recv.at[phase, 1]),
            (ew_send.at[phase, 48:96], ew_recv.at[phase, 48:96]),
            (ew_send.at[phase, 0:48], ew_recv.at[phase, 0:48]),
            (diagonal, corner_recv.at[phase, 0]),
            (diagonal, corner_recv.at[phase, 1]),
            (diagonal, corner_recv.at[phase, 2]),
            (diagonal, corner_recv.at[phase, 3]),
        ]
        return [
            pltpu.make_async_remote_copy(
                src_ref=src,
                dst_ref=dst,
                send_sem=halo_ssem.at[phase, n],
                recv_sem=halo_rsem.at[phase, n],
                device_id=beside(*sides[n]),
                device_id_type=MESH,
            )
            for n, (src, dst) in enumerate(pairs)
        ]

    def halo_pack(phase):
        ref = (act, grad)[phase]
        first, last = centre[phase](0), centre[phase](TILES)
        ns_send[phase, 0] = pack(ref[first : first + TILE, :].astype(F32), False)
        ns_send[phase, 1] = pack(ref[last : last + TILE, :].astype(F32), True)
        row, col = iota((96, 256), 0), iota((96, 256), 1)

        def gather(t, total):
            pick = ((row == 4 * t + col) & (col < 4)) | ((row == 4 * t + col - 204) & (col >= 252))
            return total + dot_nt(one_hot(pick), ref[at(centre[phase](t), TILE), :])

        edge = lax.fori_loop(0, TILES + 1, gather, jnp.zeros((96, 256), F32))
        ew_send[phase] = edge.astype(BF16)
        row, col = iota((8, 256), 0), iota((8, 256), 1)
        pick = one_hot(((row == col) & (row < 4)) | ((row == col - 248) & (row >= 4)))
        corners = [dot_nt(pick, ns_send[phase, n]) for n in range(2)]
        corner_send[phase] = jnp.concatenate(corners, axis=0).astype(BF16)

    up, down, left, right = c > 0, c < COLS - 1, r > 0, r < ROWS - 1

    def only(flag, value):
        return jnp.where(flag, value, 0.0)

    def halo_edge(phase):
        row, lane = iota((96, 128), 0), iota((96, 128), 1)
        straight = ((row == lane) & (row < 48) & right) | ((row == lane - 16) & (lane >= 64) & left)
        edge = dot_tn(ew_recv[phase], one_hot(straight))
        row, lane = iota((16, 128), 0), iota((16, 128), 1)

        def place(n, first, start, flag):
            hit = (row >= first) & (row < first + 4) & (lane == row - first + start) & flag
            return dot_tn(corner_recv[phase, n], one_hot(hit))

        above = place(0, 12, 64, left & up) + place(1, 8, 0, right & up)
        below = place(2, 4, 96, left & down) + place(3, 0, 32, right & down)
        return (edge + unpack(above, True) + unpack(below, False)).astype(BF16)

    def halo_rows(phase):
        above = only(up, unpack(ns_recv[phase, 0], True))
        below = only(down, unpack(ns_recv[phase, 1], False))
        return above, below

    def act_fill():
        above, below = halo_rows(0)
        for t, value in ((0, above), (TILES, below)):
            rows = slice(TAPS * t + TILE, TAPS * t + 2 * TILE)
            act[rows, :] = (act[rows, :].astype(F32) + value).astype(BF16)
        edge = halo_edge(0)
        from_j, to_j = iota((256, 512), 0), iota((256, 512), 1)
        shift = one_hot(((to_j < 256) & (from_j == to_j - 4)) | ((to_j >= 256) & (from_j == to_j - 252)))
        lane, col = iota((128, 512), 0), iota((128, 512), 1)

        def spread(t, _):
            place = ((col < 4) & (lane == 64 + 4 * t + col)) | ((col >= 508) & (lane == 4 * t + col - 508))
            both = dot(act[at(TAPS * t + TILE, TILE), :], shift) + dot(edge, one_hot(place))
            act[at(TAPS * t, TILE), :] = both[:, :256].astype(BF16)
            act[at(TAPS * t + 2 * TILE, TILE), :] = both[:, 256:].astype(BF16)
            return 0

        lax.fori_loop(0, TILES + 1, spread, 0)

    def rows_of(part):
        return pl.ds(*SLICES[part])

    def spread_copy(part, n):
        dx, dy = lax.div(n, 4), lax.rem(n, 4)
        to_x, to_y = lax.rem(b + dx, 4), lax.rem(y + dy, 4)
        return pltpu.make_async_remote_copy(
            src_ref=mir_send.at[to_x, rows_of(part), at(32 * to_y, 32), :],
            dst_ref=relay.at[y, to_x, rows_of(part)],
            send_sem=spread_ssem.at[part, n],
            recv_sem=spread_rsem.at[part, n],
            device_id=member_b(4 * to_y + b),
            device_id_type=MESH,
        )

    def relay_copy(part, n):
        dx, dy = lax.div(n, 4), lax.rem(n, 4)
        to_x, from_y = lax.rem(b + dx, 4), lax.rem(y - dy + 4, 4)
        return pltpu.make_async_remote_copy(
            src_ref=relay.at[from_y, to_x, rows_of(part)],
            dst_ref=mir_recv.at[b, rows_of(part), at(32 * y, 32), :],
            send_sem=mir_ssem.at[part, n],
            recv_sem=mir_rsem.at[part, 4 * y + b],
            device_id=mirror_to(to_x, from_y),
            device_id_type=MESH,
        )

    def own_copy(part):
        return pltpu.make_async_copy(
            relay.at[y, b, rows_of(part)],
            mir_recv.at[b, rows_of(part), at(32 * y, 32), :],
            mir_rsem.at[part, 4 * y + b],
        )

    def arrival(part, n):
        from_y, from_x = lax.div(n, 4), lax.rem(n, 4)
        return pltpu.make_async_remote_copy(
            src_ref=relay.at[from_y, from_x, rows_of(part)],
            dst_ref=mir_recv.at[from_x, rows_of(part), at(32 * from_y, 32), :],
            send_sem=mir_ssem.at[part, n],
            recv_sem=mir_rsem.at[part, n],
            device_id=mirror_from(from_x, from_y),
            device_id_type=MESH,
        )

    for x in range(4):
        relay[y, x] = mir_send[x, :, at(32 * y, 32), :]
    pl.semaphore_wait(barrier, 2 * GROUP + 8 + 2 * (GROUP - 1) - 2 * own_mirror.astype(jnp.int32))

    def relayed(n):
        return lax.rem(n, 4) > 0

    def each(part, step, count=GROUP):
        lax.fori_loop(0, count, lambda n, _: step(part, n), 0)

    def send_spread(part, n):
        @pl.when(relayed(n))
        def _():
            spread_copy(part, n).start()

        return 0

    def start_own(part, m):
        stays = own_mirror & (m == 0)

        @pl.when(stays)
        def _():
            own_copy(part).start()

        @pl.when(jnp.logical_not(stays))
        def _():
            relay_copy(part, 4 * m).start()

        return 0

    def pass_on(part, n):
        @pl.when(relayed(n))
        def _():
            spread_copy(part, n).wait_recv()
            relay_copy(part, n).start()

        return 0

    def sent(part, n):
        @pl.when(relayed(n))
        def _():
            spread_copy(part, n).wait_send()

        @pl.when(jnp.logical_not(own_mirror & (n == 0)))
        def _():
            relay_copy(part, n).wait_send()

        return 0

    for part in range(len(SLICES)):
        each(part, send_spread)
    for part in range(len(SLICES)):
        each(part, start_own, 4)
    activations()
    halo_pack(0)
    for copy in halo_copies(0):
        copy.start()

    each(0, pass_on)

    for copy in loads:
        copy.wait()

    spread_out = (lax.div(iota((256, 32), 0), 8) == iota((256, 32), 1)).astype(F32).astype(BF16)
    spread_in = (lax.div(iota((32, 256), 1), 8) == iota((32, 256), 0)).astype(F32).astype(BF16)
    row_out, row_in = lax.rem(iota((256, 256), 0), 8), lax.rem(iota((256, 256), 1), 8)

    def expand(w, turned):
        rows = dot_nt(spread_out, w) if turned else dot(spread_out, w)
        return dot(rows.astype(BF16), spread_in)

    def banded(taps):
        near = jnp.where(row_in == row_out, taps[0], 0.0) + jnp.where(row_in == row_out + 4, taps[1], 0.0)
        far = jnp.where(row_in == row_out, taps[2], 0.0) + jnp.where(row_in == row_out - 4, taps[1], 0.0)
        return near.astype(BF16), far.astype(BF16)

    for tap in range(3):
        near, far = banded([expand(wconv_ref[n, tap], False) for n in range(3)])
        mat_f[:, tap * TILE : (tap + 1) * TILE] = near
        mat_f[:, TAPS + tap * TILE : TAPS + (tap + 1) * TILE] = far
        near, far = banded([expand(wconv_ref[2 - n, 2 - tap], True) for n in range(3)])
        mat_b[tap * TILE : (tap + 1) * TILE, :TILE] = near
        mat_b[tap * TILE : (tap + 1) * TILE, TILE:] = far
    mat_p[...] = jnp.where(row_in == row_out, expand(wpoint_ref[...], True), 0.0).astype(BF16)

    bias_col = jnp.sum(
        jnp.where(lax.div(iota((256, 32), 0), 8) == iota((256, 32), 1), bias_ref[...], 0.0), axis=1, keepdims=True
    )
    mask_row = mask_ref[:, at(256 * a, 256)].astype(F32)
    diagonal = iota((64, 256), 1) == iota((64, 256), 0) + 64 * b
    row_keep = jnp.sum(jnp.where(diagonal, mask_row, 0.0), axis=1, keepdims=True)
    keep[...] = row_keep * (0.5 * mask_ref[:, at(256 * r, 256)].astype(F32))

    csum[...] = jnp.zeros_like(csum)
    psum[...] = jnp.zeros_like(psum)
    bsum[...] = jnp.zeros_like(bsum)

    for part in range(1, len(SLICES)):
        each(part, pass_on)
    for copy in halo_copies(0):
        copy.wait_recv()
    act_fill()

    def forward(t, _):
        v = dot(mat_f[...], act[pl.ds(pl.multiple_of(TAPS * t, TAPS), 2 * TAPS), :])
        v = v + bias_col
        s = sigmoid(v)
        post[at(TILE * t, TILE), :] = (v * s).astype(BF16)
        pre_slope[at(TILE * t, TILE), :] = s * (1.0 + v * (1.0 - s))
        return 0

    lax.fori_loop(0, TILES, forward, 0)

    prev[...] = jnp.zeros_like(prev)
    left_half = iota((8, 8, 128), 2) < 64

    def arrive(part, n):
        stays = own_mirror & (n == 4 * y + b)

        @pl.when(stays)
        def _():
            own_copy(part).wait()

        @pl.when(jnp.logical_not(stays))
        def _():
            arrival(part, n).wait_recv()

        return 0

    def chunk(k, _):
        for part, (first, _) in enumerate(SLICES):

            @pl.when(k == first)
            def _():
                each(part, arrive)

        here = cot[:, at(16 * k, 16), :].astype(F32)
        keep_rows = keep[at(16 * k, 16), :]
        got = [mir_recv[n, k].astype(F32).reshape(8, 16, 256) for n in range(4)]
        for h in range(2):
            t = 2 * k + h
            part = [v[:, 8 * h : 8 * h + 8, :] for v in got]
            quads = []
            for m in range(4):
                cols = slice(128 * (m // 2), 128 * (m // 2) + 128)
                pieces = []
                for n in (0, 2):
                    one, two = part[n][:, :, cols], part[n + 1][:, :, cols]
                    if m % 2 == 0:
                        pieces.append(jnp.where(left_half, one, pltpu.roll(two, 64, 2)))
                    else:
                        pieces.append(jnp.where(left_half, pltpu.roll(one, 64, 2), two))
                quads.append(jnp.concatenate(pieces, axis=2))
            mirrored = jnp.stack(quads, axis=1).reshape(32, 8, 256)
            residual = keep_rows[8 * h : 8 * h + 8][None] * (here[:, 8 * h : 8 * h + 8, :] + mirrored)
            residual = residual.reshape(TILE, 256)
            half = residual.astype(BF16)
            res[at(TILE * t, TILE), :] = residual
            res_half[at(TILE * t, TILE), :] = half
            g = pre_slope[at(TILE * t, TILE), :] * dot(mat_p[...], half)
            gnat[at(TILE * t, TILE), :] = g.astype(BF16)
            turned = pltpu.roll(g.reshape(32, 8, 256), 4, 1)
            put(1, t, jnp.where(low, prev[...], turned))
            prev[...] = turned

        @pl.when(k == 3)
        def _():
            put(1, TILES, jnp.where(low, prev[...], 0.0))

        total, point, line = csum[...], psum[...], bsum[...]
        for h in range(2):
            t = 2 * k + h
            g = gnat[at(TILE * t, TILE), :]
            total = total + dot_nt(g, act[pl.ds(pl.multiple_of(TAPS * t, TAPS), 2 * TAPS), :])
            point = point + dot_nt(res_half[at(TILE * t, TILE), :], post[at(TILE * t, TILE), :])
            wide = g.astype(F32)
            line = line + wide[:, :128] + wide[:, 128:]
        csum[...] = total
        psum[...] = point
        bsum[...] = line
        return 0

    lax.fori_loop(0, 4, chunk, 0)

    def exchange(stage, me, member, order, source, dst):
        def copy(to):
            return pltpu.make_async_remote_copy(
                src_ref=source(to),
                dst_ref=dst.at[me],
                send_sem=red_ssem.at[stage],
                recv_sem=red_rsem.at[stage],
                device_id=member(to),
                device_id_type=MESH,
            )

        def start():
            for to in order:
                copy(to).start()

        def wait(sem):
            others = dst.at[0 : GROUP - 1]
            pltpu.make_async_copy(others, others, sem.at[stage]).wait()

        return (
            copy,
            start,
            lambda: wait(red_rsem),
            lambda: wait(red_ssem),
        )

    def hops(d, ring):
        return min(d, ring - d)

    def far_first(rings):
        offsets = [(i, j) for i in range(rings[0]) for j in range(rings[1])]
        return sorted(offsets, key=lambda o: -hops(o[0], rings[0]) - hops(o[1], rings[1]))[:-1]

    z, core = lax.div(group_a, 2), lax.rem(group_a, 2)
    order_a = [2 * lax.rem(z + i, 8) + lax.rem(core + j, 2) for i, j in far_first((8, 2))]
    order_b = [4 * lax.rem(y + i, 4) + lax.rem(b + j, 4) for i, j in far_first((4, 4))]
    first_copy, _, arrive1, leave1 = exchange(0, group_b, member_b, order_b, lambda m: payload.at[m], part1)
    _, start2, arrive2, leave2 = exchange(1, group_a, member_a, order_a, lambda m: sum1, part2)
    _, start3, arrive3, leave3 = exchange(2, group_b, member_b, order_b, lambda m: sum2, part3)

    def send_payload(m):
        @pl.when(group_b == m)
        def _():
            part1[m] = payload[m]

        @pl.when(group_b != m)
        def _():
            first_copy(m).start()

    col_in = lax.div(iota((256, 128), 0), 8)
    col_out = iota((256, 128), 1)
    for quad in range(3):
        lanes = jnp.zeros((256, 128), F32)
        for slot in range(4):
            n = 4 * quad + slot
            if n > 9:
                continue
            if n == 9:
                v = jnp.where(row_in == row_out, psum[...], 0.0)
            else:
                row_tap, col_tap = n // 3, n % 3
                near = csum[:, col_tap * TILE : (col_tap + 1) * TILE]
                far = csum[:, TAPS + col_tap * TILE : TAPS + (col_tap + 1) * TILE]
                if row_tap == 0:
                    v = jnp.where(row_in == row_out, near, 0.0)
                elif row_tap == 2:
                    v = jnp.where(row_in == row_out, far, 0.0)
                else:
                    v = jnp.where(row_in == row_out + 4, near, 0.0) + jnp.where(row_in == row_out - 4, far, 0.0)
            pick = (col_out == 32 * slot + col_in).astype(F32).astype(BF16)
            high = v.astype(BF16)
            lanes = lanes + (dot(high, pick) + dot((v - high.astype(F32)).astype(BF16), pick))
        if quad == 2:
            line = jnp.sum(bsum[...], axis=1, keepdims=True)
            lanes = lanes + jnp.where((col_out >= 64) & (col_out < 96), line, 0.0)
        lanes = jnp.sum(lanes.reshape(32, 8, 128), axis=1)
        for o in range(4):
            payload[4 * quad + o] = lanes[8 * o : 8 * o + 8]
            send_payload(4 * quad + o)
    for o in range(12, GROUP):
        payload[o] = jnp.zeros((8, 128), F32)
        send_payload(o)

    def total_of(ref):
        total = ref[0]
        for n in range(1, GROUP):
            total = total + ref[n]
        return total

    halo_pack(1)
    for copy in halo_copies(1):
        copy.start()

    lane256 = iota((TILE, 256), 1)

    def over_taps(v):
        west = jnp.where(lane256 >= 4, pltpu.roll(v[:TILE], 4, 1), 0.0)
        east = jnp.where(lane256 < 252, pltpu.roll(v[2 * TILE :], 252, 1), 0.0)
        return v[TILE : 2 * TILE] + west + east

    def inner(t, _):
        v = dot(mat_b[...], grad[pl.ds(pl.multiple_of(TILE * t, TILE), 2 * TILE), :])
        pre_slope[at(TILE * t, TILE), :] = over_taps(v)
        return 0

    lax.fori_loop(0, FIRST, inner, 0)
    arrive1()
    sum1[...] = total_of(part1)
    part2[group_a] = sum1[...]
    start2()
    lax.fori_loop(FIRST, SECOND, inner, 0)
    leave1()
    arrive2()
    sum2[...] = total_of(part2)
    part3[group_b] = sum2[...]
    start3()

    leave2()
    lax.fori_loop(SECOND, TILES, inner, 0)
    for copy in halo_copies(1):
        copy.wait()
    above, below = halo_rows(1)
    pre_slope[:TILE, :] += over_taps(dot(mat_b[:, :TILE], above.astype(BF16)))
    pre_slope[TILE * (TILES - 1) :, :] += over_taps(dot(mat_b[:, TILE:], below.astype(BF16)))
    edge = halo_edge(1)
    from_west = dot(mat_b[:TILE, :TILE], edge) + pltpu.roll(dot(mat_b[:TILE, TILE:], edge), 124, 1)
    from_east = dot(mat_b[2 * TILE :, :TILE], edge) + pltpu.roll(dot(mat_b[2 * TILE :, TILE:], edge), 124, 1)
    lane128 = iota((TILE, 128), 1)
    outer = jnp.where(lane128 < 64, from_east, from_west)

    def store_out(k):
        rows = at(16 * k, 16)
        return pltpu.make_async_copy(out.at[:, rows, :], fg_hbm.at[:, rows, :], out_sem.at[k])

    def backward(k, _):
        halves = []
        for h in range(2):
            t = 2 * k + h
            west = jnp.where(lane128 < 4, pltpu.roll(outer, lax.rem(192 - 4 * t, 128), 1), 0.0)
            east = jnp.where(lane128 >= 124, pltpu.roll(outer, 124 - 4 * t, 1), 0.0)
            v = pre_slope[at(TILE * t, TILE), :] + jnp.concatenate([west, east], axis=1)
            v = res[at(TILE * t, TILE), :] + slope[at(TILE * t, TILE), :] * v
            halves.append(v.reshape(32, 8, 256))
        out[:, at(16 * k, 16), :] = jnp.concatenate(halves, axis=1).astype(BF16)
        store_out(k).start()
        return 0

    lax.fori_loop(0, 4, backward, 0)
    for part in range(len(SLICES)):
        each(part, sent)
    for copy in halo_copies(0):
        copy.wait_send()
    arrive3()

    store_sums = pltpu.make_async_copy(part3.at[0:12], sums_hbm, out_sem.at[4])
    store_sums.start()

    leave3()
    for k in range(4):
        store_out(k).wait()
    store_sums.wait()


def finish(
    fg_hbm, sums_hbm, out_hbm, conv_hbm, point_hbm, biasg_hbm, held, sums_ref, conv_ref, point_ref, biasg_ref, sem
):
    parts = [slice(8 * n, 8 * n + 8) for n in range(4)]
    loads = [pltpu.make_async_copy(fg_hbm.at[p], held.at[p], sem.at[0, n]) for n, p in enumerate(parts)]
    stores = [pltpu.make_async_copy(held.at[p], out_hbm.at[p], sem.at[1, n]) for n, p in enumerate(parts)]
    load_sums = pltpu.make_async_copy(sums_hbm, sums_ref, sem.at[2, 0])
    load_sums.start()
    for copy in loads:
        copy.start()
    for load, store in zip(loads, stores):
        load.wait()
        store.start()
    load_sums.wait()
    scale = 1.0 / 2048.0
    for quad in range(3):
        lanes = jnp.concatenate([sums_ref[4 * quad + o] for o in range(4)], axis=0) * scale
        for slot in range(4):
            n = 4 * quad + slot
            block = lanes if slot == 0 else pltpu.roll(lanes, 128 - 32 * slot, 1)
            if n < 9:
                conv_ref[n // 3, n % 3] = block[:, :32]
            elif n == 9:
                point_ref[...] = block[:, :32]
            elif n == 10:
                square = block[:, :32]
                biasg_ref[...] = jnp.sum(
                    jnp.where(iota((32, 32), 0) == iota((32, 32), 1), square, 0.0), axis=0, keepdims=True
                )
    small = [
        pltpu.make_async_copy(source, target, sem.at[2, 1 + n])
        for n, (source, target) in enumerate([(conv_ref, conv_hbm), (point_ref, point_hbm), (biasg_ref, biasg_hbm)])
    ]
    for copy in small:
        copy.start()
    for copy in stores + small:
        copy.wait()


def shards(features, cotangent, mask, w_conv, w_point, bias):
    hbm = pl.BlockSpec(memory_space=pl.ANY)
    big = (TILES * TILE, 256)
    fg, sums = pl.pallas_call(
        kernel,
        out_shape=(
            jax.ShapeDtypeStruct((32, 64, 256), BF16),
            jax.ShapeDtypeStruct((12, 8, 128), F32),
        ),
        in_specs=[hbm] * 6,
        out_specs=(hbm, hbm),
        scratch_shapes=[
            pltpu.VMEM((1, 2048), jnp.int32),
            pltpu.VMEM((3, 3, 32, 32), BF16),
            pltpu.VMEM((32, 32), BF16),
            pltpu.VMEM((1, 32), F32),
            pltpu.VMEM((32, 64, 256), BF16),
            pltpu.VMEM((32, 64, 256), BF16),
            pltpu.VMEM((4, 4, 128, 256), BF16),
            pltpu.VMEM((4, 4, 4, 32, 256), BF16),
            pltpu.VMEM((4, 4, 128, 256), BF16),
            pltpu.VMEM(((TILES + 1) * TAPS, 256), BF16),
            pltpu.VMEM(((TILES + 1) * TILE, 256), BF16),
            pltpu.VMEM(big, F32),
            pltpu.VMEM(big, BF16),
            pltpu.VMEM(big, F32),
            pltpu.VMEM(big, F32),
            pltpu.VMEM(big, BF16),
            pltpu.VMEM(big, BF16),
            pltpu.VMEM((TILE, 2 * TAPS), BF16),
            pltpu.VMEM((TAPS, 2 * TILE), BF16),
            pltpu.VMEM((TILE, TILE), BF16),
            pltpu.VMEM((64, 256), F32),
            pltpu.VMEM((32, 8, 256), F32),
            pltpu.VMEM((TILE, 2 * TAPS), F32),
            pltpu.VMEM((TILE, TILE), F32),
            pltpu.VMEM((TILE, 128), F32),
            pltpu.VMEM((32, 64, 256), BF16),
            pltpu.VMEM((2, 2, 128, 256), BF16),
            pltpu.VMEM((2, 96, 256), BF16),
            pltpu.VMEM((2, 16, 128), BF16),
            pltpu.VMEM((2, 2, 128, 256), BF16),
            pltpu.VMEM((2, 96, 256), BF16),
            pltpu.VMEM((2, 4, 16, 128), BF16),
            pltpu.VMEM((GROUP, 8, 128), F32),
            pltpu.VMEM((GROUP, 8, 128), F32),
            pltpu.VMEM((8, 128), F32),
            pltpu.VMEM((GROUP, 8, 128), F32),
            pltpu.VMEM((8, 128), F32),
            pltpu.VMEM((GROUP, 8, 128), F32),
            pltpu.SemaphoreType.DMA((6,)),
            pltpu.SemaphoreType.DMA((5,)),
            pltpu.SemaphoreType.DMA((len(SLICES), GROUP)),
            pltpu.SemaphoreType.DMA((len(SLICES), GROUP)),
            pltpu.SemaphoreType.DMA((len(SLICES), GROUP)),
            pltpu.SemaphoreType.DMA((len(SLICES), GROUP)),
            pltpu.SemaphoreType.DMA((2, 8)),
            pltpu.SemaphoreType.DMA((2, 8)),
            pltpu.SemaphoreType.DMA((3,)),
            pltpu.SemaphoreType.DMA((3,)),
        ],
        compiler_params=pltpu.CompilerParams(
            collective_id=0, has_side_effects=True, vmem_limit_bytes=56 * 1024 * 1024
        ),
        cost_estimate=pl.CostEstimate(flops=5_400_000_000, bytes_accessed=3 * 1024 * 1024, transcendentals=2_000_000),
    )(features, cotangent, mask.reshape(1, 2048), w_conv, w_point, bias.reshape(1, 32))
    fg, conv, point, bias_grad = pl.pallas_call(
        finish,
        out_shape=(
            jax.ShapeDtypeStruct((32, 64, 256), BF16),
            jax.ShapeDtypeStruct((3, 3, 32, 32), F32),
            jax.ShapeDtypeStruct((32, 32), F32),
            jax.ShapeDtypeStruct((1, 32), F32),
        ),
        in_specs=[hbm, hbm],
        out_specs=(hbm, hbm, hbm, hbm),
        scratch_shapes=[
            pltpu.VMEM((32, 64, 256), BF16),
            pltpu.VMEM((12, 8, 128), F32),
            pltpu.VMEM((3, 3, 32, 32), F32),
            pltpu.VMEM((32, 32), F32),
            pltpu.VMEM((1, 32), F32),
            pltpu.SemaphoreType.DMA((3, 4)),
        ],
    )(fg, sums)
    return fg, conv, point, bias_grad.reshape(32)


def solution(mesh):
    in_specs = (P(None, "col", "row"), P(None, "col", "row"), P(), P(), P(), P())
    out_specs = (P(None, "col", "row"), P(), P(), P())
    return jax.shard_map(shards, mesh=mesh, in_specs=in_specs, out_specs=out_specs, check_vma=False)
```

```python
import jax
import jax.numpy as jnp
from jax import lax
from jax.experimental import pallas as pl
from jax.experimental.pallas import tpu as pltpu
from jax.sharding import PartitionSpec as P

F32, BF16 = jnp.float32, jnp.bfloat16
MESH = pl.DeviceIdType.MESH
ROWS, COLS = 8, 32
TILE = 256
TAPS = 3 * TILE
TILES = 8
GROUP = 16
FIRST, SECOND = 2, 5
SLICES = ((0, 2), (2, 1), (3, 1))
NT = (((1,), (1,)), ((), ()))
TN = (((0,), (0,)), ((), ()))


def iota(shape, dim):
    return lax.broadcasted_iota(jnp.int32, shape, dim)


def dot(x, y):
    return jnp.dot(x, y, preferred_element_type=F32)


def dot_nt(x, y):
    return lax.dot_general(x, y, NT, preferred_element_type=F32)


def dot_tn(x, y):
    return lax.dot_general(x, y, TN, preferred_element_type=F32)


def one_hot(where):
    return where.astype(F32).astype(BF16)


def at(start, size):
    return pl.ds(pl.multiple_of(start, size), size)


def sigmoid(v):
    return 1.0 / (1.0 + jnp.exp(-v))


def pack(tile, bottom):
    v = tile.reshape(16, 2, 8, 256)
    low = iota((16, 8, 256), 1) < 4
    if bottom:
        v = jnp.where(low, v[:, 0], pltpu.roll(v[:, 1], 4, 1))
    else:
        v = jnp.where(low, pltpu.roll(v[:, 0], 4, 1), v[:, 1])
    return v.reshape(128, 256).astype(BF16)


def unpack(packed, bottom):
    width = packed.shape[1]
    v = packed.astype(F32).reshape(16, 8, width)
    turned = pltpu.roll(v, 4, 1)
    low = iota((16, 8, width), 1) < 4
    if bottom:
        pair = [jnp.where(low, v, 0.0), jnp.where(low, turned, 0.0)]
    else:
        pair = [jnp.where(low, 0.0, turned), jnp.where(low, 0.0, v)]
    return jnp.stack(pair, axis=1).reshape(TILE, width)


def kernel(
    feat_hbm, cot_hbm, mask_hbm, wconv_hbm, wpoint_hbm, bias_hbm,
    fg_hbm, sums_hbm,
    mask_ref, wconv_ref, wpoint_ref, bias_ref,
    feat, cot, mir_send, relay, mir_recv, act, grad, res, res_half, slope, pre_slope, post, gnat,
    mat_f, mat_b, mat_p, keep, prev, csum, psum, bsum, out,
    ns_send, ew_send, corner_send, ns_recv, ew_recv, corner_recv, payload, part1, sum1, part2, sum2, part3,
    in_sem, out_sem, spread_ssem, spread_rsem, mir_ssem, mir_rsem, halo_ssem, halo_rsem, red_ssem, red_rsem,
):
    r, c = lax.axis_index("row"), lax.axis_index("col")
    a, b = lax.div(c, 4), lax.rem(c, 4)
    y, zh = lax.div(c, 8), lax.rem(a, 2)
    group_a, group_b = zh * 8 + r, y * 4 + b

    def mirror_to(x, row):
        return {"row": 2 * row + zh, "col": 4 * r + x}

    def mirror_from(x, row):
        return {"row": a, "col": 8 * row + 4 * lax.rem(r, 2) + x}

    def member_a(m):
        return {"row": lax.rem(m, 8), "col": y * 8 + lax.div(m, 8) * 4 + b}

    def member_b(m):
        return {"row": r, "col": lax.div(m, 4) * 8 + zh * 4 + lax.rem(m, 4)}

    def beside(dr, dc):
        return {"row": lax.rem(r + dr + ROWS, ROWS), "col": lax.rem(c + dc + COLS, COLS)}

    own_mirror = a == r
    sides = [(0, 1), (0, -1), (1, 0), (-1, 0), (1, 1), (-1, 1), (1, -1), (-1, -1)]

    barrier = pltpu.get_barrier_semaphore()

    def greet(device):
        pl.semaphore_signal(barrier, inc=1, device_id=device, device_id_type=MESH)

    @pl.when(jnp.logical_not(own_mirror))
    def _():
        greet(mirror_to(b, y))
        greet(mirror_from(b, y))

    def greet_mirrors(n, _):
        x, row = lax.rem(b + lax.div(n, 4), 4), lax.rem(y + n, 4)
        greet(mirror_to(x, row))
        greet(mirror_from(x, row))
        return 0

    lax.fori_loop(1, GROUP, greet_mirrors, 0)
    for dr, dc in sides:
        greet(beside(dr, dc))

    def greet_groups(d, _):
        greet(member_a(lax.rem(group_a + d, GROUP)))
        greet(member_b(lax.rem(group_b + d, GROUP)))
        return 0

    lax.fori_loop(1, GROUP, greet_groups, 0)

    load_cot = pltpu.make_async_copy(cot_hbm, cot, in_sem.at[0])
    load_feat = pltpu.make_async_copy(feat_hbm, feat, in_sem.at[1])
    loads = [
        pltpu.make_async_copy(source, target, in_sem.at[2 + n])
        for n, (source, target) in enumerate(
            [(mask_hbm, mask_ref), (wconv_hbm, wconv_ref), (wpoint_hbm, wpoint_ref), (bias_hbm, bias_ref)]
        )
    ]
    load_cot.start()
    load_feat.start()
    for copy in loads:
        copy.start()

    load_cot.wait()
    ident = (iota((256, 256), 0) == iota((256, 256), 1)).astype(BF16)

    def turn(g, _):
        block = cot[at(4 * g, 4)].reshape(256, 256)
        turned = dot_nt(ident, block).astype(BF16)
        mir_send[:, :, at(16 * g, 16), :] = turned.reshape(4, 4, 16, 256)
        return 0

    lax.fori_loop(0, 8, turn, 0)

    low = iota((32, 8, 256), 1) < 4

    centre = {0: lambda t: TAPS * t + TILE, 1: lambda t: TILE * t}

    def put(phase, t, tile):
        ref = (act, grad)[phase]
        ref[at(centre[phase](t), TILE), :] = tile.reshape(TILE, 256).astype(BF16)

    def activations():
        load_feat.wait()
        prev[...] = jnp.zeros_like(prev)

        def activate(k, _):
            x = feat[:, at(16 * k, 16), :].astype(F32)
            for h in range(2):
                t = 2 * k + h
                v = x[:, 8 * h : 8 * h + 8, :]
                s = sigmoid(v)
                slope[at(TILE * t, TILE), :] = (s * (1.0 + v * (1.0 - s))).reshape(TILE, 256)
                turned = pltpu.roll(v * s, 4, 1)
                put(0, t, jnp.where(low, prev[...], turned))
                prev[...] = turned
            return 0

        lax.fori_loop(0, 4, activate, 0)
        put(0, TILES, jnp.where(low, prev[...], 0.0))

    def halo_copies(phase):
        diagonal = corner_send.at[phase]
        pairs = [
            (ns_send.at[phase, 1], ns_recv.at[phase, 0]),
            (ns_send.at[phase, 0], ns_recv.at[phase, 1]),
            (ew_send.at[phase, 48:96], ew_recv.at[phase, 48:96]),
            (ew_send.at[phase, 0:48], ew_recv.at[phase, 0:48]),
            (diagonal, corner_recv.at[phase, 0]),
            (diagonal, corner_recv.at[phase, 1]),
            (diagonal, corner_recv.at[phase, 2]),
            (diagonal, corner_recv.at[phase, 3]),
        ]
        return [
            pltpu.make_async_remote_copy(
                src_ref=src,
                dst_ref=dst,
                send_sem=halo_ssem.at[phase, n],
                recv_sem=halo_rsem.at[phase, n],
                device_id=beside(*sides[n]),
                device_id_type=MESH,
            )
            for n, (src, dst) in enumerate(pairs)
        ]

    def halo_pack(phase):
        ref = (act, grad)[phase]
        first, last = centre[phase](0), centre[phase](TILES)
        ns_send[phase, 0] = pack(ref[first : first + TILE, :].astype(F32), False)
        ns_send[phase, 1] = pack(ref[last : last + TILE, :].astype(F32), True)
        row, col = iota((96, 256), 0), iota((96, 256), 1)

        def gather(t, total):
            pick = ((row == 4 * t + col) & (col < 4)) | ((row == 4 * t + col - 204) & (col >= 252))
            return total + dot_nt(one_hot(pick), ref[at(centre[phase](t), TILE), :])

        edge = lax.fori_loop(0, TILES + 1, gather, jnp.zeros((96, 256), F32))
        ew_send[phase] = edge.astype(BF16)
        row, col = iota((8, 256), 0), iota((8, 256), 1)
        pick = one_hot(((row == col) & (row < 4)) | ((row == col - 248) & (row >= 4)))
        corners = [dot_nt(pick, ns_send[phase, n]) for n in range(2)]
        corner_send[phase] = jnp.concatenate(corners, axis=0).astype(BF16)

    up, down, left, right = c > 0, c < COLS - 1, r > 0, r < ROWS - 1

    def only(flag, value):
        return jnp.where(flag, value, 0.0)

    def halo_edge(phase):
        row, lane = iota((96, 128), 0), iota((96, 128), 1)
        straight = ((row == lane) & (row < 48) & right) | ((row == lane - 16) & (lane >= 64) & left)
        edge = dot_tn(ew_recv[phase], one_hot(straight))
        row, lane = iota((16, 128), 0), iota((16, 128), 1)

        def place(n, first, start, flag):
            hit = (row >= first) & (row < first + 4) & (lane == row - first + start) & flag
            return dot_tn(corner_recv[phase, n], one_hot(hit))

        above = place(0, 12, 64, left & up) + place(1, 8, 0, right & up)
        below = place(2, 4, 96, left & down) + place(3, 0, 32, right & down)
        return (edge + unpack(above, True) + unpack(below, False)).astype(BF16)

    def halo_rows(phase):
        above = only(up, unpack(ns_recv[phase, 0], True))
        below = only(down, unpack(ns_recv[phase, 1], False))
        return above, below

    def act_fill():
        above, below = halo_rows(0)
        for t, value in ((0, above), (TILES, below)):
            rows = slice(TAPS * t + TILE, TAPS * t + 2 * TILE)
            act[rows, :] = (act[rows, :].astype(F32) + value).astype(BF16)
        edge = halo_edge(0)
        from_j, to_j = iota((256, 512), 0), iota((256, 512), 1)
        shift = one_hot(((to_j < 256) & (from_j == to_j - 4)) | ((to_j >= 256) & (from_j == to_j - 252)))
        lane, col = iota((128, 512), 0), iota((128, 512), 1)

        def spread(t, _):
            place = ((col < 4) & (lane == 64 + 4 * t + col)) | ((col >= 508) & (lane == 4 * t + col - 508))
            both = dot(act[at(TAPS * t + TILE, TILE), :], shift) + dot(edge, one_hot(place))
            act[at(TAPS * t, TILE), :] = both[:, :256].astype(BF16)
            act[at(TAPS * t + 2 * TILE, TILE), :] = both[:, 256:].astype(BF16)
            return 0

        lax.fori_loop(0, TILES + 1, spread, 0)

    def rows_of(part):
        return pl.ds(*SLICES[part])

    def spread_copy(part, n):
        dx, dy = lax.div(n, 4), lax.rem(n, 4)
        to_x, to_y = lax.rem(b + dx, 4), lax.rem(y + dy, 4)
        return pltpu.make_async_remote_copy(
            src_ref=mir_send.at[to_x, rows_of(part), at(32 * to_y, 32), :],
            dst_ref=relay.at[y, to_x, rows_of(part)],
            send_sem=spread_ssem.at[part, n],
            recv_sem=spread_rsem.at[part, n],
            device_id=member_b(4 * to_y + b),
            device_id_type=MESH,
        )

    def relay_copy(part, n):
        dx, dy = lax.div(n, 4), lax.rem(n, 4)
        to_x, from_y = lax.rem(b + dx, 4), lax.rem(y - dy + 4, 4)
        return pltpu.make_async_remote_copy(
            src_ref=relay.at[from_y, to_x, rows_of(part)],
            dst_ref=mir_recv.at[b, rows_of(part), at(32 * y, 32), :],
            send_sem=mir_ssem.at[part, n],
            recv_sem=mir_rsem.at[part, 4 * y + b],
            device_id=mirror_to(to_x, from_y),
            device_id_type=MESH,
        )

    def own_copy(part):
        return pltpu.make_async_copy(
            relay.at[y, b, rows_of(part)],
            mir_recv.at[b, rows_of(part), at(32 * y, 32), :],
            mir_rsem.at[part, 4 * y + b],
        )

    def arrival(part, n):
        from_y, from_x = lax.div(n, 4), lax.rem(n, 4)
        return pltpu.make_async_remote_copy(
            src_ref=relay.at[from_y, from_x, rows_of(part)],
            dst_ref=mir_recv.at[from_x, rows_of(part), at(32 * from_y, 32), :],
            send_sem=mir_ssem.at[part, n],
            recv_sem=mir_rsem.at[part, n],
            device_id=mirror_from(from_x, from_y),
            device_id_type=MESH,
        )

    for x in range(4):
        relay[y, x] = mir_send[x, :, at(32 * y, 32), :]
    pl.semaphore_wait(barrier, 2 * GROUP + 8 + 2 * (GROUP - 1) - 2 * own_mirror.astype(jnp.int32))

    def relayed(n):
        return lax.rem(n, 4) > 0

    def each(part, step, count=GROUP):
        lax.fori_loop(0, count, lambda n, _: step(part, n), 0)

    def send_spread(part, n):
        @pl.when(relayed(n))
        def _():
            spread_copy(part, n).start()

        return 0

    def start_own(part, m):
        stays = own_mirror & (m == 0)

        @pl.when(stays)
        def _():
            own_copy(part).start()

        @pl.when(jnp.logical_not(stays))
        def _():
            relay_copy(part, 4 * m).start()

        return 0

    def pass_on(part, n):
        @pl.when(relayed(n))
        def _():
            spread_copy(part, n).wait_recv()
            relay_copy(part, n).start()

        return 0

    def sent(part, n):
        @pl.when(relayed(n))
        def _():
            spread_copy(part, n).wait_send()

        @pl.when(jnp.logical_not(own_mirror & (n == 0)))
        def _():
            relay_copy(part, n).wait_send()

        return 0

    for part in range(len(SLICES)):
        each(part, send_spread)
    for part in range(len(SLICES)):
        each(part, start_own, 4)
    activations()
    halo_pack(0)
    for copy in halo_copies(0):
        copy.start()

    each(0, pass_on)

    for copy in loads:
        copy.wait()

    spread_out = (lax.div(iota((256, 32), 0), 8) == iota((256, 32), 1)).astype(F32).astype(BF16)
    spread_in = (lax.div(iota((32, 256), 1), 8) == iota((32, 256), 0)).astype(F32).astype(BF16)
    row_out, row_in = lax.rem(iota((256, 256), 0), 8), lax.rem(iota((256, 256), 1), 8)

    def expand(w, turned):
        rows = dot_nt(spread_out, w) if turned else dot(spread_out, w)
        return dot(rows.astype(BF16), spread_in)

    def banded(taps):
        near = jnp.where(row_in == row_out, taps[0], 0.0) + jnp.where(row_in == row_out + 4, taps[1], 0.0)
        far = jnp.where(row_in == row_out, taps[2], 0.0) + jnp.where(row_in == row_out - 4, taps[1], 0.0)
        return near.astype(BF16), far.astype(BF16)

    for tap in range(3):
        near, far = banded([expand(wconv_ref[n, tap], False) for n in range(3)])
        mat_f[:, tap * TILE : (tap + 1) * TILE] = near
        mat_f[:, TAPS + tap * TILE : TAPS + (tap + 1) * TILE] = far
        near, far = banded([expand(wconv_ref[2 - n, 2 - tap], True) for n in range(3)])
        mat_b[tap * TILE : (tap + 1) * TILE, :TILE] = near
        mat_b[tap * TILE : (tap + 1) * TILE, TILE:] = far
    mat_p[...] = jnp.where(row_in == row_out, expand(wpoint_ref[...], True), 0.0).astype(BF16)

    bias_col = jnp.sum(
        jnp.where(lax.div(iota((256, 32), 0), 8) == iota((256, 32), 1), bias_ref[...], 0.0), axis=1, keepdims=True
    )
    mask_row = mask_ref[:, at(256 * a, 256)].astype(F32)
    diagonal = iota((64, 256), 1) == iota((64, 256), 0) + 64 * b
    row_keep = jnp.sum(jnp.where(diagonal, mask_row, 0.0), axis=1, keepdims=True)
    keep[...] = row_keep * (0.5 * mask_ref[:, at(256 * r, 256)].astype(F32))

    csum[...] = jnp.zeros_like(csum)
    psum[...] = jnp.zeros_like(psum)
    bsum[...] = jnp.zeros_like(bsum)

    for part in range(1, len(SLICES)):
        each(part, pass_on)
    for copy in halo_copies(0):
        copy.wait_recv()
    act_fill()

    def forward(t, _):
        v = dot(mat_f[...], act[pl.ds(pl.multiple_of(TAPS * t, TAPS), 2 * TAPS), :])
        v = v + bias_col
        s = sigmoid(v)
        post[at(TILE * t, TILE), :] = (v * s).astype(BF16)
        pre_slope[at(TILE * t, TILE), :] = s * (1.0 + v * (1.0 - s))
        return 0

    lax.fori_loop(0, TILES, forward, 0)

    prev[...] = jnp.zeros_like(prev)
    left_half = iota((8, 8, 128), 2) < 64

    def arrive(part, n):
        stays = own_mirror & (n == 4 * y + b)

        @pl.when(stays)
        def _():
            own_copy(part).wait()

        @pl.when(jnp.logical_not(stays))
        def _():
            arrival(part, n).wait_recv()

        return 0

    def chunk(k, _):
        for part, (first, _) in enumerate(SLICES):

            @pl.when(k == first)
            def _():
                each(part, arrive)

        here = cot[:, at(16 * k, 16), :].astype(F32)
        keep_rows = keep[at(16 * k, 16), :]
        got = [mir_recv[n, k].astype(F32).reshape(8, 16, 256) for n in range(4)]
        for h in range(2):
            t = 2 * k + h
            part = [v[:, 8 * h : 8 * h + 8, :] for v in got]
            quads = []
            for m in range(4):
                cols = slice(128 * (m // 2), 128 * (m // 2) + 128)
                pieces = []
                for n in (0, 2):
                    one, two = part[n][:, :, cols], part[n + 1][:, :, cols]
                    if m % 2 == 0:
                        pieces.append(jnp.where(left_half, one, pltpu.roll(two, 64, 2)))
                    else:
                        pieces.append(jnp.where(left_half, pltpu.roll(one, 64, 2), two))
                quads.append(jnp.concatenate(pieces, axis=2))
            mirrored = jnp.stack(quads, axis=1).reshape(32, 8, 256)
            residual = keep_rows[8 * h : 8 * h + 8][None] * (here[:, 8 * h : 8 * h + 8, :] + mirrored)
            residual = residual.reshape(TILE, 256)
            half = residual.astype(BF16)
            res[at(TILE * t, TILE), :] = residual
            res_half[at(TILE * t, TILE), :] = half
            g = pre_slope[at(TILE * t, TILE), :] * dot(mat_p[...], half)
            gnat[at(TILE * t, TILE), :] = g.astype(BF16)
            turned = pltpu.roll(g.reshape(32, 8, 256), 4, 1)
            put(1, t, jnp.where(low, prev[...], turned))
            prev[...] = turned

        @pl.when(k == 3)
        def _():
            put(1, TILES, jnp.where(low, prev[...], 0.0))

        total, point, line = csum[...], psum[...], bsum[...]
        for h in range(2):
            t = 2 * k + h
            g = gnat[at(TILE * t, TILE), :]
            total = total + dot_nt(g, act[pl.ds(pl.multiple_of(TAPS * t, TAPS), 2 * TAPS), :])
            point = point + dot_nt(res_half[at(TILE * t, TILE), :], post[at(TILE * t, TILE), :])
            wide = g.astype(F32)
            line = line + wide[:, :128] + wide[:, 128:]
        csum[...] = total
        psum[...] = point
        bsum[...] = line
        return 0

    lax.fori_loop(0, 4, chunk, 0)

    def exchange(stage, me, member, order, source, dst):
        def copy(to):
            return pltpu.make_async_remote_copy(
                src_ref=source(to),
                dst_ref=dst.at[me],
                send_sem=red_ssem.at[stage],
                recv_sem=red_rsem.at[stage],
                device_id=member(to),
                device_id_type=MESH,
            )

        def start():
            for to in order:
                copy(to).start()

        def wait(sem):
            others = dst.at[0 : GROUP - 1]
            pltpu.make_async_copy(others, others, sem.at[stage]).wait()

        return (
            copy,
            start,
            lambda: wait(red_rsem),
            lambda: wait(red_ssem),
        )

    def hops(d, ring):
        return min(d, ring - d)

    def far_first(rings):
        offsets = [(i, j) for i in range(rings[0]) for j in range(rings[1])]
        return sorted(offsets, key=lambda o: -hops(o[0], rings[0]) - hops(o[1], rings[1]))[:-1]

    z, core = lax.div(group_a, 2), lax.rem(group_a, 2)
    order_a = [2 * lax.rem(z + i, 8) + lax.rem(core + j, 2) for i, j in far_first((8, 2))]
    order_b = [4 * lax.rem(y + i, 4) + lax.rem(b + j, 4) for i, j in far_first((4, 4))]
    first_copy, _, arrive1, leave1 = exchange(0, group_b, member_b, order_b, lambda m: payload.at[m], part1)
    _, start2, arrive2, leave2 = exchange(1, group_a, member_a, order_a, lambda m: sum1, part2)
    _, start3, arrive3, leave3 = exchange(2, group_b, member_b, order_b, lambda m: sum2, part3)

    def send_payload(m):
        @pl.when(group_b == m)
        def _():
            part1[m] = payload[m]

        @pl.when(group_b != m)
        def _():
            first_copy(m).start()

    col_in = lax.div(iota((256, 128), 0), 8)
    col_out = iota((256, 128), 1)
    for quad in range(3):
        lanes = jnp.zeros((256, 128), F32)
        for slot in range(4):
            n = 4 * quad + slot
            if n > 9:
                continue
            if n == 9:
                v = jnp.where(row_in == row_out, psum[...], 0.0)
            else:
                row_tap, col_tap = n // 3, n % 3
                near = csum[:, col_tap * TILE : (col_tap + 1) * TILE]
                far = csum[:, TAPS + col_tap * TILE : TAPS + (col_tap + 1) * TILE]
                if row_tap == 0:
                    v = jnp.where(row_in == row_out, near, 0.0)
                elif row_tap == 2:
                    v = jnp.where(row_in == row_out, far, 0.0)
                else:
                    v = jnp.where(row_in == row_out + 4, near, 0.0) + jnp.where(row_in == row_out - 4, far, 0.0)
            pick = (col_out == 32 * slot + col_in).astype(F32).astype(BF16)
            high = v.astype(BF16)
            lanes = lanes + (dot(high, pick) + dot((v - high.astype(F32)).astype(BF16), pick))
        if quad == 2:
            line = jnp.sum(bsum[...], axis=1, keepdims=True)
            lanes = lanes + jnp.where((col_out >= 64) & (col_out < 96), line, 0.0)
        lanes = jnp.sum(lanes.reshape(32, 8, 128), axis=1)
        for o in range(4):
            payload[4 * quad + o] = lanes[8 * o : 8 * o + 8]
            send_payload(4 * quad + o)
    for o in range(12, GROUP):
        payload[o] = jnp.zeros((8, 128), F32)
        send_payload(o)

    def total_of(ref):
        total = ref[0]
        for n in range(1, GROUP):
            total = total + ref[n]
        return total

    halo_pack(1)
    for copy in halo_copies(1):
        copy.start()

    lane256 = iota((TILE, 256), 1)

    def over_taps(v):
        west = jnp.where(lane256 >= 4, pltpu.roll(v[:TILE], 4, 1), 0.0)
        east = jnp.where(lane256 < 252, pltpu.roll(v[2 * TILE :], 252, 1), 0.0)
        return v[TILE : 2 * TILE] + west + east

    def inner(t, _):
        v = dot(mat_b[...], grad[pl.ds(pl.multiple_of(TILE * t, TILE), 2 * TILE), :])
        pre_slope[at(TILE * t, TILE), :] = over_taps(v)
        return 0

    lax.fori_loop(0, FIRST, inner, 0)
    arrive1()
    sum1[...] = total_of(part1)
    part2[group_a] = sum1[...]
    start2()
    lax.fori_loop(FIRST, SECOND, inner, 0)
    leave1()
    arrive2()
    sum2[...] = total_of(part2)
    part3[group_b] = sum2[...]
    start3()

    leave2()
    lax.fori_loop(SECOND, TILES, inner, 0)
    for copy in halo_copies(1):
        copy.wait()
    above, below = halo_rows(1)
    pre_slope[:TILE, :] += over_taps(dot(mat_b[:, :TILE], above.astype(BF16)))
    pre_slope[TILE * (TILES - 1) :, :] += over_taps(dot(mat_b[:, TILE:], below.astype(BF16)))
    edge = halo_edge(1)
    from_west = dot(mat_b[:TILE, :TILE], edge) + pltpu.roll(dot(mat_b[:TILE, TILE:], edge), 124, 1)
    from_east = dot(mat_b[2 * TILE :, :TILE], edge) + pltpu.roll(dot(mat_b[2 * TILE :, TILE:], edge), 124, 1)
    lane128 = iota((TILE, 128), 1)
    outer = jnp.where(lane128 < 64, from_east, from_west)

    def store_out(k):
        rows = at(16 * k, 16)
        return pltpu.make_async_copy(out.at[:, rows, :], fg_hbm.at[:, rows, :], out_sem.at[k])

    def backward(k, _):
        halves = []
        for h in range(2):
            t = 2 * k + h
            west = jnp.where(lane128 < 4, pltpu.roll(outer, lax.rem(192 - 4 * t, 128), 1), 0.0)
            east = jnp.where(lane128 >= 124, pltpu.roll(outer, 124 - 4 * t, 1), 0.0)
            v = pre_slope[at(TILE * t, TILE), :] + jnp.concatenate([west, east], axis=1)
            v = res[at(TILE * t, TILE), :] + slope[at(TILE * t, TILE), :] * v
            halves.append(v.reshape(32, 8, 256))
        out[:, at(16 * k, 16), :] = jnp.concatenate(halves, axis=1).astype(BF16)
        store_out(k).start()
        return 0

    lax.fori_loop(0, 4, backward, 0)
    for part in range(len(SLICES)):
        each(part, sent)
    for copy in halo_copies(0):
        copy.wait_send()
    arrive3()

    store_sums = pltpu.make_async_copy(part3.at[0:12], sums_hbm, out_sem.at[4])
    store_sums.start()

    leave3()
    for k in range(4):
        store_out(k).wait()
    store_sums.wait()


def finish(
    fg_hbm, sums_hbm, out_hbm, conv_hbm, point_hbm, biasg_hbm, held, sums_ref, conv_ref, point_ref, biasg_ref, sem
):
    parts = [slice(8 * n, 8 * n + 8) for n in range(4)]
    loads = [pltpu.make_async_copy(fg_hbm.at[p], held.at[p], sem.at[0, n]) for n, p in enumerate(parts)]
    stores = [pltpu.make_async_copy(held.at[p], out_hbm.at[p], sem.at[1, n]) for n, p in enumerate(parts)]
    load_sums = pltpu.make_async_copy(sums_hbm, sums_ref, sem.at[2, 0])
    load_sums.start()
    for copy in loads:
        copy.start()
    for load, store in zip(loads, stores):
        load.wait()
        store.start()
    load_sums.wait()
    scale = 1.0 / 2048.0
    for quad in range(3):
        lanes = jnp.concatenate([sums_ref[4 * quad + o] for o in range(4)], axis=0) * scale
        for slot in range(4):
            n = 4 * quad + slot
            block = lanes if slot == 0 else pltpu.roll(lanes, 128 - 32 * slot, 1)
            if n < 9:
                conv_ref[n // 3, n % 3] = block[:, :32]
            elif n == 9:
                point_ref[...] = block[:, :32]
            elif n == 10:
                square = block[:, :32]
                biasg_ref[...] = jnp.sum(
                    jnp.where(iota((32, 32), 0) == iota((32, 32), 1), square, 0.0), axis=0, keepdims=True
                )
    small = [
        pltpu.make_async_copy(source, target, sem.at[2, 1 + n])
        for n, (source, target) in enumerate([(conv_ref, conv_hbm), (point_ref, point_hbm), (biasg_ref, biasg_hbm)])
    ]
    for copy in small:
        copy.start()
    for copy in stores + small:
        copy.wait()


def shards(features, cotangent, mask, w_conv, w_point, bias):
    hbm = pl.BlockSpec(memory_space=pl.ANY)
    big = (TILES * TILE, 256)
    fg, sums = pl.pallas_call(
        kernel,
        out_shape=(
            jax.ShapeDtypeStruct((32, 64, 256), BF16),
            jax.ShapeDtypeStruct((12, 8, 128), F32),
        ),
        in_specs=[hbm] * 6,
        out_specs=(hbm, hbm),
        scratch_shapes=[
            pltpu.VMEM((1, 2048), jnp.int32),
            pltpu.VMEM((3, 3, 32, 32), BF16),
            pltpu.VMEM((32, 32), BF16),
            pltpu.VMEM((1, 32), F32),
            pltpu.VMEM((32, 64, 256), BF16),
            pltpu.VMEM((32, 64, 256), BF16),
            pltpu.VMEM((4, 4, 128, 256), BF16),
            pltpu.VMEM((4, 4, 4, 32, 256), BF16),
            pltpu.VMEM((4, 4, 128, 256), BF16),
            pltpu.VMEM(((TILES + 1) * TAPS, 256), BF16),
            pltpu.VMEM(((TILES + 1) * TILE, 256), BF16),
            pltpu.VMEM(big, F32),
            pltpu.VMEM(big, BF16),
            pltpu.VMEM(big, F32),
            pltpu.VMEM(big, F32),
            pltpu.VMEM(big, BF16),
            pltpu.VMEM(big, BF16),
            pltpu.VMEM((TILE, 2 * TAPS), BF16),
            pltpu.VMEM((TAPS, 2 * TILE), BF16),
            pltpu.VMEM((TILE, TILE), BF16),
            pltpu.VMEM((64, 256), F32),
            pltpu.VMEM((32, 8, 256), F32),
            pltpu.VMEM((TILE, 2 * TAPS), F32),
            pltpu.VMEM((TILE, TILE), F32),
            pltpu.VMEM((TILE, 128), F32),
            pltpu.VMEM((32, 64, 256), BF16),
            pltpu.VMEM((2, 2, 128, 256), BF16),
            pltpu.VMEM((2, 96, 256), BF16),
            pltpu.VMEM((2, 16, 128), BF16),
            pltpu.VMEM((2, 2, 128, 256), BF16),
            pltpu.VMEM((2, 96, 256), BF16),
            pltpu.VMEM((2, 4, 16, 128), BF16),
            pltpu.VMEM((GROUP, 8, 128), F32),
            pltpu.VMEM((GROUP, 8, 128), F32),
            pltpu.VMEM((8, 128), F32),
            pltpu.VMEM((GROUP, 8, 128), F32),
            pltpu.VMEM((8, 128), F32),
            pltpu.VMEM((GROUP, 8, 128), F32),
            pltpu.SemaphoreType.DMA((6,)),
            pltpu.SemaphoreType.DMA((5,)),
            pltpu.SemaphoreType.DMA((len(SLICES), GROUP)),
            pltpu.SemaphoreType.DMA((len(SLICES), GROUP)),
            pltpu.SemaphoreType.DMA((len(SLICES), GROUP)),
            pltpu.SemaphoreType.DMA((len(SLICES), GROUP)),
            pltpu.SemaphoreType.DMA((2, 8)),
            pltpu.SemaphoreType.DMA((2, 8)),
            pltpu.SemaphoreType.DMA((3,)),
            pltpu.SemaphoreType.DMA((3,)),
        ],
        compiler_params=pltpu.CompilerParams(
            collective_id=0, has_side_effects=True, vmem_limit_bytes=56 * 1024 * 1024
        ),
        cost_estimate=pl.CostEstimate(flops=5_400_000_000, bytes_accessed=3 * 1024 * 1024, transcendentals=2_000_000),
    )(features, cotangent, mask.reshape(1, 2048), w_conv, w_point, bias.reshape(1, 32))
    fg, conv, point, bias_grad = pl.pallas_call(
        finish,
        out_shape=(
            jax.ShapeDtypeStruct((32, 64, 256), BF16),
            jax.ShapeDtypeStruct((3, 3, 32, 32), F32),
            jax.ShapeDtypeStruct((32, 32), F32),
            jax.ShapeDtypeStruct((1, 32), F32),
        ),
        in_specs=[hbm, hbm],
        out_specs=(hbm, hbm, hbm, hbm),
        scratch_shapes=[
            pltpu.VMEM((32, 64, 256), BF16),
            pltpu.VMEM((12, 8, 128), F32),
            pltpu.VMEM((3, 3, 32, 32), F32),
            pltpu.VMEM((32, 32), F32),
            pltpu.VMEM((1, 32), F32),
            pltpu.SemaphoreType.DMA((3, 4)),
        ],
    )(fg, sums)
    return fg, conv, point, bias_grad.reshape(32)


def solution(mesh):
    in_specs = (P(None, "col", "row"), P(None, "col", "row"), P(), P(), P(), P())
    out_specs = (P(None, "col", "row"), P(), P(), P())
    return jax.shard_map(shards, mesh=mesh, in_specs=in_specs, out_specs=out_specs, check_vma=False)
```
